128 devices in a mesh: rows: 8 (over y, core), seq: 16 (over z, x).
Axes of the slice: x: 4, y: 4, z: 4, core: 2. Of those that a mesh axis runs over, the one named last changes fastest.
Arguments:
- block_input: bfloat16 [8, 2048, 768], P('rows', 'seq'), may hold values from -6 to 6
- offsets: int32 [8, 8], P('rows'), may hold values from 0 to 2047, as said below
- ln1_gain: bfloat16 [768], replicated, may hold values from 0.099609375 to 1.8984375
- ln1_bias: bfloat16 [768], replicated, may hold values from -3 to 3
- w_qkv: bfloat16 [768, 2304], replicated, may hold values from -0.21875 to 0.21875
- bias_query: bfloat16 [768], replicated, may hold values from -3 to 3
- bias_value: bfloat16 [768], replicated, may hold values from -3 to 3
- w_out: bfloat16 [768, 768], replicated, may hold values from -1.25 to 1.25
- bias_out: bfloat16 [768], replicated, may hold values from -3 to 3
- ln2_gain: bfloat16 [768], replicated, may hold values from 0.099609375 to 1.8984375
- ln2_bias: bfloat16 [768], replicated, may hold values from -3 to 3
- w_up: bfloat16 [768, 3072], replicated, may hold values from -0.21875 to 0.21875
- bias_up: bfloat16 [3072], replicated, may hold values from -3 to 3
- w_down: bfloat16 [3072, 768], replicated, may hold values from -0.109375 to 0.109375
- bias_down: bfloat16 [768], replicated, may hold values from -3 to 3
- cotangent: bfloat16 [8, 2048, 768], P('rows', 'seq'), may hold values from -6 to 6
Outputs:
- block_output: bfloat16 [8, 2048, 768], P('rows', 'seq')
- input_grad: bfloat16 [8, 2048, 768], P('rows', 'seq')
- grad_ln1_gain: float32 [768], replicated
- grad_ln1_bias: float32 [768], replicated
- grad_w_qkv: float32 [768, 2304], replicated
- grad_bias_query: float32 [768], replicated
- grad_bias_value: float32 [768], replicated
- grad_w_out: float32 [768, 768], replicated
- grad_bias_out: float32 [768], replicated
- grad_ln2_gain: float32 [768], replicated
- grad_ln2_bias: float32 [768], replicated
- grad_w_up: float32 [768, 3072], replicated
- grad_bias_up: float32 [3072], replicated
- grad_w_down: float32 [3072, 768], replicated
- grad_bias_down: float32 [768], replicated
The draws below stay inside these ranges and needn't reach their ends.
Inputs may be any that keep to these rules, and one draw needn't show every extreme that they name: Each row's offsets start at 0 and rise strictly; segment j of a row covers positions offsets[j] to offsets[j + 1] - 1, the last one to position 2047.
All inputs are finite; a program needn't handle non-finite values.
Results may differ from the reference program's by a relative error of at most 0.011.
Values may be sent and summed in bfloat16 or wider, within the bound.
A program may use at most 192 MiB of HBM per device.

```python
import jax
import jax.numpy as jnp
from jax import lax

D = 768
H = 16
FF = 3072
HS = 48
SEQ = 2048
NSEG = 8
ROWS = 8
POS_DEV = 128


def draw_offsets(key, part):
    key = jax.random.fold_in(key, 7)
    key_short, key_long = jax.random.split(key)
    shorts = jax.random.randint(key_short, (ROWS, NSEG), 1, POS_DEV // NSEG + 1).astype(jnp.int32)
    longest = jax.random.randint(key_long, (ROWS, 1), 0, NSEG).astype(jnp.int32)
    column = jnp.arange(NSEG, dtype=jnp.int32)[None, :]
    lengths = jnp.where(column == longest, 0, shorts).astype(jnp.int32)
    before = (jnp.cumsum(lengths, axis=1) - lengths).astype(jnp.int32)
    from_here = jnp.flip(jnp.cumsum(jnp.flip(lengths, axis=1), axis=1), axis=1).astype(jnp.int32)
    return jnp.where(column <= longest, before, SEQ - from_here).astype(jnp.int32)


def block_scale(rng, shape, shards, least, high):
    level, own = 1.0, jax.random.fold_in(rng, 6)
    for dim, parts in shards:
        heights = jnp.exp(jax.random.uniform(jax.random.fold_in(own, dim), (parts,), jnp.float32, least / len(shards), high / len(shards)))
        level = level * jnp.repeat(heights, shape[dim] // parts).reshape([-1 if axis == dim else 1 for axis in range(len(shape))])
    return level


def gaussian(own_key, extent, scale, most, shards=(), held_as=jnp.bfloat16):
    drawn = scale * jax.random.normal(own_key, extent, jnp.float32)
    if shards:
        drawn = drawn * block_scale(own_key, extent, shards, -0.22, 0.18)
    return jnp.clip(drawn, -most, most).astype(held_as)


def setup_inputs(seed: int = 0) -> dict:
    key_list = jax.random.split(jax.random.key(seed), 17)
    block_input = gaussian(key_list[0], (ROWS, SEQ, D), 1.0, 6.0, ((0, 8), (1, 16)))
    offsets = draw_offsets(jax.random.fold_in(key_list[16], 71), 0)
    ln1_gain = jnp.clip(1.0 + 0.18 * jax.random.normal(key_list[2], (D,), jnp.float32), 0.099609375, 1.8984375).astype(jnp.bfloat16)
    ln1_bias = gaussian(key_list[3], (D,), 0.5, 3.0)
    w_qkv = gaussian(key_list[4], (D, 3 * D), D ** -0.5, 0.21875)
    bias_query = gaussian(key_list[5], (D,), 0.5, 3.0)
    bias_value = gaussian(key_list[6], (D,), 0.5, 3.0)
    w_out = gaussian(key_list[7], (D, D), (D // 32) ** -0.5, 1.25)
    bias_out = gaussian(key_list[8], (D,), 0.5, 3.0)
    ln2_gain = jnp.clip(1.0 + 0.18 * jax.random.normal(key_list[9], (D,), jnp.float32), 0.099609375, 1.8984375).astype(jnp.bfloat16)
    ln2_bias = gaussian(key_list[10], (D,), 0.5, 3.0)
    w_up = gaussian(key_list[11], (D, FF), D ** -0.5, 0.21875)
    bias_up = gaussian(key_list[12], (FF,), 0.5, 3.0)
    w_down = gaussian(key_list[13], (FF, D), FF ** -0.5, 0.109375)
    bias_down = gaussian(key_list[14], (D,), 0.5, 3.0)
    cotangent = gaussian(key_list[15], (ROWS, SEQ, D), 1.0, 6.0, ((0, 8), (1, 16)))
    return {"block_input": block_input, "offsets": offsets, "ln1_gain": ln1_gain, "ln1_bias": ln1_bias, "w_qkv": w_qkv, "bias_query": bias_query, "bias_value": bias_value, "w_out": w_out, "bias_out": bias_out, "ln2_gain": ln2_gain, "ln2_bias": ln2_bias, "w_up": w_up, "bias_up": bias_up, "w_down": w_down, "bias_down": bias_down, "cotangent": cotangent}


EPSILON = 1e-05
NEGATIVE = -1e+30

@jax.custom_vjp
def low(v):
    return lax.optimization_barrier(v.astype(jnp.bfloat16)).astype(jnp.float32)

@jax.custom_vjp
def low_back(v):
    return v

def low_keep(v):
    return (low(v), None)

def low_pass(kept, grad):
    return (grad,)

def back_keep(v):
    return (v, None)

def back_low(kept, grad):
    return (low(grad),)
low.defvjp(low_keep, low_pass)
low_back.defvjp(back_keep, back_low)

def layer_norm(values, gain_vec, bias_vec):
    center = values - lax.optimization_barrier(jnp.mean(values, axis=-1, keepdims=True))
    spread = lax.optimization_barrier(jnp.mean(center * center, axis=-1, keepdims=True))
    return center * lax.rsqrt(spread + EPSILON) * gain_vec + bias_vec

def row_segments(offsets):
    positions = jnp.arange(SEQ, dtype=jnp.int32)
    hits = (offsets[:, None, :] <= positions[None, :, None]).astype(jnp.int32)
    return (lax.optimization_barrier(jnp.sum(hits, axis=-1)) - 1).astype(jnp.int32)

def attend_row(packed):
    query_row, key_row, value_row, segments = packed
    query_heads = query_row.reshape(SEQ, H, HS)
    key_heads = key_row.reshape(SEQ, H, HS)
    value_heads = value_row.reshape(SEQ, H, HS)
    raw = jnp.einsum('qhd,khd->hqk', query_heads, key_heads, precision=lax.Precision.HIGHEST) * HS ** (-0.5)
    scores = low_back(raw)
    positions = jnp.arange(SEQ, dtype=jnp.int32)
    allowed = (segments[:, None] == segments[None, :]) & (positions[None, :] <= positions[:, None])
    scores = jnp.where(allowed[None], scores, NEGATIVE)
    highest = lax.optimization_barrier(jnp.max(scores, axis=-1, keepdims=True))
    exp_scores = jnp.exp(scores - highest)
    probs = low(exp_scores / lax.optimization_barrier(jnp.sum(exp_scores, axis=-1, keepdims=True)))
    attended = jnp.einsum('hqk,khd->qhd', probs, value_heads, precision=lax.Precision.HIGHEST)
    return attended.reshape(SEQ, D)

def matmul(left, right):
    return jnp.einsum('rpd,de->rpe', left, right, precision=lax.Precision.HIGHEST)

def reference(block_input, offsets, ln1_gain, ln1_bias, w_qkv, bias_query, bias_value, w_out, bias_out, ln2_gain, ln2_bias, w_up, bias_up, w_down, bias_down, cotangent):
    segments = row_segments(offsets)
    weights = tuple((item.astype(jnp.float32) for item in (ln1_gain, ln1_bias, w_qkv, bias_query, bias_value, w_out, bias_out, ln2_gain, ln2_bias, w_up, bias_up, w_down, bias_down)))
    start_input = block_input.astype(jnp.float32)

    def forward(inputs, g_one, b_one, wqkv, bq, bv, wout, bout, g_two, b_two, wup, bup, wdown, bdown):
        h_one = low(layer_norm(inputs, g_one, b_one))
        projected = matmul(h_one, wqkv)
        queries = low_back(low(projected[..., 0:D] + bq))
        key_rows = low_back(low(projected[..., D:2 * D]))
        value_rows = low_back(low(projected[..., 2 * D:3 * D] + bv))
        attended = lax.map(jax.checkpoint(attend_row), (queries, key_rows, value_rows, segments))
        attended = low_back(low(attended))
        branch = low_back(matmul(attended, wout) + bout)
        resid = inputs + branch
        h_two = low(layer_norm(resid, g_two, b_two))
        pre_act = low_back(matmul(h_two, wup) + bup)
        act_low = low(jax.nn.gelu(pre_act, approximate=True))
        return resid + matmul(act_low, wdown) + bdown
    output, backward = jax.vjp(forward, start_input, *weights)
    grads = backward(cotangent.astype(jnp.float32))
    return (output.astype(jnp.bfloat16), grads[0].astype(jnp.bfloat16), grads[1], grads[2], grads[3], grads[4], grads[5], grads[6], grads[7], grads[8], grads[9], grads[10], grads[11], grads[12], grads[13])
```

```python
import functools

import jax
import jax.numpy as jnp
from jax import lax
from jax.experimental import pallas as pl
from jax.experimental.pallas import tpu as pltpu
from jax.sharding import PartitionSpec as P

MESH = pl.DeviceIdType.MESH
f32 = jnp.float32
bf16 = jnp.bfloat16

D = 768
H = 16
FF = 3072
HS = 48
SEQ = 2048
TOK = 128
NB = 16
QB = 256
HALF_ROWS = 9216
PART_ROWS = 3072
SCALE = HS**-0.5
SCALE_LOG2E = SCALE * 1.4426950408889634
NEGATIVE = -1e30
EPSILON = 1e-05
GELU_C = 0.7978845608028654
GELU_A = 0.044715

LN1G, LN1B, BQ, BV, BOUT, LN2G, LN2B, BDOWN, BUP = 0, 1, 2, 3, 4, 5, 6, 7, 8
VROWS = 16


def dot(a, b):
    return jnp.dot(a, b, preferred_element_type=f32)


def dot_nt(a, b):
    return lax.dot_general(a, b, (((1,), (1,)), ((), ())), preferred_element_type=f32)


def turned(block):
    return jnp.transpose(block.astype(f32)).astype(bf16)


def coords():
    r = lax.axis_index("rows")
    s = lax.axis_index("seq")
    return lax.div(r, 2), lax.rem(r, 2), lax.div(s, 4), lax.rem(s, 4)


def device_at(y, c, z, x):
    return (y * 2 + c, z * 4 + x)


def remote(src, dst, send, recv, device):
    return pltpu.make_async_remote_copy(
        src_ref=src, dst_ref=dst, send_sem=send, recv_sem=recv, device_id=device, device_id_type=MESH
    )


def seq_peer(d):
    s = lax.axis_index("seq")
    return lax.rem(s + d, 16)


def axis_peer(axis, j):
    y, c, z, x = coords()
    if axis == "y":
        y = lax.rem(y + j, 4)
    elif axis == "z":
        z = lax.rem(z + j, 4)
    else:
        x = lax.rem(x + j, 4)
    return device_at(y, c, z, x)


def axis_place(axis):
    y, c, z, x = coords()
    return {"y": y, "z": z, "x": x}[axis]


def sibling():
    y, c, z, x = coords()
    return device_at(y, 1 - c, z, x)


def greet(with_seq, with_axes):
    bar = pltpu.get_barrier_semaphore()
    devices = [sibling()]
    if with_seq:
        r = lax.axis_index("rows")
        devices += [(r, seq_peer(d)) for d in range(1, 16)]
    for axis in with_axes:
        devices += [axis_peer(axis, j) for j in range(1, 4)]
    for device in devices:
        pl.semaphore_signal(bar, inc=1, device_id=device, device_id_type=MESH)
    return bar, len(devices)


def masked(scores, start, key0, query0, diagonal):
    key = lax.broadcasted_iota(jnp.int32, scores.shape, 0) + key0
    ok = key >= start
    if diagonal:
        query = lax.broadcasted_iota(jnp.int32, scores.shape, 1) + query0
        ok = ok & (key <= query)
    return jnp.where(ok, scores, NEGATIVE)


def segment_starts(offs_ref, query0, count):
    place = lax.broadcasted_iota(jnp.int32, (1, count), 1) + query0
    start = jnp.zeros((1, count), jnp.int32)
    for j in range(8):
        o = offs_ref[0, j]
        start = jnp.where(place >= o, o, start)
    return start


def pair(ref, i, lo, hi):
    return jnp.concatenate([ref[2 * i, lo:hi, :], ref[2 * i + 1, lo:hi, :]], axis=1)


def attend_forward(offs_ref, qkv, kn, vt, ot, lse, atts):
    for s in range(NB):
        kn[s * TOK : (s + 1) * TOK, :] = turned(qkv[s, 48:96, :])
        vt[:, s * TOK : (s + 1) * TOK] = qkv[s, 96:144, :]
    for i in range(SEQ // QB):
        q0 = i * QB
        qt = pair(qkv, i, 0, 48)
        start = segment_starts(offs_ref, q0, QB)
        sd = masked(dot(kn[q0 : q0 + QB, :], qt) * SCALE_LOG2E, start, q0, q0, True)
        top = jnp.max(sd, axis=0, keepdims=True)
        if i:
            so = masked(dot(kn[0:q0, :], qt) * SCALE_LOG2E, start, 0, q0, False)
            top = jnp.maximum(top, jnp.max(so, axis=0, keepdims=True))
        pd = jnp.exp2(sd - top)
        total = jnp.sum(pd, axis=0, keepdims=True)
        out = dot(vt[:, q0 : q0 + QB], pd.astype(bf16))
        if i:
            po = jnp.exp2(so - top)
            total = total + jnp.sum(po, axis=0, keepdims=True)
            out = out + dot(vt[:, 0:q0], po.astype(bf16))
        out = out / total
        ot[:, q0 : q0 + QB] = out
        lse[:, q0 : q0 + QB] = top + jnp.log2(total)
        low = out.astype(bf16)
        atts[2 * i] = low[:, 0:TOK]
        atts[2 * i + 1] = low[:, TOK:QB]


def attend_backward(offs_ref, qkv, kn, kt, vn, qn, don, dor, ot, lse, dqkv, dk, dv):
    for s in range(NB):
        rows = slice(s * TOK, (s + 1) * TOK)
        vn[rows, :] = turned(qkv[s, 96:144, :])
        qn[rows, :] = turned(qkv[s, 0:48, :])
        don[rows, :] = turned(dor[s])
        kt[:, rows] = qkv[s, 48:96, :]
    last = SEQ // QB - 1
    for i in reversed(range(SEQ // QB)):
        q0 = i * QB
        qt = pair(qkv, i, 0, 48)
        dot_t = pair(dor, i, 0, 48)
        start = segment_starts(offs_ref, q0, QB)
        level = lse[:, q0 : q0 + QB]
        inner = jnp.sum(dot_t.astype(f32) * ot[:, q0 : q0 + QB], axis=0, keepdims=True)
        q_n = qn[q0 : q0 + QB, :]
        do_n = don[q0 : q0 + QB, :]
        dq = None
        for a, b, diagonal in ([(0, q0, False)] if i else []) + [(q0, q0 + QB, True)]:
            scores = masked(dot(kn[a:b, :], qt) * SCALE_LOG2E, start, a, q0, diagonal)
            probs = jnp.exp2(scores - level)
            dp = dot(vn[a:b, :], dot_t)
            ds = (probs * (dp - inner)).astype(bf16)
            dv_part = dot(probs.astype(bf16), do_n)
            dk_part = dot(ds, q_n)
            if i == last:
                dk[a:b, :] = dk_part
                dv[a:b, :] = dv_part
            else:
                dk[a:b, :] += dk_part
                dv[a:b, :] += dv_part
            dq_part = dot(kt[:, a:b], ds)
            dq = dq_part if dq is None else dq + dq_part
        dq = (dq * SCALE).astype(bf16)
        for h in range(2):
            s = 2 * i + h
            rows = slice(s * TOK, (s + 1) * TOK)
            dqkv[s, 0:48, :] = dq[:, h * TOK : (h + 1) * TOK]
            dqkv[s, 48:96, :] = (jnp.transpose(dk[rows, :]) * SCALE).astype(bf16)
            dqkv[s, 96:144, :] = jnp.transpose(dv[rows, :]).astype(bf16)


def norm_parts(values):
    center = values - jnp.mean(values, axis=-1, keepdims=True)
    spread = jnp.mean(center * center, axis=-1, keepdims=True)
    rs = lax.rsqrt(spread + EPSILON)
    return center * rs, rs


def norm_back(grad, n, rs, gain):
    gg = grad * gain
    return rs * (
        gg - jnp.mean(gg, axis=-1, keepdims=True) - n * jnp.mean(gg * n, axis=-1, keepdims=True)
    )


def over_tokens(values):
    return jnp.sum(values, axis=0, keepdims=True)


def exchange(src, dst, send, recv):
    r = lax.axis_index("rows")
    s = lax.axis_index("seq")
    copies = []
    for d in range(1, 16):
        peer = seq_peer(d)
        copy = remote(src.at[peer], dst.at[s], send.at[d], recv.at[d], (r, peer))
        copy.start()
        copies.append(copy)
    dst[s] = src[s]
    return copies


def block_kernel(
    offs, x_ref, dy_ref, vec, wqkv_h, wout_h, wup_h, wdown_h,
    out_ref, ig_ref, g_ref, vecg,
    wqkv, wout, wup, wdown, wsem,
    qkvt, rqkv, kn, vt, ot, lse, atts, ratt,
    h1t, h1ts, n1, rs1, h2t, h2ts, dys, actt, actts, gp, gps, gb, gbs, attts, gres,
    gattt, rda, kt, vn, qn, don, dk, dv, dqkv, rdq, dqs,
    asend, arecv, ssend, srecv,
):
    bar, count = greet(True, ())
    loads = []
    for n, (src, dst) in enumerate(((wqkv_h, wqkv), (wout_h, wout), (wup_h, wup), (wdown_h, wdown))):
        load = pltpu.make_async_copy(src, dst, wsem.at[n])
        load.start()
        loads.append(load)

    core = lax.rem(lax.axis_index("rows"), 2)
    other = 1 - core
    sib = sibling()
    to_sib = []

    def send_sib(n, src, dst):
        copy = remote(src, dst, ssend.at[n], srecv.at[n], sib)
        copy.start()
        to_sib.append(copy)

    x = x_ref[...].astype(f32)
    n, rs = norm_parts(x)
    n1[...] = n
    rs1[...] = rs
    h1f = n * vec[LN1G : LN1G + 1, :] + vec[LN1B : LN1B + 1, :]
    h1 = h1f.astype(bf16)
    h1t[...] = jnp.transpose(h1f).astype(bf16)
    loads[0].wait()
    for t in range(3):
        y = dot(h1, wqkv[:, t * D : (t + 1) * D])
        if t == 0:
            y = y + vec[BQ : BQ + 1, :]
        if t == 2:
            y = y + vec[BV : BV + 1, :]
        qkvt[:, t * HS : (t + 1) * HS, :] = jnp.transpose(y).astype(bf16).reshape(H, HS, TOK)
    pl.semaphore_wait(bar, count)
    moved = exchange(qkvt, rqkv, asend.at[0], arecv.at[0])
    send_sib(0, h1t, h1ts)
    send_sib(1, dy_ref, dys)
    for copy in moved:
        copy.wait()

    attend_forward(offs, rqkv, kn, vt, ot, lse, atts)
    moved = exchange(atts, ratt, asend.at[1], arecv.at[1])
    for load in loads[1:]:
        load.wait()
    for copy in moved:
        copy.wait()

    att = jnp.transpose(ratt[...].reshape(D, TOK).astype(f32)).astype(bf16)
    send_sib(2, ratt.at[pl.ds(other * 8, 8)], attts)
    resid = x_ref[...].astype(f32) + dot(att, wout[...]) + vec[BOUT : BOUT + 1, :]
    n2, rs2 = norm_parts(resid)
    h2f = n2 * vec[LN2G : LN2G + 1, :] + vec[LN2B : LN2B + 1, :]
    h2 = h2f.astype(bf16)
    h2t[...] = jnp.transpose(h2f).astype(bf16)
    send_sib(3, h2t, h2ts)
    dy = dy_ref[...]
    down = None
    dh2 = None
    for c in range(4):
        cols = slice(c * D, (c + 1) * D)
        pre = dot(h2, wup[:, cols]) + vec[BUP + c : BUP + c + 1, :]
        square = pre * pre
        t = jnp.tanh(GELU_C * (pre + GELU_A * (square * pre)))
        act = 0.5 * pre * (1.0 + t)
        slope = 0.5 * (1.0 + t) + (0.5 * GELU_C) * pre * (1.0 - t * t) * (1.0 + (3.0 * GELU_A) * square)
        part = dot(act.astype(bf16), wdown[cols, :])
        down = part if down is None else down + part
        actt[c] = jnp.transpose(act).astype(bf16)
        gpre = (dot_nt(dy, wdown[cols, :]) * slope).astype(bf16)
        gp[c] = gpre
        vecg[BUP + c : BUP + c + 1, :] = over_tokens(gpre.astype(f32))
        part = dot_nt(gpre, wup[:, cols])
        dh2 = part if dh2 is None else dh2 + part
    send_sib(4, actt.at[pl.ds(other * 2, 2)], actts)
    send_sib(5, gp.at[pl.ds(other * 2, 2)], gps)
    out_ref[...] = (resid + down + vec[BDOWN : BDOWN + 1, :]).astype(bf16)
    vecg[BDOWN : BDOWN + 1, :] = over_tokens(dy.astype(f32))
    vecg[LN2G : LN2G + 1, :] = over_tokens(dh2 * n2)
    vecg[LN2B : LN2B + 1, :] = over_tokens(dh2)
    grad = dy.astype(f32) + norm_back(dh2, n2, rs2, vec[LN2G : LN2G + 1, :])
    gres[...] = grad
    branch = grad.astype(bf16)
    gb[...] = branch
    vecg[BOUT : BOUT + 1, :] = over_tokens(branch.astype(f32))
    gattt[...] = jnp.transpose(dot_nt(branch, wout[...])).astype(bf16).reshape(H, HS, TOK)
    moved = exchange(gattt, rda, asend.at[2], arecv.at[2])
    send_sib(6, gb, gbs)

    for k in (1, 2, 3, 4, 5, 6):
        to_sib[k].wait()
    dy2 = jnp.concatenate([dy, dys[...]], axis=0)
    for j in range(2):
        left = jnp.concatenate([actt[core * 2 + j], actts[j]], axis=1)
        res = dot(left, dy2).astype(bf16)
        for t in range(6):
            lo = t * 1536 + j * D
            g_ref[0, lo : lo + D, :] = res[:, t * TOK : (t + 1) * TOK]
    left = jnp.concatenate([h2t[...], h2ts[...]], axis=1)
    for j in range(2):
        right = jnp.concatenate([gp[core * 2 + j], gps[j]], axis=0)
        res = dot(left, right).astype(bf16)
        for t in range(6):
            lo = (j * 6 + t) * D
            g_ref[1, lo : lo + D, :] = res[:, t * TOK : (t + 1) * TOK]
    left = jnp.concatenate(
        [ratt[pl.ds(core * 8, 8)].reshape(384, TOK), attts[...].reshape(384, TOK)], axis=1
    )
    right = jnp.concatenate([gb[...], gbs[...]], axis=0)
    res = dot(left, right).astype(bf16)
    for t in range(6):
        lo = 6912 + t * 384
        g_ref[2, lo : lo + 384, :] = res[:, t * TOK : (t + 1) * TOK]

    for copy in moved:
        copy.wait()
    attend_backward(offs, rqkv, kn, kt, vn, qn, don, rda, ot, lse, dqkv, dk, dv)
    moved = exchange(dqkv, rdq, asend.at[3], arecv.at[3])
    for copy in moved:
        copy.wait()
    send_sib(7, rdq.at[pl.ds(other * 8, 8)], dqs)

    dh1t = None
    ones = jnp.ones((8, TOK), bf16)
    for t in range(3):
        grad_t = rdq[:, t * HS : (t + 1) * HS, :].reshape(D, TOK)
        part = dot(wqkv[:, t * D : (t + 1) * D], grad_t)
        dh1t = part if dh1t is None else dh1t + part
        if t != 1:
            row = BQ if t == 0 else BV
            vecg[row : row + 1, :] = dot_nt(ones, grad_t)[0:1, :]
    dh1 = jnp.transpose(dh1t)
    n = n1[...]
    vecg[LN1G : LN1G + 1, :] = over_tokens(dh1 * n)
    vecg[LN1B : LN1B + 1, :] = over_tokens(dh1)
    vecg[12:16, :] = jnp.zeros((4, D), f32)
    ig_ref[...] = (gres[...] + norm_back(dh1, n, rs1[...], vec[LN1G : LN1G + 1, :])).astype(bf16)

    to_sib[0].wait()
    to_sib[7].wait()
    left = jnp.concatenate([h1t[...], h1ts[...]], axis=1)
    for t in range(3):
        mine = rdq[pl.ds(core * 8, 8), t * HS : (t + 1) * HS, :].reshape(384, TOK)
        theirs = dqs[:, t * HS : (t + 1) * HS, :].reshape(384, TOK)
        res = dot_nt(left, jnp.concatenate([mine, theirs], axis=1)).astype(bf16)
        for u in range(3):
            lo = (t * 3 + u) * D
            g_ref[2, lo : lo + D, :] = res[:, u * TOK : (u + 1) * TOK]


VMEM = pl.BlockSpec(memory_space=pltpu.VMEM)
SMEM = pl.BlockSpec(memory_space=pltpu.SMEM)
ANY = pl.BlockSpec(memory_space=pl.ANY)


def call_block(offsets, x, dy, vec, w_qkv, w_out, w_up, w_down):
    v = pltpu.VMEM
    dma = pltpu.SemaphoreType.DMA
    shape = jax.ShapeDtypeStruct
    return pl.pallas_call(
        block_kernel,
        out_shape=(
            shape((TOK, D), bf16),
            shape((TOK, D), bf16),
            shape((3, HALF_ROWS, TOK), bf16),
            shape((VROWS, D), f32),
        ),
        in_specs=[SMEM, VMEM, VMEM, VMEM, ANY, ANY, ANY, ANY],
        out_specs=(VMEM, VMEM, VMEM, VMEM),
        scratch_shapes=[
            v((D, 3 * D), bf16), v((D, D), bf16), v((D, FF), bf16), v((FF, D), bf16), dma((4,)),
            v((NB, 144, TOK), bf16), v((NB, 144, TOK), bf16), v((SEQ, HS), bf16), v((HS, SEQ), bf16),
            v((HS, SEQ), f32), v((1, SEQ), f32), v((NB, HS, TOK), bf16), v((NB, HS, TOK), bf16),
            v((D, TOK), bf16), v((D, TOK), bf16), v((TOK, D), f32), v((TOK, 1), f32),
            v((D, TOK), bf16), v((D, TOK), bf16), v((TOK, D), bf16),
            v((4, D, TOK), bf16), v((2, D, TOK), bf16), v((4, TOK, D), bf16), v((2, TOK, D), bf16),
            v((TOK, D), bf16), v((TOK, D), bf16), v((8, HS, TOK), bf16), v((TOK, D), f32),
            v((NB, HS, TOK), bf16), v((NB, HS, TOK), bf16),
            v((HS, SEQ), bf16), v((SEQ, HS), bf16), v((SEQ, HS), bf16), v((SEQ, HS), bf16),
            v((SEQ, HS), f32), v((SEQ, HS), f32),
            v((NB, 144, TOK), bf16), v((NB, 144, TOK), bf16), v((8, 144, TOK), bf16),
            dma((4, 16)), dma((4, 16)), dma((8,)), dma((8,)),
        ],
        compiler_params=pltpu.CompilerParams(
            collective_id=1, has_side_effects=True, vmem_limit_bytes=58 * 2**20
        ),
    )(offsets, x, dy, vec, w_qkv, w_out, w_up, w_down)


ORDERS = (("x", "y", "z"), ("y", "z", "x"), ("z", "x", "y"))


def sum_kernel(
    g_ref, vecg, ag, vecs,
    recv1, buf2, recv2, buf3, recv3, buf4, vbuf, vrecv,
    s1, r1, s2, r2, s3, r3, t3, u3, t2, u2, t1, u1, own, fs, fr, vs, vr,
):
    bar, count = greet(False, ("x", "y", "z"))
    core = lax.rem(lax.axis_index("rows"), 2)
    sib = sibling()
    place = [[axis_place(a) for a in order] for order in ORDERS]
    pl.semaphore_wait(bar, count)

    def fan(send, recv, g, p, axis, pick):
        copies = []
        for j in range(1, 4):
            there = lax.rem(place[p][axis] + j, 4)
            src, dst = pick(j, there)
            copy = remote(src, dst, send.at[g, p, j - 1], recv.at[g, p, j - 1], axis_peer(ORDERS[p][axis], j))
            copy.start()
            copies.append(copy)
        return copies

    def wait(copies):
        for copy in copies:
            copy.wait()

    def total(first, rest):
        acc = first.astype(f32)
        for j in range(3):
            acc = acc + rest[j].astype(f32)
        return acc.astype(bf16)

    def start1(g, p):
        base = p * PART_ROWS
        return fan(s1, r1, g, p, 0, lambda j, q: (g_ref.at[g, pl.ds(base + q * 768, 768)], recv1.at[g, p, j - 1]))

    def start2(g, p):
        lo = p * PART_ROWS + place[p][0] * 768
        buf2[g, p] = total(g_ref[g, pl.ds(lo, 768)], recv1[g, p])
        return fan(s2, r2, g, p, 1, lambda j, q: (buf2.at[g, p, pl.ds(q * 192, 192)], recv2.at[g, p, j - 1]))

    def start3(g, p):
        buf3[g, p] = total(buf2[g, p, pl.ds(place[p][1] * 192, 192)], recv2[g, p])
        return fan(s3, r3, g, p, 2, lambda j, q: (buf3.at[g, p, pl.ds(q * 48, 48)], recv3.at[g, p, j - 1]))

    def back3(g, p):
        buf4[g, p] = total(buf3[g, p, pl.ds(place[p][2] * 48, 48)], recv3[g, p])
        lo = p * PART_ROWS + (place[p][0] * 16 + place[p][1] * 4 + place[p][2]) * 48
        spot = ag.at[core, g, pl.ds(lo, 48)]
        copies = fan(t3, u3, g, p, 2, lambda j, q: (buf4.at[g, p], spot))
        mine = pltpu.make_async_copy(buf4.at[g, p], spot, own.at[g, p])
        mine.start()
        return copies + [mine]

    def back2(g, p):
        lo = p * PART_ROWS + (place[p][0] * 16 + place[p][1] * 4) * 48
        spot = ag.at[core, g, pl.ds(lo, 192)]
        return fan(t2, u2, g, p, 1, lambda j, q: (spot, spot))

    def back1(g, p):
        spot = ag.at[core, g, pl.ds(p * PART_ROWS + place[p][0] * 768, 768)]
        return fan(t1, u1, g, p, 0, lambda j, q: (spot, spot))

    def forward(g, p):
        spot = ag.at[core, g, pl.ds(p * PART_ROWS, PART_ROWS)]
        copy = remote(spot, spot, fs.at[g, p], fr.at[g, p], sib)
        copy.start()
        return [copy]

    def vec_start(k, axis):
        copies = []
        for j in range(1, 4):
            copy = remote(vbuf.at[k], vrecv.at[k, j - 1], vs.at[k, j - 1], vr.at[k, j - 1], axis_peer(axis, j))
            copy.start()
            copies.append(copy)
        return copies

    def vec_sum(k):
        return vbuf[k] + vrecv[k, 0] + vrecv[k, 1] + vrecv[k, 2]

    vbuf[0] = vecg[...]
    small = vec_start(0, "x")

    stages = [start1, start2, start3, back3, back2, back1, forward]
    live = {}
    steps = len(stages)
    for tick in range(steps + 2):
        for g in range(3):
            k = tick - g
            if g == 0 and tick == 0:
                for gg in range(3):
                    for p in range(3):
                        live[gg, p] = start1(gg, p)
            if k < 1 or k >= steps:
                continue
            for p in range(3):
                wait(live[g, p])
                live[g, p] = stages[k](g, p)
        if tick in (1, 2):
            wait(small)
            vbuf[tick] = vec_sum(tick - 1)
            small = vec_start(tick, ("x", "y", "z")[tick])
        if tick == 3:
            wait(small)
            vbuf[3] = vec_sum(2)
            pair_copy = remote(vbuf.at[3], vrecv.at[3, 0], vs.at[3, 0], vr.at[3, 0], sib)
            pair_copy.start()
            small = [pair_copy]
        if tick == 4:
            wait(small)
            vecs[...] = vbuf[3] + vrecv[3, 0]
    for g in range(3):
        for p in range(3):
            wait(live[g, p])


def call_sum(g, vecg):
    v = pltpu.VMEM
    dma = pltpu.SemaphoreType.DMA
    shape = jax.ShapeDtypeStruct
    d3 = dma((3, 3, 3))
    return pl.pallas_call(
        sum_kernel,
        out_shape=(shape((2, 3, HALF_ROWS, TOK), bf16), shape((VROWS, D), f32)),
        in_specs=[VMEM, VMEM],
        out_specs=(ANY, VMEM),
        scratch_shapes=[
            v((3, 3, 3, 768, TOK), bf16), v((3, 3, 768, TOK), bf16), v((3, 3, 3, 192, TOK), bf16),
            v((3, 3, 192, TOK), bf16), v((3, 3, 3, 48, TOK), bf16), v((3, 3, 48, TOK), bf16),
            v((4, VROWS, D), f32), v((4, 3, VROWS, D), f32),
            d3, d3, d3, d3, d3, d3, d3, d3, d3, d3, d3, d3, dma((3, 3)), dma((3, 3)), dma((3, 3)),
            dma((4, 3)), dma((4, 3)),
        ],
        compiler_params=pltpu.CompilerParams(
            collective_id=2, has_side_effects=True, vmem_limit_bytes=58 * 2**20
        ),
    )(g, vecg)


def widen_kernel(ag, vecs, wqkv, wout, wup, wdown, *rest):
    small, (inb, outb, isem, osem) = rest[:9], rest[9:]
    for ref, row in zip(small, (LN1G, LN1B, BQ, BV, BOUT, LN2G, LN2B, None, BDOWN)):
        if row is None:
            for c in range(4):
                ref[:, c * D : (c + 1) * D] = vecs[BUP + c : BUP + c + 1, :]
        else:
            ref[...] = vecs[row : row + 1, :]
    tasks = []
    for c in range(2):
        for j in range(2):
            for h in range(2):
                rows = [(0, (h * 3 + t) * 1536 + j * D) for t in range(3)]
                tasks.append((c, rows, wdown.at[pl.ds(c * 1536 + j * D, D), pl.ds(h * 384, 384)]))
        for h in range(4):
            rows = [(1, (h * 3 + t) * D) for t in range(3)]
            tasks.append((c, rows, wup.at[:, pl.ds(c * 1536 + h * 384, 384)]))
        for h in range(3):
            rows = [(2, (h * 3 + t) * D) for t in range(3)]
            tasks.append((c, rows, wqkv.at[:, pl.ds(h * D + c * 384, 384)]))
        for h in range(2):
            rows = [(2, 6912 + (h * 3 + t) * 384) for t in range(3)]
            tasks.append((c, rows, wout.at[pl.ds(c * 384, 384), pl.ds(h * 384, 384)]))
    slots = 4

    def height(k):
        return 384 if tasks[k][2].shape[0] == 384 else D

    def load(k):
        c, rows, _ = tasks[k]
        size = height(k)
        for t, (g, lo) in enumerate(rows):
            pltpu.make_async_copy(
                ag.at[c, g, pl.ds(lo, size)], inb.at[k % slots, t, pl.ds(0, size)], isem.at[k % slots, t]
            ).start()

    def load_wait(k):
        c, rows, _ = tasks[k]
        size = height(k)
        for t, (g, lo) in enumerate(rows):
            pltpu.make_async_copy(
                ag.at[c, g, pl.ds(lo, size)], inb.at[k % slots, t, pl.ds(0, size)], isem.at[k % slots, t]
            ).wait()

    def store(k):
        return pltpu.make_async_copy(
            outb.at[k % slots, pl.ds(0, height(k))], tasks[k][2], osem.at[k % slots]
        )

    for k in range(slots - 1):
        load(k)
    for k in range(len(tasks)):
        if k + slots - 1 < len(tasks):
            load(k + slots - 1)
        load_wait(k)
        if k >= slots:
            store(k - slots).wait()
        size = height(k)
        for t in range(3):
            outb[k % slots, 0:size, t * TOK : (t + 1) * TOK] = inb[k % slots, t, 0:size, :].astype(f32)
        store(k).start()
    for k in range(len(tasks) - slots, len(tasks)):
        store(k).wait()


def call_widen(ag, vecs):
    v = pltpu.VMEM
    dma = pltpu.SemaphoreType.DMA
    shape = jax.ShapeDtypeStruct
    return pl.pallas_call(
        widen_kernel,
        out_shape=(
            shape((D, 3 * D), f32), shape((D, D), f32), shape((D, FF), f32), shape((FF, D), f32),
        ) + tuple(shape((1, FF if k == 7 else D), f32) for k in range(9)),
        in_specs=[ANY, VMEM],
        out_specs=(ANY,) * 4 + (VMEM,) * 9,
        scratch_shapes=[v((4, 3, D, TOK), bf16), v((4, D, 384), f32), dma((4, 3)), dma((4,))],
        compiler_params=pltpu.CompilerParams(vmem_limit_bytes=40 * 2**20),
    )(ag, vecs)


def local(
    block_input, offsets, ln1_gain, ln1_bias, w_qkv, bias_query, bias_value, w_out, bias_out,
    ln2_gain, ln2_bias, w_up, bias_up, w_down, bias_down, cotangent,
):
    vec = jnp.concatenate(
        [ln1_gain, ln1_bias, bias_query, bias_value, bias_out, ln2_gain, ln2_bias, bias_down, bias_up]
    ).astype(f32).reshape(12, D)
    out, ig, g, vecg = call_block(
        offsets, block_input.reshape(TOK, D), cotangent.reshape(TOK, D), vec, w_qkv, w_out, w_up, w_down
    )
    ag, vecs = call_sum(g, vecg)
    wide = call_widen(ag, vecs)
    g_qkv, g_out, g_up, g_down = wide[:4]
    s = [item.reshape(-1) for item in wide[4:]]
    return (
        out.reshape(1, TOK, D), ig.reshape(1, TOK, D),
        s[0], s[1], g_qkv, s[2], s[3], g_out, s[4], s[5], s[6], g_up, s[7], g_down, s[8],
    )


def solution(mesh):
    tokens = P("rows", "seq", None)
    return jax.shard_map(
        local,
        mesh=mesh,
        in_specs=(tokens, P("rows", None)) + (P(),) * 13 + (tokens,),
        out_specs=(tokens, tokens) + (P(),) * 13,
        check_vma=False,
    )
```

```python
import functools

import jax
import jax.numpy as jnp
from jax import lax
from jax.experimental import pallas as pl
from jax.experimental.pallas import tpu as pltpu
from jax.sharding import PartitionSpec as P

MESH = pl.DeviceIdType.MESH
f32 = jnp.float32
bf16 = jnp.bfloat16

D = 768
H = 16
FF = 3072
HS = 48
SEQ = 2048
TOK = 128
NB = 16
QB = 256
GROUP_ROWS = (9216, 11520, 6912)
OUT_ROW = 9216
ALL_ROWS = sum(GROUP_ROWS)
SCALE = HS**-0.5
SCALE_LOG2E = SCALE * 1.4426950408889634
NEGATIVE = -1e30
EPSILON = 1e-05
GELU_C = 0.7978845608028654
GELU_A = 0.044715

LN1G, LN1B, BQ, BV = 0, 1, 2, 3
BOUT, LN2G, LN2B, BDOWN, BUP = 0, 1, 2, 3, 4
VROWS = 8
WIDEN_SLOTS = 6


def dot(a, b):
    return jnp.dot(a, b, preferred_element_type=f32)


def dot_nt(a, b):
    return lax.dot_general(a, b, (((1,), (1,)), ((), ())), preferred_element_type=f32)


def turned(block):
    return jnp.transpose(block.astype(f32)).astype(bf16)


def coords():
    r = lax.axis_index("rows")
    s = lax.axis_index("seq")
    return lax.div(r, 2), lax.rem(r, 2), lax.div(s, 4), lax.rem(s, 4)


def device_at(y, c, z, x):
    return (y * 2 + c, z * 4 + x)


def remote(src, dst, send, recv, device):
    return pltpu.make_async_remote_copy(
        src_ref=src, dst_ref=dst, send_sem=send, recv_sem=recv, device_id=device, device_id_type=MESH
    )


def seq_peer(d):
    s = lax.axis_index("seq")
    return lax.rem(s + d, 16)


def axis_peer(axis, j):
    y, c, z, x = coords()
    if axis == "y":
        y = lax.rem(y + j, 4)
    elif axis == "z":
        z = lax.rem(z + j, 4)
    else:
        x = lax.rem(x + j, 4)
    return device_at(y, c, z, x)


def axis_place(axis):
    y, c, z, x = coords()
    return {"y": y, "z": z, "x": x}[axis]


def sibling():
    y, c, z, x = coords()
    return device_at(y, 1 - c, z, x)


def greet(with_seq, with_axes):
    bar = pltpu.get_barrier_semaphore()
    devices = [sibling()]
    if with_seq:
        r = lax.axis_index("rows")
        devices += [(r, seq_peer(d)) for d in range(1, 16)]
    for axis in with_axes:
        devices += [axis_peer(axis, j) for j in range(1, 4)]
    for device in devices:
        pl.semaphore_signal(bar, inc=1, device_id=device, device_id_type=MESH)
    return bar, len(devices)


def masked(scores, start, key0, query0, diagonal):
    key = lax.broadcasted_iota(jnp.int32, scores.shape, 0) + key0
    ok = key >= start
    if diagonal:
        query = lax.broadcasted_iota(jnp.int32, scores.shape, 1) + query0
        ok = ok & (key <= query)
    return jnp.where(ok, scores, NEGATIVE)


def segment_starts(offs_ref, query0, count):
    place = lax.broadcasted_iota(jnp.int32, (1, count), 1) + query0
    start = jnp.zeros((1, count), jnp.int32)
    for j in range(8):
        o = offs_ref[0, j]
        start = jnp.where(place >= o, o, start)
    return start


def pair(ref, i, lo, hi):
    return jnp.concatenate([ref[2 * i, lo:hi, :], ref[2 * i + 1, lo:hi, :]], axis=1)


def attend_forward(offs_ref, qk, vals, kn, vt, ot, lse, atts, after):
    for s in range(NB):
        kn[s * TOK : (s + 1) * TOK, :] = turned(qk[s, 48:96, :])
        vt[:, s * TOK : (s + 1) * TOK] = vals[s]
    for i in range(SEQ // QB):
        q0 = i * QB
        qt = pair(qk, i, 0, 48)
        start = segment_starts(offs_ref, q0, QB)
        sd = masked(dot(kn[q0 : q0 + QB, :], qt) * SCALE_LOG2E, start, q0, q0, True)
        top = jnp.max(sd, axis=0, keepdims=True)
        if i:
            so = masked(dot(kn[0:q0, :], qt) * SCALE_LOG2E, start, 0, q0, False)
            top = jnp.maximum(top, jnp.max(so, axis=0, keepdims=True))
        pd = jnp.exp2(sd - top)
        total = jnp.sum(pd, axis=0, keepdims=True)
        out = dot(vt[:, q0 : q0 + QB], pd.astype(bf16))
        if i:
            po = jnp.exp2(so - top)
            total = total + jnp.sum(po, axis=0, keepdims=True)
            out = out + dot(vt[:, 0:q0], po.astype(bf16))
        out = out / total
        ot[:, q0 : q0 + QB] = out
        lse[:, q0 : q0 + QB] = top + jnp.log2(total)
        low = out.astype(bf16)
        atts[2 * i] = low[:, 0:TOK]
        atts[2 * i + 1] = low[:, TOK:QB]
        after(2 * i)
        after(2 * i + 1)


def attend_backward(offs_ref, qk, vals, kn, kt, vn, qn, don, dor, ot, lse, dqkv, dk, dv, after):
    for s in range(NB):
        rows = slice(s * TOK, (s + 1) * TOK)
        vn[rows, :] = turned(vals[s])
        qn[rows, :] = turned(qk[s, 0:48, :])
        don[rows, :] = turned(dor[s])
        kt[:, rows] = qk[s, 48:96, :]
    last = SEQ // QB - 1
    for i in reversed(range(SEQ // QB)):
        q0 = i * QB
        qt = pair(qk, i, 0, 48)
        dot_t = pair(dor, i, 0, 48)
        start = segment_starts(offs_ref, q0, QB)
        level = lse[:, q0 : q0 + QB]
        inner = jnp.sum(dot_t.astype(f32) * ot[:, q0 : q0 + QB], axis=0, keepdims=True)
        q_n = qn[q0 : q0 + QB, :]
        do_n = don[q0 : q0 + QB, :]
        dq = None
        for a, b, diagonal in ([(0, q0, False)] if i else []) + [(q0, q0 + QB, True)]:
            scores = masked(dot(kn[a:b, :], qt) * SCALE_LOG2E, start, a, q0, diagonal)
            probs = jnp.exp2(scores - level)
            dp = dot(vn[a:b, :], dot_t)
            ds = (probs * (dp - inner)).astype(bf16)
            dv_part = dot(probs.astype(bf16), do_n)
            dk_part = dot(ds, q_n)
            if i == last:
                dk[a:b, :] = dk_part
                dv[a:b, :] = dv_part
            else:
                dk[a:b, :] += dk_part
                dv[a:b, :] += dv_part
            dq_part = dot(kt[:, a:b], ds)
            dq = dq_part if dq is None else dq + dq_part
        dq = (dq * SCALE).astype(bf16)
        for h in range(2):
            s = 2 * i + h
            rows = slice(s * TOK, (s + 1) * TOK)
            dqkv[s, 0:48, :] = dq[:, h * TOK : (h + 1) * TOK]
            dqkv[s, 48:96, :] = (jnp.transpose(dk[rows, :]) * SCALE).astype(bf16)
            dqkv[s, 96:144, :] = jnp.transpose(dv[rows, :]).astype(bf16)
        after(i)


def norm_parts(values):
    center = values - jnp.mean(values, axis=-1, keepdims=True)
    spread = jnp.mean(center * center, axis=-1, keepdims=True)
    rs = lax.rsqrt(spread + EPSILON)
    return center * rs, rs


def norm_back(grad, n, rs, gain):
    gg = grad * gain
    return rs * (
        gg - jnp.mean(gg, axis=-1, keepdims=True) - n * jnp.mean(gg * n, axis=-1, keepdims=True)
    )


def over_tokens(values):
    return jnp.sum(values, axis=0, keepdims=True)


ORDERS = (("x", "y", "z"), ("y", "z", "x"), ("z", "x", "y"))


class Sums:
    def __init__(self, group, ag, near, buf2, recv2, recv3, buf4, send, recv, own):
        self.group, self.ag, self.near = group, ag, near
        self.buf2, self.recv2, self.recv3, self.buf4 = buf2, recv2, recv3, buf4
        self.send, self.recv, self.own = send, recv, own
        self.core = lax.rem(lax.axis_index("rows"), 2)
        self.place = [[axis_place(a) for a in order] for order in ORDERS]
        keys = [(g, p) for g in range(3) for p in range(3)]
        self.live = {key: [] for key in keys}
        self.later = {key: [] for key in keys}
        self.used = {key: 0 for key in keys}
        self.mine = {}
        self.at = [0, 0, 0]
        self.sent = []
        self.shared = []
        self.stages = [
            self.near_first, self.near_second, self.across, self.third,
            self.back_across, self.back_near, self.back_far, self.back_last,
        ]

    def go(self, g, p, src, dst, device):
        n = self.used[g, p]
        self.used[g, p] = n + 1
        copy = remote(src, dst, self.send.at[g, p, n], self.recv.at[g, p, n], device)
        copy.start()
        self.sent.append(copy)
        return copy

    def step(self, *groups):
        for g in groups:
            k = self.at[g]
            if k >= len(self.stages):
                continue
            self.at[g] = k + 1
            for p in range(3):
                for copy in self.live[g, p]:
                    copy.wait_recv()
                self.live[g, p] = self.stages[k](g, p)

    def end(self):
        while min(self.at) < len(self.stages):
            self.step(*[g for g in (2, 0, 1) if self.at[g] == min(self.at)])
        for copies in self.live.values():
            for copy in copies:
                copy.wait_recv()
        for copy in self.shared:
            copy.wait_recv()
        for copy in self.sent:
            copy.wait_send()

    def there(self, p, axis, j):
        return lax.rem(self.place[p][axis] + j, 4)

    def ends(self, p):
        return axis_peer(ORDERS[p][0], 1), axis_peer(ORDERS[p][0], 3)

    def block(self, g, p, j, lo, size):
        quarter = GROUP_ROWS[g] // 12
        return pl.ds(p * quarter * 4 + self.there(p, 0, j) * quarter + lo, size)

    def near_first(self, g, p):
        right, left = self.ends(p)
        group, near = self.group[g], self.near[g]
        quarter = GROUP_ROWS[g] // 12
        half = quarter // 2
        first = [
            self.go(g, p, group.at[self.block(g, p, 2, 0, half)], near.at[p, pl.ds(0, half)], right),
            self.go(g, p, group.at[self.block(g, p, 2, half, half)], near.at[p, pl.ds(half, half)], left),
        ]
        self.later[g, p] = [
            self.go(g, p, group.at[self.block(g, p, 1, half, half)], near.at[p, pl.ds(quarter + half, half)], right),
            self.go(g, p, group.at[self.block(g, p, 3, 0, half)], near.at[p, pl.ds(2 * quarter, half)], left),
        ]
        return first

    def near_second(self, g, p):
        right, left = self.ends(p)
        group, near = self.group[g], self.near[g]
        quarter = GROUP_ROWS[g] // 12
        half = quarter // 2
        copies = []
        for j, lo, device in ((1, 0, right), (3, half, left)):
            rows = self.block(g, p, j, lo, half)
            both = group[rows].astype(f32) + near[p, lo : lo + half].astype(f32)
            group[rows] = both.astype(bf16)
            spot = near.at[p, pl.ds((quarter if j == 1 else 2 * quarter) + lo, half)]
            copies.append(self.go(g, p, group.at[rows], spot, device))
        return copies + self.later[g, p]

    def fan(self, g, p, axis, pick):
        copies = []
        for j in range(1, 4):
            src, dst = pick(j, self.there(p, axis, j))
            copies.append(self.go(g, p, src, dst, axis_peer(ORDERS[p][axis], j)))
        return copies

    def across(self, g, p):
        quarter = GROUP_ROWS[g] // 12
        size = quarter // 4
        near, buf2, recv2 = self.near[g], self.buf2[g], self.recv2[g]
        mine = self.group[g][self.block(g, p, 0, 0, quarter)].astype(f32)
        mine = mine + near[p, quarter : 2 * quarter].astype(f32) + near[p, 2 * quarter : 3 * quarter].astype(f32)
        buf2[p] = mine.astype(bf16)
        return self.fan(g, p, 1, lambda j, q: (buf2.at[p, pl.ds(q * size, size)], recv2.at[p, j - 1]))

    def third(self, g, p):
        size = GROUP_ROWS[g] // 48
        recv2, recv3 = self.recv2[g], self.recv3[g]
        acc = self.buf2[g][p, pl.ds(self.place[p][1] * size, size)].astype(f32)
        for j in range(3):
            acc = acc + recv2[p, j].astype(f32)
        here = self.place[p][2]
        recv3[p, here] = acc.astype(bf16)
        return self.fan(g, p, 2, lambda j, q: (recv3.at[p, here], recv3.at[p, here]))

    def spot(self, g, p, lo, size):
        base = sum(GROUP_ROWS[:g]) + p * (GROUP_ROWS[g] // 3)
        return self.ag.at[self.core, pl.ds(base + lo, size)]

    def back_across(self, g, p):
        size = GROUP_ROWS[g] // 48
        recv3, buf4 = self.recv3[g], self.buf4[g]
        acc = recv3[p, 0].astype(f32)
        for j in range(1, 4):
            acc = acc + recv3[p, j].astype(f32)
        buf4[p] = acc.astype(bf16)
        spot = self.spot(g, p, (self.place[p][0] * 4 + self.place[p][1]) * size, size)
        copies = self.fan(g, p, 1, lambda j, q: (buf4.at[p], spot))
        self.mine[g, p] = pltpu.make_async_copy(buf4.at[p], spot, self.own.at[g, p])
        self.mine[g, p].start()
        return copies

    def whole(self, g, p, j, lo=0, size=None):
        quarter = GROUP_ROWS[g] // 12
        return self.spot(g, p, self.there(p, 0, j) * quarter + lo, size or quarter)

    def share(self, g, p, j):
        spot = self.whole(g, p, j)
        self.shared.append(self.go(g, p, spot, spot, sibling()))

    def back_near(self, g, p):
        self.mine[g, p].wait()
        right, left = self.ends(p)
        spot = self.whole(g, p, 0)
        copies = [self.go(g, p, spot, spot, right), self.go(g, p, spot, spot, left)]
        self.share(g, p, 0)
        return copies

    def back_far(self, g, p):
        right, left = self.ends(p)
        half = GROUP_ROWS[g] // 24
        low = self.whole(g, p, 3, 0, half)
        high = self.whole(g, p, 1, half, half)
        copies = [self.go(g, p, low, low, right), self.go(g, p, high, high, left)]
        self.share(g, p, 1)
        self.share(g, p, 3)
        return copies

    def back_last(self, g, p):
        self.share(g, p, 2)
        return []


def exchange(src, dst, send, recv):
    r = lax.axis_index("rows")
    s = lax.axis_index("seq")
    copies = []
    for d in range(1, 16):
        peer = seq_peer(d)
        copy = remote(src.at[peer], dst.at[s], send.at[d], recv.at[d], (r, peer))
        copy.start()
        copies.append(copy)
    dst[s] = src[s]
    return copies


def hand_on(src, dst, send, recv, block):
    r = lax.axis_index("rows")
    s = lax.axis_index("seq")
    d = lax.rem(block - s + 16, 16)

    @pl.when(s != block)
    def _():
        remote(src.at[block], dst.at[s], send.at[d], recv.at[d], (r, block)).start()

    @pl.when(s == block)
    def _():
        dst[s] = src[block]


def handed(src, dst, send, recv):
    r = lax.axis_index("rows")
    s = lax.axis_index("seq")
    return [remote(src.at[0], dst.at[s], send.at[d], recv.at[d], (r, seq_peer(d))) for d in range(1, 16)]


class Vectors:
    def __init__(self, buf, slots, send_sem, recv_sem):
        self.buf, self.slots, self.send_sem, self.recv_sem = buf, slots, send_sem, recv_sem
        self.at = 0
        self.live = []

    def step(self):
        k = self.at
        self.at = k + 1
        for copy in self.live:
            copy.wait()
        self.live = []
        if k == 0:
            value = self.buf[0]
        else:
            value = self.slots[k - 1, 0]
            for j in range(1, 4 if k < 4 else 2):
                value = value + self.slots[k - 1, j]
        if k == 4:
            self.buf[1] = value
            return
        here = axis_place("xyz"[k]) if k < 3 else lax.rem(lax.axis_index("rows"), 2)
        devices = [axis_peer("xyz"[k], j) for j in range(1, 4)] if k < 3 else [sibling()]
        self.slots[k, here] = value
        for j, device in enumerate(devices):
            spot = self.slots.at[k, here]
            copy = remote(spot, spot, self.send_sem.at[k, j], self.recv_sem.at[k, j], device)
            copy.start()
            self.live.append(copy)


def block_kernel(
    offs_h, x_h, dy_h, ln1g_h, ln1b_h, bq_h, bv_h, bout_h, ln2g_h, ln2b_h, bup_h, bdown_h,
    wqkv_h, wout_h, wup_h, wdown_h,
    out_h, ig_h, ag, vecs_h,
    offs, x_ref, dy_ref, ln1g, ln1b, bq, bv, bout, ln2g, ln2b, bup, bdown,
    out_ref, ig_ref, vecs,
    wqkv, wout, wup, wdown, wsem,
    qkt, vals, rqk, rv, kn, vt, ot, lse, atts, ratt,
    h1t, h1ts, n1, rs1, h2t, h2ts, dys, actt, actts, gp, gps, gb, gbs, attts, gres,
    gattt, rda, kt, vn, qn, don, dk, dv, dqkv, rdq, dqs,
    asend, arecv, ssend, srecv,
    *rest,
):
    group, near, buf2, recv2, recv3, buf4 = [rest[3 * k : 3 * k + 3] for k in range(6)]
    (gsend, grecv, gown, vbuf, vrecv, vsend, vrsem, lbuf, lrecv, lsend, lrsem, osem) = rest[18:]
    loads = {}

    def load(name, src, dst):
        copy = pltpu.make_async_copy(src, dst, wsem.at[len(loads)])
        copy.start()
        loads[name] = copy

    load("x", x_h, x_ref)
    load("ln1g", ln1g_h, ln1g)
    load("ln1b", ln1b_h, ln1b)
    for t in (1, 0, 2):
        cols = pl.ds(t * D, D)
        load(f"qkv{t}", wqkv_h.at[:, cols], wqkv.at[:, cols])
    load("bq", bq_h, bq)
    load("bv", bv_h, bv)
    load("dy", dy_h, dy_ref)
    load("offs", offs_h, offs)
    load("out", wout_h, wout)
    for name, src, dst in (
        ("bout", bout_h, bout), ("ln2g", ln2g_h, ln2g), ("ln2b", ln2b_h, ln2b),
        ("bup", bup_h, bup), ("bdown", bdown_h, bdown),
    ):
        load(name, src, dst)
    load("up", wup_h, wup)
    load("down", wdown_h, wdown)
    stores = []

    def ready(*names):
        for name in names:
            loads[name].wait()

    def store(src, dst):
        copy = pltpu.make_async_copy(src, dst, osem.at[len(stores)])
        copy.start()
        stores.append(copy)

    bar, count = greet(True, ("y",))
    vecg = vbuf.at[0]
    vecl = lbuf.at[0]
    early = Vectors(vbuf, vrecv, vsend, vrsem)
    late = Vectors(lbuf, lrecv, lsend, lrsem)
    sums = Sums(group, ag, near, buf2, recv2, recv3, buf4, gsend, grecv, gown)

    def line(ref):
        return ref[...].astype(f32).reshape(1, D)

    core = lax.rem(lax.axis_index("rows"), 2)
    other = 1 - core
    sib = sibling()
    to_sib = []

    def send_sib(n, src, dst):
        copy = remote(src, dst, ssend.at[n], srecv.at[n], sib)
        copy.start()
        to_sib.append(copy)

    ready("x", "ln1g", "ln1b")
    x = x_ref[...].astype(f32)
    n, rs = norm_parts(x)
    n1[...] = n
    rs1[...] = rs
    h1f = n * line(ln1g) + line(ln1b)
    h1 = h1f.astype(bf16)
    h1t[...] = jnp.transpose(h1f).astype(bf16)
    for t in (1, 0, 2):
        ready(f"qkv{t}")
        y = dot(h1, wqkv[:, t * D : (t + 1) * D])
        if t == 0:
            ready("bq")
            y = y + line(bq)
        if t == 2:
            ready("bv")
            y = y + line(bv)
        low = jnp.transpose(y).astype(bf16).reshape(H, HS, TOK)
        if t < 2:
            qkt[:, t * HS : (t + 1) * HS, :] = low
        else:
            vals[...] = low
        if t == 0:
            pl.semaphore_wait(bar, count)
            moved = exchange(qkt, rqk, asend.at[0], arecv.at[0])
    moved += exchange(vals, rv, asend.at[1], arecv.at[1])
    send_sib(0, h1t, h1ts)
    ready("dy", "offs")
    send_sib(1, dy_ref, dys)
    for copy in moved:
        copy.wait()

    attend_forward(
        offs, rqk, rv, kn, vt, ot, lse, atts,
        lambda block: hand_on(atts, ratt, asend.at[2], arecv.at[2], block),
    )
    moved = handed(atts, ratt, asend.at[2], arecv.at[2])
    ready("out", "bout", "ln2g", "ln2b", "bup", "bdown", "up", "down")
    for copy in moved:
        copy.wait()

    att = jnp.transpose(ratt[...].reshape(D, TOK).astype(f32)).astype(bf16)
    send_sib(2, ratt.at[pl.ds(other * 8, 8)], attts)
    resid = x_ref[...].astype(f32) + dot(att, wout[...]) + line(bout)
    n2, rs2 = norm_parts(resid)
    h2f = n2 * line(ln2g) + line(ln2b)
    h2 = h2f.astype(bf16)
    h2t[...] = jnp.transpose(h2f).astype(bf16)
    send_sib(3, h2t, h2ts)
    dy = dy_ref[...]
    down = None
    dh2 = None
    for c in range(4):
        cols = slice(c * D, (c + 1) * D)
        pre = dot(h2, wup[:, cols]) + bup[cols].astype(f32).reshape(1, D)
        square = pre * pre
        t = jnp.tanh(GELU_C * (pre + GELU_A * (square * pre)))
        act = 0.5 * pre * (1.0 + t)
        slope = 0.5 * (1.0 + t) + (0.5 * GELU_C) * pre * (1.0 - t * t) * (1.0 + (3.0 * GELU_A) * square)
        part = dot(act.astype(bf16), wdown[cols, :])
        down = part if down is None else down + part
        actt[c] = jnp.transpose(act).astype(bf16)
        gpre = (dot_nt(dy, wdown[cols, :]) * slope).astype(bf16)
        gp[c] = gpre
        vecg[BUP + c : BUP + c + 1, :] = over_tokens(gpre.astype(f32))
        part = dot_nt(gpre, wup[:, cols])
        dh2 = part if dh2 is None else dh2 + part
    send_sib(4, actt.at[pl.ds(other * 2, 2)], actts)
    send_sib(5, gp.at[pl.ds(other * 2, 2)], gps)
    out_ref[...] = (resid + down + line(bdown)).astype(bf16)
    store(out_ref, out_h)
    vecg[BDOWN : BDOWN + 1, :] = over_tokens(dy.astype(f32))
    vecg[LN2G : LN2G + 1, :] = over_tokens(dh2 * n2)
    vecg[LN2B : LN2B + 1, :] = over_tokens(dh2)
    grad = dy.astype(f32) + norm_back(dh2, n2, rs2, line(ln2g))
    gres[...] = grad
    branch = grad.astype(bf16)
    gb[...] = branch
    vecg[BOUT : BOUT + 1, :] = over_tokens(branch.astype(f32))
    early.step()
    gattt[...] = jnp.transpose(dot_nt(branch, wout[...])).astype(bf16).reshape(H, HS, TOK)
    moved = exchange(gattt, rda, asend.at[3], arecv.at[3])
    send_sib(6, gb, gbs)

    for k in (1, 2, 3, 4, 5, 6):
        to_sib[k].wait()
    dy2 = jnp.concatenate([dy, dys[...]], axis=0)
    for j in range(2):
        left = jnp.concatenate([actt[core * 2 + j], actts[j]], axis=1)
        res = dot(left, dy2).astype(bf16)
        for t in range(6):
            lo = t * 1536 + j * D
            group[0][lo : lo + D, :] = res[:, t * TOK : (t + 1) * TOK]
    sums.step(0)
    left = jnp.concatenate([h2t[...], h2ts[...]], axis=1)
    for j in range(2):
        right = jnp.concatenate([gp[core * 2 + j], gps[j]], axis=0)
        res = dot(left, right).astype(bf16)
        for t in range(6):
            lo = (j * 6 + t) * D
            group[1][lo : lo + D, :] = res[:, t * TOK : (t + 1) * TOK]
    left = jnp.concatenate(
        [ratt[pl.ds(core * 8, 8)].reshape(384, TOK), attts[...].reshape(384, TOK)], axis=1
    )
    right = jnp.concatenate([gb[...], gbs[...]], axis=0)
    res = dot(left, right).astype(bf16)
    for t in range(6):
        lo = OUT_ROW + t * 384
        group[1][lo : lo + 384, :] = res[:, t * TOK : (t + 1) * TOK]
    sums.step(1)

    for copy in moved:
        copy.wait()
    def between(i):
        for half in (0, 1):
            hand_on(dqkv, rdq, asend.at[4], arecv.at[4], 2 * i + half)
        if i == 4:
            early.step()

    attend_backward(offs, rqk, rv, kn, kt, vn, qn, don, rda, ot, lse, dqkv, dk, dv, between)
    sums.step(0)
    early.step()
    sums.step(1)
    for copy in handed(dqkv, rdq, asend.at[4], arecv.at[4]):
        copy.wait()
    send_sib(7, rdq.at[pl.ds(other * 8, 8)], dqs)

    dh1t = None
    ones = jnp.ones((8, TOK), bf16)
    for t in range(3):
        grad_t = rdq[:, t * HS : (t + 1) * HS, :].reshape(D, TOK)
        part = dot(wqkv[:, t * D : (t + 1) * D], grad_t)
        dh1t = part if dh1t is None else dh1t + part
        if t != 1:
            row = BQ if t == 0 else BV
            vecl[row : row + 1, :] = dot_nt(ones, grad_t)[0:1, :]
    to_sib[0].wait()
    to_sib[7].wait()
    left = jnp.concatenate([h1t[...], h1ts[...]], axis=1)
    for t in range(3):
        mine = rdq[pl.ds(core * 8, 8), t * HS : (t + 1) * HS, :].reshape(384, TOK)
        theirs = dqs[:, t * HS : (t + 1) * HS, :].reshape(384, TOK)
        res = dot_nt(left, jnp.concatenate([mine, theirs], axis=1)).astype(bf16)
        for u in range(3):
            lo = (t * 3 + u) * D
            group[2][lo : lo + D, :] = res[:, u * TOK : (u + 1) * TOK]
    sums.step(2)

    dh1 = jnp.transpose(dh1t)
    n = n1[...]
    vecl[LN1G : LN1G + 1, :] = over_tokens(dh1 * n)
    vecl[LN1B : LN1B + 1, :] = over_tokens(dh1)
    vecl[4:8, :] = jnp.zeros((4, D), f32)
    late.step()
    ig_ref[...] = (gres[...] + norm_back(dh1, n, rs1[...], line(ln1g))).astype(bf16)
    store(ig_ref, ig_h)
    early.step()

    sums.step(0, 2)
    late.step()
    sums.step(1, 2)
    late.step()
    early.step()
    vecs[0] = vbuf[1]
    sums.step(0, 2)
    late.step()
    sums.step(1, 0, 2)
    late.step()
    vecs[1] = lbuf[1]
    store(vecs, vecs_h)
    sums.step(1, 0, 2)
    sums.step(1, 0, 2)
    sums.end()
    for copy in stores:
        copy.wait()


VMEM = pl.BlockSpec(memory_space=pltpu.VMEM)
SMEM = pl.BlockSpec(memory_space=pltpu.SMEM)
ANY = pl.BlockSpec(memory_space=pl.ANY)


def call_block(offsets, x, dy, vectors, weights):
    v = pltpu.VMEM
    dma = pltpu.SemaphoreType.DMA
    shape = jax.ShapeDtypeStruct
    return pl.pallas_call(
        block_kernel,
        out_shape=(
            shape((TOK, D), bf16),
            shape((TOK, D), bf16),
            shape((2, ALL_ROWS, TOK), bf16),
            shape((2, VROWS, D), f32),
        ),
        in_specs=[ANY] * 16,
        out_specs=(ANY, ANY, ANY, ANY),
        scratch_shapes=[
            pltpu.SMEM((1, 8), jnp.int32), v((TOK, D), bf16), v((TOK, D), bf16),
            *[v((FF if k == 7 else D,), bf16) for k in range(9)],
            v((TOK, D), bf16), v((TOK, D), bf16), v((2, VROWS, D), f32),
            v((D, 3 * D), bf16), v((D, D), bf16), v((D, FF), bf16), v((FF, D), bf16), dma((20,)),
            v((NB, 96, TOK), bf16), v((NB, HS, TOK), bf16), v((NB, 96, TOK), bf16), v((NB, HS, TOK), bf16),
            v((SEQ, HS), bf16), v((HS, SEQ), bf16),
            v((HS, SEQ), f32), v((1, SEQ), f32), v((NB, HS, TOK), bf16), v((NB, HS, TOK), bf16),
            v((D, TOK), bf16), v((D, TOK), bf16), v((TOK, D), f32), v((TOK, 1), f32),
            v((D, TOK), bf16), v((D, TOK), bf16), v((TOK, D), bf16),
            v((4, D, TOK), bf16), v((2, D, TOK), bf16), v((4, TOK, D), bf16), v((2, TOK, D), bf16),
            v((TOK, D), bf16), v((TOK, D), bf16), v((8, HS, TOK), bf16), v((TOK, D), f32),
            v((NB, HS, TOK), bf16), v((NB, HS, TOK), bf16),
            v((HS, SEQ), bf16), v((SEQ, HS), bf16), v((SEQ, HS), bf16), v((SEQ, HS), bf16),
            v((SEQ, HS), f32), v((SEQ, HS), f32),
            v((NB, 144, TOK), bf16), v((NB, 144, TOK), bf16), v((8, 144, TOK), bf16),
            dma((5, 16)), dma((5, 16)), dma((8,)), dma((8,)),
            *[v((r, TOK), bf16) for r in GROUP_ROWS],
            *[v((3, r // 4, TOK), bf16) for r in GROUP_ROWS],
            *[v((3, r // 12, TOK), bf16) for r in GROUP_ROWS],
            *[v((3, 3, r // 48, TOK), bf16) for r in GROUP_ROWS],
            *[v((3, 4, r // 48, TOK), bf16) for r in GROUP_ROWS],
            *[v((3, r // 48, TOK), bf16) for r in GROUP_ROWS],
            dma((3, 3, 23)), dma((3, 3, 23)), dma((3, 3)),
            v((2, VROWS, D), f32), v((4, 4, VROWS, D), f32), dma((4, 3)), dma((4, 3)),
            v((2, VROWS, D), f32), v((4, 4, VROWS, D), f32), dma((4, 3)), dma((4, 3)), dma((3,)),
        ],
        compiler_params=pltpu.CompilerParams(
            collective_id=1, has_side_effects=True, vmem_limit_bytes=58 * 2**20
        ),
    )(offsets, x, dy, *vectors, *weights)


def widen_kernel(ag, vecs_h, done_h, ig_h, wqkv, wout, wup, wdown, out_h, grad_h, *rest):
    small_h, small, (vecs, inb, outb, isem, osem, vsem, ssem) = rest[:9], rest[9:18], rest[18:]
    passed = [
        pltpu.make_async_copy(done_h, out_h, vsem.at[0]),
        pltpu.make_async_copy(ig_h, grad_h, vsem.at[1]),
    ]
    for copy in passed:
        copy.start()
    fetch = pltpu.make_async_copy(vecs_h, vecs, vsem.at[2])
    fetch.start()

    def narrow():
        fetch.wait()
        fill()
        for k in range(9):
            copy = pltpu.make_async_copy(small[k], small_h[k], ssem.at[k])
            copy.start()
            passed.append(copy)

    def fill():
        places = ((1, LN1G), (1, LN1B), (1, BQ), (1, BV), (0, BOUT), (0, LN2G), (0, LN2B), (0, BUP), (0, BDOWN))
        for ref, (k, row) in zip(small, places):
            if row == BUP:
                for c in range(4):
                    ref[c * D : (c + 1) * D] = vecs[0, BUP + c : BUP + c + 1, :].reshape(D)
            else:
                ref[...] = vecs[k, row : row + 1, :].reshape(D)

    tasks = []
    for c in range(2):
        for j in range(2):
            for h in range(2):
                rows = [(h * 3 + t) * 1536 + j * D for t in range(3)]
                tasks.append((c, rows, wdown.at[pl.ds(c * 1536 + j * D, D), pl.ds(h * 384, 384)]))
        for h in range(4):
            rows = [GROUP_ROWS[0] + (h * 3 + t) * D for t in range(3)]
            tasks.append((c, rows, wup.at[:, pl.ds(c * 1536 + h * 384, 384)]))
        for h in range(3):
            rows = [GROUP_ROWS[0] + GROUP_ROWS[1] + (h * 3 + t) * D for t in range(3)]
            tasks.append((c, rows, wqkv.at[:, pl.ds(h * D + c * 384, 384)]))
        for h in range(2):
            rows = [GROUP_ROWS[0] + OUT_ROW + (h * 3 + t) * 384 for t in range(3)]
            tasks.append((c, rows, wout.at[pl.ds(c * 384, 384), pl.ds(h * 384, 384)]))
    slots = WIDEN_SLOTS

    def height(k):
        return 384 if tasks[k][2].shape[0] == 384 else D

    def load(k):
        c, rows, _ = tasks[k]
        size = height(k)
        for t, lo in enumerate(rows):
            pltpu.make_async_copy(
                ag.at[c, pl.ds(lo, size)], inb.at[k % slots, t, pl.ds(0, size)], isem.at[k % slots, t]
            ).start()

    def load_wait(k):
        c, rows, _ = tasks[k]
        size = height(k)
        for t, lo in enumerate(rows):
            pltpu.make_async_copy(
                ag.at[c, pl.ds(lo, size)], inb.at[k % slots, t, pl.ds(0, size)], isem.at[k % slots, t]
            ).wait()

    def store(k):
        return pltpu.make_async_copy(
            outb.at[k % slots, pl.ds(0, height(k))], tasks[k][2], osem.at[k % slots]
        )

    for k in range(slots - 1):
        load(k)
    narrow()
    for k in range(len(tasks)):
        if k + slots - 1 < len(tasks):
            load(k + slots - 1)
        load_wait(k)
        if k >= slots:
            store(k - slots).wait()
        size = height(k)
        for t in range(3):
            outb[k % slots, 0:size, t * TOK : (t + 1) * TOK] = inb[k % slots, t, 0:size, :].astype(f32)
        store(k).start()
    for k in range(len(tasks) - slots, len(tasks)):
        store(k).wait()
    for copy in passed:
        copy.wait()


def call_widen(ag, vecs, out, ig):
    v = pltpu.VMEM
    dma = pltpu.SemaphoreType.DMA
    shape = jax.ShapeDtypeStruct
    return pl.pallas_call(
        widen_kernel,
        out_shape=(
            shape((D, 3 * D), f32), shape((D, D), f32), shape((D, FF), f32), shape((FF, D), f32),
            shape((TOK, D), bf16), shape((TOK, D), bf16),
        ) + tuple(shape((FF if k == 7 else D,), f32) for k in range(9)),
        in_specs=[ANY] * 4,
        out_specs=(ANY,) * 15,
        scratch_shapes=[
            *[v((FF if k == 7 else D,), f32) for k in range(9)], v((2, VROWS, D), f32),
            v((WIDEN_SLOTS, 3, D, TOK), bf16), v((WIDEN_SLOTS, D, 384), f32), dma((WIDEN_SLOTS, 3)), dma((WIDEN_SLOTS,)),
            dma((3,)), dma((9,)),
        ],
        compiler_params=pltpu.CompilerParams(vmem_limit_bytes=58 * 2**20),
    )(ag, vecs, out, ig)


def local(
    block_input, offsets, ln1_gain, ln1_bias, w_qkv, bias_query, bias_value, w_out, bias_out,
    ln2_gain, ln2_bias, w_up, bias_up, w_down, bias_down, cotangent,
):
    out, ig, ag, vecs = call_block(
        offsets, block_input.reshape(TOK, D), cotangent.reshape(TOK, D),
        (ln1_gain, ln1_bias, bias_query, bias_value, bias_out, ln2_gain, ln2_bias, bias_up, bias_down),
        (w_qkv, w_out, w_up, w_down),
    )
    wide = call_widen(ag, vecs, out, ig)
    g_qkv, g_out, g_up, g_down, out, ig = wide[:6]
    s = wide[6:]
    return (
        out.reshape(1, TOK, D), ig.reshape(1, TOK, D),
        s[0], s[1], g_qkv, s[2], s[3], g_out, s[4], s[5], s[6], g_up, s[7], g_down, s[8],
    )


def solution(mesh):
    tokens = P("rows", "seq", None)
    return jax.shard_map(
        local,
        mesh=mesh,
        in_specs=(tokens, P("rows", None)) + (P(),) * 13 + (tokens,),
        out_specs=(tokens, tokens) + (P(),) * 13,
        check_vma=False,
    )
```

```python
import functools

import jax
import jax.numpy as jnp
from jax import lax
from jax.experimental import pallas as pl
from jax.experimental.pallas import tpu as pltpu
from jax.sharding import PartitionSpec as P

MESH = pl.DeviceIdType.MESH
f32 = jnp.float32
bf16 = jnp.bfloat16

D = 768
H = 16
FF = 3072
HS = 48
SEQ = 2048
TOK = 128
NB = 16
QB = 256
CUT_DOWN = (80, 64)
CUT_UP = (80, 64)
CUT_OUT = (32, 16)
SHARE = 112
HEAD_ROWS = 4 * SHARE
ROWS_LAST = SHARE + sum(CUT_OUT)
WAYS_DOWN = ((0, 48, "xzy"), (48, 48, "zyx"), (96, 48, "yxz"))
WAYS_UP = WAYS_DOWN
WAYS_LAST = ((0, 64, "xzy"), (64, 48, "zyx"), (112, 48, "yxz"))
SCALE = HS**-0.5
SCALE_LOG2E = SCALE * 1.4426950408889634
NEGATIVE = -1e30
EPSILON = 1e-05
GELU_C = 0.7978845608028654
GELU_A = 0.044715

LN1G, LN1B, BQ, BV = 0, 1, 2, 3
BOUT, LN2G, LN2B, BDOWN, BUP = 0, 1, 2, 3, 4
VROWS = 8
WIDEN_SLOTS = 6


def dot(a, b):
    return jnp.dot(a, b, preferred_element_type=f32)


def dot_nt(a, b):
    return lax.dot_general(a, b, (((1,), (1,)), ((), ())), preferred_element_type=f32)


def turned(block):
    return jnp.transpose(block.astype(f32)).astype(bf16)


def coords():
    r = lax.axis_index("rows")
    s = lax.axis_index("seq")
    return lax.div(r, 2), lax.rem(r, 2), lax.div(s, 4), lax.rem(s, 4)


def device_at(y, c, z, x):
    return (y * 2 + c, z * 4 + x)


def remote(src, dst, send, recv, device):
    return pltpu.make_async_remote_copy(
        src_ref=src, dst_ref=dst, send_sem=send, recv_sem=recv, device_id=device, device_id_type=MESH
    )


def seq_peer(d):
    s = lax.axis_index("seq")
    return lax.rem(s + d, 16)


def axis_peer(axis, j):
    y, c, z, x = coords()
    if axis == "y":
        y = lax.rem(y + j, 4)
    elif axis == "z":
        z = lax.rem(z + j, 4)
    else:
        x = lax.rem(x + j, 4)
    return device_at(y, c, z, x)


def axis_place(axis):
    y, c, z, x = coords()
    return {"y": y, "z": z, "x": x}[axis]


def sibling():
    y, c, z, x = coords()
    return device_at(y, 1 - c, z, x)


def greet():
    bar = pltpu.get_barrier_semaphore()
    r = lax.axis_index("rows")
    s = lax.axis_index("seq")
    devices = [(r, seq_peer(d)) for d in range(1, 16)] + [(lax.rem(r + d, 8), s) for d in range(1, 8)]
    for device in devices:
        pl.semaphore_signal(bar, inc=1, device_id=device, device_id_type=MESH)
    return bar, len(devices)


def masked(scores, start, key0, query0, diagonal):
    key = lax.broadcasted_iota(jnp.int32, scores.shape, 0) + key0
    ok = key >= start
    if diagonal:
        query = lax.broadcasted_iota(jnp.int32, scores.shape, 1) + query0
        ok = ok & (key <= query)
    return jnp.where(ok, scores, NEGATIVE)


def segment_starts(offs_ref, query0, count):
    place = lax.broadcasted_iota(jnp.int32, (1, count), 1) + query0
    start = jnp.zeros((1, count), jnp.int32)
    for j in range(8):
        o = offs_ref[0, j]
        start = jnp.where(place >= o, o, start)
    return start


def pair(ref, i, lo, hi):
    return jnp.concatenate([ref[2 * i, lo:hi, :], ref[2 * i + 1, lo:hi, :]], axis=1)


def attend_forward(offs_ref, qk, vals, kn, vt, ot, lse, atts, after):
    for s in range(NB):
        kn[s * TOK : (s + 1) * TOK, :] = turned(qk[s, 48:96, :])
        vt[:, s * TOK : (s + 1) * TOK] = vals[s]
    for i in range(SEQ // QB):
        q0 = i * QB
        qt = pair(qk, i, 0, 48)
        start = segment_starts(offs_ref, q0, QB)
        sd = masked(dot(kn[q0 : q0 + QB, :], qt) * SCALE_LOG2E, start, q0, q0, True)
        top = jnp.max(sd, axis=0, keepdims=True)
        if i:
            so = masked(dot(kn[0:q0, :], qt) * SCALE_LOG2E, start, 0, q0, False)
            top = jnp.maximum(top, jnp.max(so, axis=0, keepdims=True))
        pd = jnp.exp2(sd - top)
        total = jnp.sum(pd, axis=0, keepdims=True)
        out = dot(vt[:, q0 : q0 + QB], pd.astype(bf16))
        if i:
            po = jnp.exp2(so - top)
            total = total + jnp.sum(po, axis=0, keepdims=True)
            out = out + dot(vt[:, 0:q0], po.astype(bf16))
        out = out / total
        ot[:, q0 : q0 + QB] = out
        lse[:, q0 : q0 + QB] = top + jnp.log2(total)
        low = out.astype(bf16)
        atts[2 * i] = low[:, 0:TOK]
        atts[2 * i + 1] = low[:, TOK:QB]
        after(2 * i)
        after(2 * i + 1)


def attend_backward(offs_ref, qk, vals, kn, kt, vn, qn, don, dor, ot, lse, dqkv, dk, dv, after):
    for s in range(NB):
        rows = slice(s * TOK, (s + 1) * TOK)
        vn[rows, :] = turned(vals[s])
        qn[rows, :] = turned(qk[s, 0:48, :])
        don[rows, :] = turned(dor[s])
        kt[:, rows] = qk[s, 48:96, :]
    last = SEQ // QB - 1
    for i in reversed(range(SEQ // QB)):
        q0 = i * QB
        qt = pair(qk, i, 0, 48)
        dot_t = pair(dor, i, 0, 48)
        start = segment_starts(offs_ref, q0, QB)
        level = lse[:, q0 : q0 + QB]
        inner = jnp.sum(dot_t.astype(f32) * ot[:, q0 : q0 + QB], axis=0, keepdims=True)
        q_n = qn[q0 : q0 + QB, :]
        do_n = don[q0 : q0 + QB, :]
        dq = None
        for a, b, diagonal in ([(0, q0, False)] if i else []) + [(q0, q0 + QB, True)]:
            scores = masked(dot(kn[a:b, :], qt) * SCALE_LOG2E, start, a, q0, diagonal)
            probs = jnp.exp2(scores - level)
            dp = dot(vn[a:b, :], dot_t)
            ds = (probs * (dp - inner)).astype(bf16)
            dv_part = dot(probs.astype(bf16), do_n)
            dk_part = dot(ds, q_n)
            if i == last:
                dk[a:b, :] = dk_part
                dv[a:b, :] = dv_part
            else:
                dk[a:b, :] += dk_part
                dv[a:b, :] += dv_part
            dq_part = dot(kt[:, a:b], ds)
            dq = dq_part if dq is None else dq + dq_part
        dq = (dq * SCALE).astype(bf16)
        for h in range(2):
            s = 2 * i + h
            rows = slice(s * TOK, (s + 1) * TOK)
            dqkv[s, 0:48, :] = dq[:, h * TOK : (h + 1) * TOK]
            dqkv[s, 48:96, :] = (jnp.transpose(dk[rows, :]) * SCALE).astype(bf16)
            dqkv[s, 96:144, :] = jnp.transpose(dv[rows, :]).astype(bf16)
        after(i)


def norm_parts(values):
    center = values - jnp.mean(values, axis=-1, keepdims=True)
    spread = jnp.mean(center * center, axis=-1, keepdims=True)
    rs = lax.rsqrt(spread + EPSILON)
    return center * rs, rs


def norm_back(grad, n, rs, gain):
    gg = grad * gain
    return rs * (
        gg - jnp.mean(gg, axis=-1, keepdims=True) - n * jnp.mean(gg * n, axis=-1, keepdims=True)
    )


def over_tokens(values):
    return jnp.sum(values, axis=0, keepdims=True)


def arrived(gauge, sem):
    pltpu.make_async_copy(gauge, gauge, sem).wait()


class Steps:
    def __init__(self, send, recv):
        self.send, self.recv = send, recv
        self.sent = []
        self.live = []
        self.at = 0

    def go(self, group, src, dst, device):
        remote(src, dst, self.send.at[group], self.recv.at[group], device).start()

    def expect(self, group, gauge):
        self.live.append((group, gauge))
        self.sent.append((group, gauge))

    def collect(self):
        for group, gauge in self.live:
            arrived(gauge, self.recv.at[group])
        self.live = []

    def step(self):
        self.collect()
        k = self.at
        self.at = k + 1
        self.run(k)

    def done(self):
        for group, gauge in self.sent:
            arrived(gauge, self.send.at[group])
        self.sent = []


class Scatter(Steps):
    def __init__(self, cuts, parts, recv1, mid, recv2, share, send, recv):
        super().__init__(send, recv)
        self.cuts, self.parts, self.recv1, self.mid, self.recv2, self.share = cuts, parts, recv1, mid, recv2, share

    def put(self, value, offset):
        at, rows = 0, value.shape[0]
        while at < rows:
            k = 0 if offset < 16 * self.cuts[0] else 1
            inside = offset - k * 16 * self.cuts[0]
            block, lo = inside // self.cuts[k], inside % self.cuts[k]
            size = min(self.cuts[k] - lo, rows - at)
            self.parts[k][block // 4, block % 4, lo : lo + size, :] = value[at : at + size]
            at += size
            offset += size

    def run(self, k):
        z, x = axis_place("z"), axis_place("x")
        first, second = self.parts
        if k == 0:
            for j in range(1, 4):
                self.go(0, first.at[:, lax.rem(x + j, 4)], self.recv1[0].at[j - 1], axis_peer("x", j))
                self.go(1, second.at[lax.rem(z + j, 4)], self.recv1[1].at[j - 1], axis_peer("z", j))
            for n in range(2):
                self.expect(n, self.recv1[n])
        elif k == 1:
            for n, mine in enumerate((first[:, x], second[z])):
                acc = mine.astype(f32)
                for j in range(3):
                    acc = acc + self.recv1[n][j].astype(f32)
                self.mid[n][...] = acc.astype(bf16)
            for j in range(1, 4):
                self.go(2, self.mid[0].at[lax.rem(z + j, 4)], self.recv2[0].at[j - 1], axis_peer("z", j))
                self.go(3, self.mid[1].at[lax.rem(x + j, 4)], self.recv2[1].at[j - 1], axis_peer("x", j))
            for n in range(2):
                self.expect(2 + n, self.recv2[n])
        else:
            lo = 0
            for n, here in enumerate((z, x)):
                acc = self.mid[n][here].astype(f32)
                for j in range(3):
                    acc = acc + self.recv2[n][j].astype(f32)
                self.share[lo : lo + self.cuts[n], :] = acc.astype(bf16)
                lo += self.cuts[n]


class Spread(Steps):
    def __init__(self, share, ag, ways, send, recv, own):
        super().__init__(send, recv)
        self.share, self.ag, self.ways, self.own = share, ag, ways, own

    def spot(self, lo, size, whole, **at):
        core = lax.rem(lax.axis_index("rows"), 2)
        index = [at[a] if a in at else slice(None) if a in whole else axis_place(a) for a in "zxy"]
        return self.ag.at[(core, *index, pl.ds(lo, size))]

    def pass_on(self, spot):
        self.go(4, spot, spot, sibling())

    def run(self, k):
        ag = self.ag
        if k == 1:
            self.kept.wait()
        for lo, size, order in self.ways:
            last = order[2]
            here = axis_place(last)
            if k == 0:
                for j in range(1, 4):
                    self.go(0, self.share.at[pl.ds(lo, size)], self.spot(lo, size, ""), axis_peer(order[0], j))
            elif k == 1:
                spot = self.spot(lo, size, order[0])
                for j in range(1, 4):
                    self.go(1, spot, spot, axis_peer(order[1], j))
            elif k == 2:
                spot = self.spot(lo, size, order[:2])
                self.go(2, spot, spot, axis_peer(last, 1))
                self.go(2, spot, spot, axis_peer(last, 3))
                self.pass_on(spot)
            elif k == 3:
                before, after = lax.rem(here + 3, 4), lax.rem(here + 1, 4)
                cut = "x" if last == "z" else "z"
                low = self.spot(lo, size, order[:2], **{last: before, cut: pl.ds(0, 2)})
                high = self.spot(lo, size, order[:2], **{last: after, cut: pl.ds(2, 2)})
                self.go(3, low, low, axis_peer(last, 1))
                self.go(3, high, high, axis_peer(last, 3))
                self.pass_on(self.spot(lo, size, order[:2], **{last: before}))
                self.pass_on(self.spot(lo, size, order[:2], **{last: after}))
            elif k == 4:
                self.pass_on(self.spot(lo, size, order[:2], **{last: lax.rem(here + 2, 4)}))
        three = pl.ds(0, 3)
        if k == 0:
            self.kept = pltpu.make_async_copy(self.share, self.spot(0, self.share.shape[0], ""), self.own)
            self.kept.start()
            self.expect(0, ag.at[0, 0, 0, three])
        elif k == 1:
            self.expect(1, ag.at[0, 0, three])
        elif k == 2:
            self.expect(2, ag.at[0, pl.ds(0, 2)])
        elif k == 3:
            self.expect(3, ag.at[0, 0])
        elif k == 4:
            self.expect(4, ag.at[0])
        else:
            self.done()


class RowSwap(Steps):
    def __init__(self, src, dst, send, recv):
        super().__init__(send, recv)
        self.src, self.dst = src, dst

    def run(self, k):
        r, s = lax.axis_index("rows"), lax.axis_index("seq")
        if k == 0:
            for d in range(1, 8):
                peer = lax.rem(r + d, 8)
                self.go(0, self.src.at[peer], self.dst.at[r], (peer, s))
            self.dst[r] = self.src[r]
            self.expect(0, self.dst.at[pl.ds(0, 7)])
        else:
            self.done()


class RowGather(Steps):
    def __init__(self, dst, send, recv):
        super().__init__(send, recv)
        self.dst = dst

    def run(self, k):
        r = lax.axis_index("rows")
        dst = self.dst
        half = dst.shape[1] // 2
        before, after = lax.rem(r + 6, 8), lax.rem(r + 2, 8)
        if k == 0:
            for device in (axis_peer("y", 1), axis_peer("y", 3)):
                self.go(0, dst.at[r], dst.at[r], device)
            self.go(2, dst.at[r], dst.at[r], sibling())
            self.expect(0, dst.at[pl.ds(0, 2)])
        elif k == 1:
            low, high = dst.at[before, pl.ds(0, half)], dst.at[after, pl.ds(half, half)]
            self.go(1, low, low, axis_peer("y", 1))
            self.go(1, high, high, axis_peer("y", 3))
            for spot in (dst.at[before], dst.at[after]):
                self.go(2, spot, spot, sibling())
            self.expect(1, dst.at[0])
        elif k == 2:
            spot = dst.at[lax.rem(r + 4, 8)]
            self.go(2, spot, spot, sibling())
            self.expect(2, dst.at[pl.ds(0, 4)])
        else:
            self.done()


class Exchange:
    def __init__(self, src, dst, send, recv):
        self.src, self.dst, self.send, self.recv = src, dst, send, recv

    def all(self):
        r = lax.axis_index("rows")
        s = lax.axis_index("seq")
        for d in range(1, 16):
            peer = seq_peer(d)
            remote(self.src.at[peer], self.dst.at[s], self.send, self.recv, (r, peer)).start()
        self.dst[s] = self.src[s]
        return self

    def one(self, block):
        r = lax.axis_index("rows")
        s = lax.axis_index("seq")

        @pl.when(s != block)
        def _():
            remote(self.src.at[block], self.dst.at[s], self.send, self.recv, (r, block)).start()

        @pl.when(s == block)
        def _():
            self.dst[s] = self.src[block]

    def wait(self):
        gauge = self.dst.at[pl.ds(0, 15)]
        arrived(gauge, self.recv)
        arrived(gauge, self.send)


class Gather(Steps):
    def __init__(self, hall, send, recv):
        super().__init__(send, recv)
        self.hall = hall

    def run(self, k):
        z, x = axis_place("z"), axis_place("x")
        hall = self.hall
        if k == 0:
            for j in range(1, 4):
                self.go(0, hall.at[0, z, x], hall.at[0, z, x], axis_peer("x", j))
                self.go(0, hall.at[1, z, x], hall.at[1, z, x], axis_peer("z", j))
            self.expect(0, hall.at[:, pl.ds(0, 3), 0])
        elif k == 1:
            for j in (1, 3):
                self.go(1, hall.at[0, z], hall.at[0, z], axis_peer("z", j))
                self.go(1, hall.at[1, :, x], hall.at[1, :, x], axis_peer("x", j))
            self.expect(1, hall.at[0])
        elif k == 2:
            two, low = pl.ds(2, 2), pl.ds(0, 2)
            for spot, axis, j in (
                (hall.at[0, lax.rem(z + 3, 4), low], "z", 1),
                (hall.at[0, lax.rem(z + 1, 4), two], "z", 3),
                (hall.at[1, low, lax.rem(x + 3, 4)], "x", 1),
                (hall.at[1, two, lax.rem(x + 1, 4)], "x", 3),
            ):
                self.go(2, spot, spot, axis_peer(axis, j))
            self.expect(2, hall.at[:, :, 0])
        else:
            self.done()


class Heads(Steps):
    def __init__(self, part, sib_recv, both, y_recv, share, send, recv):
        super().__init__(send, recv)
        self.part, self.sib_recv, self.both, self.y_recv, self.share = part, sib_recv, both, y_recv, share

    def run(self, k):
        y = axis_place("y")
        if k == 0:
            self.go(0, self.part.at[1], self.sib_recv, sibling())
            self.expect(0, self.sib_recv)
        elif k == 1:
            self.both[...] = (self.part[0].astype(f32) + self.sib_recv[...].astype(f32)).astype(bf16)
            for j in range(1, 4):
                there = lax.rem(y + j, 4)
                self.go(1, self.both.at[pl.ds(there * SHARE, SHARE)], self.y_recv.at[j - 1], axis_peer("y", j))
            self.expect(1, self.y_recv)
        else:
            acc = self.both[pl.ds(y * SHARE, SHARE)].astype(f32)
            for j in range(3):
                acc = acc + self.y_recv[j].astype(f32)
            self.share[0:SHARE, :] = acc.astype(bf16)
            self.done()


class Quarters(Steps):
    def __init__(self, part, y_recv, send, recv):
        super().__init__(send, recv)
        self.part, self.y_recv = part, y_recv

    def run(self, k):
        y = axis_place("y")
        if k == 0:
            for j in range(1, 4):
                self.go(0, self.part.at[lax.rem(y + j, 4)], self.y_recv.at[j - 1], axis_peer("y", j))
            self.expect(0, self.y_recv)
        else:
            acc = self.part[y].astype(f32)
            for j in range(3):
                acc = acc + self.y_recv[j].astype(f32)
            self.done()
            return acc.astype(bf16)

    def total(self):
        self.collect()
        return self.run(1)


class Vectors:
    def __init__(self, buf, slots, send_sem, recv_sem):
        self.buf, self.slots, self.send_sem, self.recv_sem = buf, slots, send_sem, recv_sem
        self.at = 0

    def step(self):
        k = self.at
        self.at = k + 1
        if k == 0:
            value = self.buf[0]
        else:
            gauge = self.slots.at[k - 1, pl.ds(0, 3 if k < 4 else 1)]
            arrived(gauge, self.recv_sem.at[k - 1])
            arrived(gauge, self.send_sem.at[k - 1])
            value = self.slots[k - 1, 0]
            for j in range(1, 4 if k < 4 else 2):
                value = value + self.slots[k - 1, j]
        if k == 4:
            self.buf[1] = value
            return
        here = axis_place("xyz"[k]) if k < 3 else lax.rem(lax.axis_index("rows"), 2)
        devices = [axis_peer("xyz"[k], j) for j in range(1, 4)] if k < 3 else [sibling()]
        self.slots[k, here] = value
        for device in devices:
            spot = self.slots.at[k, here]
            remote(spot, spot, self.send_sem.at[k], self.recv_sem.at[k], device).start()


def block_kernel(
    offs_h, x_h, dy_h, ln1g_h, ln1b_h, bq_h, bv_h, bout_h, ln2g_h, ln2b_h, bup_h, bdown_h,
    wqkv_h, wout_h, wup_h, wdown_h,
    out_h, ig_h, ag0, ag1, agh, vecs_h,
    offs, x_ref, dy_ref, ln1g, ln1b, bq, bv, bout, ln2g, ln2b, bup, bdown,
    out_ref, ig_ref, vecs,
    wqkv, wout, wup, wdown, wsem,
    qkt, vals, rqk, rv, kn, vt, ot, lse, atts, ratt,
    hall, n1, rs1, h2ta, dya, actt, acta, gp, gpa, gb, gbs, attts, gres,
    gattt, rda, kt, vn, qn, don, dk, dv, dqkv, rdq,
    asend, arecv, ssend, srecv,
    *rest,
):
    (vbuf, vrecv, vsend, vrsem, lbuf, lrecv, lsend, lrsem, osem,
     hsend, hrecv, hpart, hsib, hboth, hy, hmine, wop, wor) = rest[:18]
    rest = rest[18:]
    sems = [rest[2 * k : 2 * k + 2] for k in range(12)]
    own, rest = rest[24], rest[25:]
    down_parts, down_recv1, down_mid, down_recv2 = [rest[2 * k : 2 * k + 2] for k in range(4)]
    up_parts, up_recv1, up_mid, up_recv2 = [rest[8 + 2 * k : 10 + 2 * k] for k in range(4)]
    out_parts, out_recv1, out_mid, out_recv2 = [rest[16 + 2 * k : 18 + 2 * k] for k in range(4)]
    down_share, up_share = rest[24:]
    loads = {}

    def load(name, src, dst):
        copy = pltpu.make_async_copy(src, dst, wsem.at[len(loads)])
        copy.start()
        loads[name] = copy

    load("x", x_h, x_ref)
    load("ln1g", ln1g_h, ln1g)
    load("ln1b", ln1b_h, ln1b)
    for t in (1, 0, 2):
        cols = pl.ds(t * D, D)
        load(f"qkv{t}", wqkv_h.at[:, cols], wqkv.at[:, cols])
    load("bq", bq_h, bq)
    load("bv", bv_h, bv)
    load("dy", dy_h, dy_ref)
    load("offs", offs_h, offs)
    load("out", wout_h, wout)
    for name, src, dst in (
        ("bout", bout_h, bout), ("ln2g", ln2g_h, ln2g), ("ln2b", ln2b_h, ln2b),
        ("bup", bup_h, bup), ("bdown", bdown_h, bdown),
    ):
        load(name, src, dst)
    load("up", wup_h, wup)
    load("down", wdown_h, wdown)
    stores = []

    def ready(*names):
        for name in names:
            loads[name].wait()

    def store(src, dst):
        copy = pltpu.make_async_copy(src, dst, osem.at[len(stores)])
        copy.start()
        stores.append(copy)

    bar, count = greet()
    vecg = vbuf.at[0]
    vecl = lbuf.at[0]
    early = Vectors(vbuf, vrecv, vsend, vrsem)
    late = Vectors(lbuf, lrecv, lsend, lrsem)
    gather = Gather(hall, hsend, hrecv)
    heads = Heads(hpart, hsib, hboth, hy, hmine, *sems[0])
    dy_rows = RowGather(dya, *sems[1])
    h2_rows = RowGather(h2ta, *sems[2])
    act_rows = RowSwap(actt, acta, *sems[3])
    gp_rows = RowSwap(gp, gpa, *sems[4])
    quarters = Quarters(wop, wor, *sems[5])
    down_sum = Scatter(CUT_DOWN, down_parts, down_recv1, down_mid, down_recv2, down_share, *sems[6])
    up_sum = Scatter(CUT_UP, up_parts, up_recv1, up_mid, up_recv2, up_share, *sems[7])
    down_all = Spread(down_share, ag0, WAYS_DOWN, *sems[8], own.at[0])
    up_all = Spread(up_share, ag1, WAYS_UP, *sems[9], own.at[1])
    head_all = Spread(hmine, agh, WAYS_LAST, *sems[10], own.at[2])
    out_sum = Scatter(CUT_OUT, out_parts, out_recv1, out_mid, out_recv2, hmine.at[pl.ds(SHARE, sum(CUT_OUT))], *sems[11])
    row = lax.axis_index("rows")

    def line(ref):
        return ref[...].astype(f32).reshape(1, D)

    core = lax.rem(lax.axis_index("rows"), 2)
    other = 1 - core
    sib = sibling()
    to_sib = []

    def send_sib(n, src, dst):
        copy = remote(src, dst, ssend.at[n], srecv.at[n], sib)
        copy.start()
        to_sib.append(copy)

    ready("x", "ln1g", "ln1b")
    x = x_ref[...].astype(f32)
    n, rs = norm_parts(x)
    n1[...] = n
    rs1[...] = rs
    h1f = n * line(ln1g) + line(ln1b)
    h1 = h1f.astype(bf16)
    for half in range(2):
        hall[half, axis_place("z"), axis_place("x")] = h1[:, half * 384 : (half + 1) * 384]
    for t in (1, 0, 2):
        ready(f"qkv{t}")
        y = dot(h1, wqkv[:, t * D : (t + 1) * D])
        if t == 0:
            ready("bq")
            y = y + line(bq)
        if t == 2:
            ready("bv")
            y = y + line(bv)
        low = jnp.transpose(y).astype(bf16).reshape(H, HS, TOK)
        if t < 2:
            qkt[:, t * HS : (t + 1) * HS, :] = low
        else:
            vals[...] = low
        if t == 0:
            pl.semaphore_wait(bar, count)
            moved = [Exchange(qkt, rqk, asend.at[0], arecv.at[0]).all()]
    moved.append(Exchange(vals, rv, asend.at[1], arecv.at[1]).all())
    ready("dy", "offs")
    dya[row] = dy_ref[...]
    dy_rows.step()
    for copy in moved:
        copy.wait()
    gather.step()

    attended = Exchange(atts, ratt, asend.at[2], arecv.at[2])
    attend_forward(
        offs, rqk, rv, kn, vt, ot, lse, atts,
        attended.one,
    )
    ready("out", "bout", "ln2g", "ln2b", "bup", "bdown", "up", "down")
    gather.step()
    attended.wait()
    dy_rows.step()

    att = jnp.transpose(ratt[...].reshape(D, TOK).astype(f32)).astype(bf16)
    send_sib(0, ratt.at[pl.ds(other * 8, 8)], attts)
    resid = x_ref[...].astype(f32) + dot(att, wout[...]) + line(bout)
    n2, rs2 = norm_parts(resid)
    h2f = n2 * line(ln2g) + line(ln2b)
    h2 = h2f.astype(bf16)
    h2ta[row] = jnp.transpose(h2f).astype(bf16)
    h2_rows.step()
    dy = dy_ref[...]
    down = None
    dh2 = None
    for c in range(4):
        cols = slice(c * D, (c + 1) * D)
        pre = dot(h2, wup[:, cols]) + bup[cols].astype(f32).reshape(1, D)
        square = pre * pre
        t = jnp.tanh(GELU_C * (pre + GELU_A * (square * pre)))
        act = 0.5 * pre * (1.0 + t)
        slope = 0.5 * (1.0 + t) + (0.5 * GELU_C) * pre * (1.0 - t * t) * (1.0 + (3.0 * GELU_A) * square)
        part = dot(act.astype(bf16), wdown[cols, :])
        down = part if down is None else down + part
        act_t = jnp.transpose(act).astype(bf16)
        actt[2 * c] = act_t[0:384]
        actt[2 * c + 1] = act_t[384:768]
        gpre = (dot_nt(dy, wdown[cols, :]) * slope).astype(bf16)
        gp[2 * c] = gpre[:, 0:384]
        gp[2 * c + 1] = gpre[:, 384:768]
        vecg[BUP + c : BUP + c + 1, :] = over_tokens(gpre.astype(f32))
        part = dot_nt(gpre, wup[:, cols])
        dh2 = part if dh2 is None else dh2 + part
    act_rows.step()
    gp_rows.step()
    out_ref[...] = (resid + down + line(bdown)).astype(bf16)
    store(out_ref, out_h)
    vecg[BDOWN : BDOWN + 1, :] = over_tokens(dy.astype(f32))
    vecg[LN2G : LN2G + 1, :] = over_tokens(dh2 * n2)
    vecg[LN2B : LN2B + 1, :] = over_tokens(dh2)
    grad = dy.astype(f32) + norm_back(dh2, n2, rs2, line(ln2g))
    gres[...] = grad
    branch = grad.astype(bf16)
    gb[...] = branch
    vecg[BOUT : BOUT + 1, :] = over_tokens(branch.astype(f32))
    gattt[...] = jnp.transpose(dot_nt(branch, wout[...])).astype(bf16).reshape(H, HS, TOK)
    moved = Exchange(gattt, rda, asend.at[3], arecv.at[3]).all()
    h2_rows.step()
    send_sib(1, gb, gbs)

    gather.step()
    moved.wait()

    def part_out():
        for copy in to_sib:
            copy.wait()
        left = jnp.concatenate(
            [ratt[pl.ds(core * 8, 8)].reshape(384, TOK), attts[...].reshape(384, TOK)], axis=1
        )
        right = jnp.concatenate([gb[...], gbs[...]], axis=0)
        res = dot(left, right).astype(bf16)
        for k in range(4):
            for t in range(6):
                wop[k, t * 96 : (t + 1) * 96, :] = res[k * 96 : (k + 1) * 96, t * TOK : (t + 1) * TOK]
        quarters.step()

    def grads_down():
        dy_rows.step()
        act_rows.step()
        left = jnp.concatenate([acta[k] for k in range(8)], axis=1)
        res = dot(left, dya[...].reshape(8 * TOK, D)).astype(bf16)
        for t in range(6):
            down_sum.put(res[:, t * TOK : (t + 1) * TOK], t * 384)
        down_sum.step()

    def grads_up():
        h2_rows.step()
        gp_rows.step()
        left = jnp.concatenate([h2ta[k] for k in range(8)], axis=1)
        res = dot(left, gpa[...].reshape(8 * TOK, 384)).astype(bf16)
        for t in range(3):
            up_sum.put(res[:, t * TOK : (t + 1) * TOK], t * D)
        up_sum.step()

    def grads_out():
        out_sum.put(quarters.total(), 0)
        out_sum.put(jnp.zeros((192, TOK), bf16), 576)
        out_sum.step()

    back = Exchange(dqkv, rdq, asend.at[4], arecv.at[4])

    def between(i):
        for half in (0, 1):
            back.one(2 * i + half)
        if i == 7:
            dy_rows.step()
            early.step()
        elif i == 6:
            part_out()
        elif i == 4:
            grads_down()
        elif i == 1:
            down_sum.step()

    attend_backward(offs, rqk, rv, kn, kt, vn, qn, don, rda, ot, lse, dqkv, dk, dv, between)
    h2_rows.step()
    grads_up()
    back.wait()

    dh1t = None
    ones = jnp.ones((8, TOK), bf16)
    for t in range(3):
        grad_t = rdq[:, t * HS : (t + 1) * HS, :].reshape(D, TOK)
        part = dot(wqkv[:, t * D : (t + 1) * D], grad_t)
        dh1t = part if dh1t is None else dh1t + part
        if t != 1:
            row = BQ if t == 0 else BV
            vecl[row : row + 1, :] = dot_nt(ones, grad_t)[0:1, :]
    dh1 = jnp.transpose(dh1t)
    n = n1[...]
    vecl[LN1G : LN1G + 1, :] = over_tokens(dh1 * n)
    vecl[LN1B : LN1B + 1, :] = over_tokens(dh1)
    vecl[4:8, :] = jnp.zeros((4, D), f32)
    gather.step()
    spread = jnp.concatenate([dqkv[k] for k in range(NB)], axis=1)

    def part_head(slot, half):
        res = dot(spread, hall[half].reshape(SEQ, 384)).astype(bf16)
        for u in range(3):
            hpart[slot, u * 144 : (u + 1) * 144, :] = res[:, u * TOK : (u + 1) * TOK]
        hpart[slot, 432:HEAD_ROWS, :] = jnp.zeros((HEAD_ROWS - 432, TOK), bf16)

    part_head(1, other)
    heads.step()
    down_sum.step()
    down_all.step()
    part_head(0, core)
    early.step()
    late.step()
    grads_out()
    heads.step()
    up_sum.step()
    down_all.step()
    late.step()
    ig_ref[...] = (gres[...] + norm_back(dh1, n, rs1[...], line(ln1g))).astype(bf16)
    store(ig_ref, ig_h)
    out_sum.step()
    heads.step()
    early.step()
    up_sum.step()
    up_all.step()
    down_all.step()
    late.step()
    out_sum.step()
    head_all.step()
    up_all.step()
    early.step()
    down_all.step()
    late.step()
    head_all.step()
    late.step()
    early.step()
    vecs[0] = vbuf[1]
    vecs[1] = lbuf[1]
    store(vecs, vecs_h)
    up_all.step()
    head_all.step()
    up_all.step()
    head_all.step()
    down_all.step()
    up_all.step()
    head_all.step()
    for item in (down_all, up_all, head_all):
        item.step()
    for item in (down_sum, up_sum, out_sum):
        item.done()
    for copy in stores:
        copy.wait()


VMEM = pl.BlockSpec(memory_space=pltpu.VMEM)
SMEM = pl.BlockSpec(memory_space=pltpu.SMEM)
ANY = pl.BlockSpec(memory_space=pl.ANY)


def call_block(offsets, x, dy, vectors, weights):
    v = pltpu.VMEM
    dma = pltpu.SemaphoreType.DMA
    shape = jax.ShapeDtypeStruct
    return pl.pallas_call(
        block_kernel,
        out_shape=(
            shape((TOK, D), bf16),
            shape((TOK, D), bf16),
            shape((2, 4, 4, 4, sum(CUT_DOWN), TOK), bf16),
            shape((2, 4, 4, 4, sum(CUT_UP), TOK), bf16),
            shape((2, 4, 4, 4, ROWS_LAST, TOK), bf16),
            shape((2, VROWS, D), f32),
        ),
        in_specs=[ANY] * 16,
        out_specs=(ANY,) * 6,
        scratch_shapes=[
            pltpu.SMEM((1, 8), jnp.int32), v((TOK, D), bf16), v((TOK, D), bf16),
            *[v((FF if k == 7 else D,), bf16) for k in range(9)],
            v((TOK, D), bf16), v((TOK, D), bf16), v((2, VROWS, D), f32),
            v((D, 3 * D), bf16), v((D, D), bf16), v((D, FF), bf16), v((FF, D), bf16), dma((20,)),
            v((NB, 96, TOK), bf16), v((NB, HS, TOK), bf16), v((NB, 96, TOK), bf16), v((NB, HS, TOK), bf16),
            v((SEQ, HS), bf16), v((HS, SEQ), bf16),
            v((HS, SEQ), f32), v((1, SEQ), f32), v((NB, HS, TOK), bf16), v((NB, HS, TOK), bf16),
            v((2, 4, 4, TOK, 384), bf16), v((TOK, D), f32), v((TOK, 1), f32),
            v((8, D, TOK), bf16), v((8, TOK, D), bf16),
            v((8, 384, TOK), bf16), v((8, 384, TOK), bf16), v((8, TOK, 384), bf16), v((8, TOK, 384), bf16),
            v((TOK, D), bf16), v((TOK, D), bf16), v((8, HS, TOK), bf16), v((TOK, D), f32),
            v((NB, HS, TOK), bf16), v((NB, HS, TOK), bf16),
            v((HS, SEQ), bf16), v((SEQ, HS), bf16), v((SEQ, HS), bf16), v((SEQ, HS), bf16),
            v((SEQ, HS), f32), v((SEQ, HS), f32),
            v((NB, 144, TOK), bf16), v((NB, 144, TOK), bf16),
            dma((5,)), dma((5,)), dma((2,)), dma((2,)),
            v((2, VROWS, D), f32), v((4, 4, VROWS, D), f32), dma((4,)), dma((4,)),
            v((2, VROWS, D), f32), v((4, 4, VROWS, D), f32), dma((4,)), dma((4,)), dma((3,)),
            dma((3,)), dma((3,)), v((2, HEAD_ROWS, TOK), bf16), v((HEAD_ROWS, TOK), bf16),
            v((HEAD_ROWS, TOK), bf16), v((3, SHARE, TOK), bf16), v((ROWS_LAST, TOK), bf16),
            v((4, 576, TOK), bf16), v((3, 576, TOK), bf16),
            *[dma((n,)) for n in (2, 3, 3, 1, 1, 1, 4, 4, 5, 5, 5, 4) for _ in range(2)], dma((3,)),
            *[
                v(lead + (cut, TOK), bf16)
                for cuts in (CUT_DOWN, CUT_UP, CUT_OUT)
                for lead in ((4, 4), (3, 4), (4,), (3,))
                for cut in cuts
            ],
            v((sum(CUT_DOWN), TOK), bf16), v((sum(CUT_UP), TOK), bf16),
        ],
        compiler_params=pltpu.CompilerParams(
            collective_id=1, has_side_effects=True, vmem_limit_bytes=58 * 2**20
        ),
    )(offsets, x, dy, *vectors, *weights)


def widen_kernel(ag0, ag1, agh, vecs_h, done_h, ig_h, wqkv, wout, wup, wdown, out_h, grad_h, *rest):
    small_h, small = rest[:9], rest[9:18]
    vecs, vsem, ssem, down_in, up_in, out_in, down_out, up_out, out_out, headb, wideb, isem, osem = (
        rest[18], rest[19], rest[20], rest[21:23], rest[23:25], rest[25:27], *rest[27:]
    )
    passed = [
        pltpu.make_async_copy(done_h, out_h, vsem.at[0]),
        pltpu.make_async_copy(ig_h, grad_h, vsem.at[1]),
    ]
    fetch = pltpu.make_async_copy(vecs_h, vecs, vsem.at[2])

    def share_loads(kind, k):
        ag, cuts, bufs, lo = ((ag0, CUT_DOWN, down_in, 0), (ag1, CUT_UP, up_in, 0), (agh, CUT_OUT, out_in, SHARE))[kind]
        copies = []
        for n in range(2):
            src = ag.at[k % 2, :, :, k // 2, pl.ds(lo, cuts[n])]
            copies.append(pltpu.make_async_copy(src, bufs[n].at[k], isem.at[kind, k, n]))
            lo += cuts[n]
        return copies

    def pieces(cuts, offset, rows):
        at = 0
        while at < rows:
            n = 0 if offset < 16 * cuts[0] else 1
            inside = offset - n * 16 * cuts[0]
            block, lo = inside // cuts[n], inside % cuts[n]
            size = min(cuts[n] - lo, rows - at)
            yield at, size, n, block, lo
            at += size
            offset += size

    def widen(bufs, cuts, k, offset, rows, dst, col):
        for at, size, n, block, lo in pieces(cuts, offset, rows):
            part = bufs[n][k, block // 4, block % 4, lo : lo + size, :]
            dst[at : at + size, col * TOK : (col + 1) * TOK] = part.astype(f32)

    down_store = [
        pltpu.make_async_copy(down_out.at[k % 3], wdown.at[pl.ds(k * 384, 384)], osem.at[0, k % 3]) for k in range(8)
    ]
    up_store = [
        pltpu.make_async_copy(up_out.at[k % 3], wup.at[:, pl.ds(k * 384, 384)], osem.at[1, k % 3]) for k in range(8)
    ]
    out_store = [
        pltpu.make_async_copy(
            out_out.at[k % 3], wout.at[pl.ds((k % 2) * 384 + (k // 2) * 96, 96)], osem.at[2, k % 3]
        )
        for k in range(8)
    ]

    cuts_head = (((0, 0, 112, 0), (1, 0, 32, 112)), ((1, 32, 80, 0), (2, 0, 64, 80)), ((2, 64, 48, 0), (3, 0, 96, 48)))

    def head_loads(k):
        return [
            pltpu.make_async_copy(
                agh.at[k // 3, :, :, y, pl.ds(lo, size)], headb.at[k, :, :, pl.ds(to, size)], isem.at[3, k, n]
            )
            for n, (y, lo, size, to) in enumerate(cuts_head[k % 3])
        ]

    head_store = [
        pltpu.make_async_copy(wideb.at[k % 3], wqkv.at[pl.ds(k * TOK, TOK)], osem.at[3, k % 3]) for k in range(6)
    ]

    fetch.start()
    for k in range(8):
        for copy in share_loads(0, k) + share_loads(1, k) + share_loads(2, k) + (head_loads(k) if k < 6 else []):
            copy.start()
    for copy in passed:
        copy.start()
    for k in range(8):
        for copy in share_loads(0, k):
            copy.wait()
        if k >= 3:
            down_store[k - 3].wait()
        for t in range(6):
            widen(down_in, CUT_DOWN, k, t * 384, 384, down_out.at[k % 3], t)
        down_store[k].start()
        for copy in share_loads(1, k):
            copy.wait()
        if k >= 3:
            up_store[k - 3].wait()
            out_store[k - 3].wait()
        for t in range(3):
            widen(up_in, CUT_UP, k, t * D, D, up_out.at[k % 3], t)
        up_store[k].start()
        for copy in share_loads(2, k):
            copy.wait()
        for t in range(6):
            widen(out_in, CUT_OUT, k, t * 96, 96, out_out.at[k % 3], t)
        out_store[k].start()
        if k < 6:
            for copy in head_loads(k):
                copy.wait()
            if k >= 3:
                head_store[k - 3].wait()
            for t in range(3):
                block = headb[k, :, :, t * HS : (t + 1) * HS, :].reshape(D, TOK)
                wideb[k % 3, :, t * D : (t + 1) * D] = jnp.transpose(block.astype(f32))
            head_store[k].start()
        if k == 0:
            fetch.wait()
            places = ((1, LN1G), (1, LN1B), (1, BQ), (1, BV), (0, BOUT), (0, LN2G), (0, LN2B), (0, BUP), (0, BDOWN))
            for n, (ref, (group, line)) in enumerate(zip(small, places)):
                if line == BUP:
                    for c in range(4):
                        ref[c * D : (c + 1) * D] = vecs[0, BUP + c : BUP + c + 1, :].reshape(D)
                else:
                    ref[...] = vecs[group, line : line + 1, :].reshape(D)
                copy = pltpu.make_async_copy(ref, small_h[n], ssem.at[n])
                copy.start()
                passed.append(copy)
    for k in range(5, 8):
        down_store[k].wait()
        up_store[k].wait()
        out_store[k].wait()
        head_store[k - 2].wait()
    for copy in passed:
        copy.wait()


def call_widen(*arrays):
    v = pltpu.VMEM
    dma = pltpu.SemaphoreType.DMA
    shape = jax.ShapeDtypeStruct
    return pl.pallas_call(
        widen_kernel,
        out_shape=(
            shape((D, 3 * D), f32), shape((D, D), f32), shape((D, FF), f32), shape((FF, D), f32),
            shape((TOK, D), bf16), shape((TOK, D), bf16),
        ) + tuple(shape((FF if k == 7 else D,), f32) for k in range(9)),
        in_specs=[ANY] * 6,
        out_specs=(ANY,) * 15,
        scratch_shapes=[
            *[v((FF if k == 7 else D,), f32) for k in range(9)], v((2, VROWS, D), f32), dma((3,)), dma((9,)),
            *[v((8, 4, 4, cut, TOK), bf16) for cut in CUT_DOWN + CUT_UP + CUT_OUT],
            v((3, 384, D), f32), v((3, D, 384), f32), v((3, 96, D), f32),
            v((6, 4, 4, 144, TOK), bf16), v((3, TOK, 3 * D), f32), dma((4, 8, 2)), dma((4, 3)),
        ],
        compiler_params=pltpu.CompilerParams(vmem_limit_bytes=58 * 2**20),
    )(*arrays)


def local(
    block_input, offsets, ln1_gain, ln1_bias, w_qkv, bias_query, bias_value, w_out, bias_out,
    ln2_gain, ln2_bias, w_up, bias_up, w_down, bias_down, cotangent,
):
    out, ig, ag0, ag1, agh, vecs = call_block(
        offsets, block_input.reshape(TOK, D), cotangent.reshape(TOK, D),
        (ln1_gain, ln1_bias, bias_query, bias_value, bias_out, ln2_gain, ln2_bias, bias_up, bias_down),
        (w_qkv, w_out, w_up, w_down),
    )
    wide = call_widen(ag0, ag1, agh, vecs, out, ig)
    g_qkv, g_out, g_up, g_down, out, ig = wide[:6]
    s = wide[6:]
    return (
        out.reshape(1, TOK, D), ig.reshape(1, TOK, D),
        s[0], s[1], g_qkv, s[2], s[3], g_out, s[4], s[5], s[6], g_up, s[7], g_down, s[8],
    )


def solution(mesh):
    tokens = P("rows", "seq", None)
    return jax.shard_map(
        local,
        mesh=mesh,
        in_specs=(tokens, P("rows", None)) + (P(),) * 13 + (tokens,),
        out_specs=(tokens, tokens) + (P(),) * 13,
        check_vma=False,
    )
```

```python
import functools

import jax
import jax.numpy as jnp
from jax import lax
from jax.experimental import pallas as pl
from jax.experimental.pallas import tpu as pltpu
from jax.sharding import PartitionSpec as P

MESH = pl.DeviceIdType.MESH
f32 = jnp.float32
bf16 = jnp.bfloat16

D = 768
H = 16
FF = 3072
HS = 48
SEQ = 2048
TOK = 128
NB = 16
QB = 256
CUT_DOWN = (80, 64)
CUT_UP = (80, 64)
CUT_OUT = (32, 16)
SHARE = 112
HEAD_ROWS = 4 * SHARE
ROWS_LAST = SHARE + sum(CUT_OUT)
WAYS_DOWN = ((0, 48, "xzy"), (48, 48, "zyx"), (96, 48, "yxz"))
WAYS_UP = WAYS_DOWN
WAYS_LAST = ((0, 64, "xzy"), (64, 48, "zyx"), (112, 48, "yxz"))
SCALE = HS**-0.5
SCALE_LOG2E = SCALE * 1.4426950408889634
NEGATIVE = -1e30
EPSILON = 1e-05
GELU_C = 0.7978845608028654
GELU_A = 0.044715

LN1G, LN1B, BQ, BV = 0, 1, 2, 3
BOUT, LN2G, LN2B, BDOWN, BUP = 0, 1, 2, 3, 4
VROWS = 8
WIDEN_SLOTS = 6


def dot(a, b):
    return jnp.dot(a, b, preferred_element_type=f32)


def dot_nt(a, b):
    return lax.dot_general(a, b, (((1,), (1,)), ((), ())), preferred_element_type=f32)


def turned(block):
    return jnp.transpose(block.astype(f32)).astype(bf16)


def coords():
    r = lax.axis_index("rows")
    s = lax.axis_index("seq")
    return lax.div(r, 2), lax.rem(r, 2), lax.div(s, 4), lax.rem(s, 4)


def device_at(y, c, z, x):
    return (y * 2 + c, z * 4 + x)


def remote(src, dst, send, recv, device):
    return pltpu.make_async_remote_copy(
        src_ref=src, dst_ref=dst, send_sem=send, recv_sem=recv, device_id=device, device_id_type=MESH
    )


def seq_peer(d):
    s = lax.axis_index("seq")
    return lax.rem(s + d, 16)


def axis_peer(axis, j):
    y, c, z, x = coords()
    if axis == "y":
        y = lax.rem(y + j, 4)
    elif axis == "z":
        z = lax.rem(z + j, 4)
    else:
        x = lax.rem(x + j, 4)
    return device_at(y, c, z, x)


def axis_place(axis):
    y, c, z, x = coords()
    return {"y": y, "z": z, "x": x}[axis]


def sibling():
    y, c, z, x = coords()
    return device_at(y, 1 - c, z, x)


def greet():
    bar = pltpu.get_barrier_semaphore()
    r = lax.axis_index("rows")
    s = lax.axis_index("seq")
    devices = [(r, seq_peer(d)) for d in range(1, 16)] + [(lax.rem(r + d, 8), s) for d in range(1, 8)]
    for device in devices:
        pl.semaphore_signal(bar, inc=1, device_id=device, device_id_type=MESH)
    return bar, len(devices)


def masked(scores, start, key0, query0, diagonal):
    key = lax.broadcasted_iota(jnp.int32, scores.shape, 0) + key0
    ok = key >= start
    if diagonal:
        query = lax.broadcasted_iota(jnp.int32, scores.shape, 1) + query0
        ok = ok & (key <= query)
    return jnp.where(ok, scores, NEGATIVE)


def segment_starts(offs_ref, query0, count):
    place = lax.broadcasted_iota(jnp.int32, (1, count), 1) + query0
    start = jnp.zeros((1, count), jnp.int32)
    for j in range(8):
        o = offs_ref[0, j]
        start = jnp.where(place >= o, o, start)
    return start


def pair(ref, i, lo, hi):
    return jnp.concatenate([ref[2 * i, lo:hi, :], ref[2 * i + 1, lo:hi, :]], axis=1)


def attend_forward(offs_ref, qk, vals, kn, vt, ot, lse, atts, after):
    for s in range(NB):
        kn[s * TOK : (s + 1) * TOK, :] = turned(qk[s, 48:96, :])
        vt[:, s * TOK : (s + 1) * TOK] = vals[s]
    for i in range(SEQ // QB):
        q0 = i * QB
        qt = pair(qk, i, 0, 48)
        start = segment_starts(offs_ref, q0, QB)
        sd = masked(dot(kn[q0 : q0 + QB, :], qt) * SCALE_LOG2E, start, q0, q0, True)
        top = jnp.max(sd, axis=0, keepdims=True)
        if i:
            so = masked(dot(kn[0:q0, :], qt) * SCALE_LOG2E, start, 0, q0, False)
            top = jnp.maximum(top, jnp.max(so, axis=0, keepdims=True))
        pd = jnp.exp2(sd - top)
        total = jnp.sum(pd, axis=0, keepdims=True)
        out = dot(vt[:, q0 : q0 + QB], pd.astype(bf16))
        if i:
            po = jnp.exp2(so - top)
            total = total + jnp.sum(po, axis=0, keepdims=True)
            out = out + dot(vt[:, 0:q0], po.astype(bf16))
        out = out / total
        ot[:, q0 : q0 + QB] = out
        lse[:, q0 : q0 + QB] = top + jnp.log2(total)
        low = out.astype(bf16)
        atts[2 * i] = low[:, 0:TOK]
        atts[2 * i + 1] = low[:, TOK:QB]
        after(2 * i)
        after(2 * i + 1)


def attend_backward(offs_ref, qk, vals, kn, kt, vn, qn, don, dor, ot, lse, dqkv, dk, dv, after):
    for s in range(NB):
        rows = slice(s * TOK, (s + 1) * TOK)
        vn[rows, :] = turned(vals[s])
        qn[rows, :] = turned(qk[s, 0:48, :])
        don[rows, :] = turned(dor[s])
        kt[:, rows] = qk[s, 48:96, :]
    last = SEQ // QB - 1
    for i in reversed(range(SEQ // QB)):
        q0 = i * QB
        qt = pair(qk, i, 0, 48)
        dot_t = pair(dor, i, 0, 48)
        start = segment_starts(offs_ref, q0, QB)
        level = lse[:, q0 : q0 + QB]
        inner = jnp.sum(dot_t.astype(f32) * ot[:, q0 : q0 + QB], axis=0, keepdims=True)
        q_n = qn[q0 : q0 + QB, :]
        do_n = don[q0 : q0 + QB, :]
        dq = None
        for a, b, diagonal in ([(0, q0, False)] if i else []) + [(q0, q0 + QB, True)]:
            scores = masked(dot(kn[a:b, :], qt) * SCALE_LOG2E, start, a, q0, diagonal)
            probs = jnp.exp2(scores - level)
            dp = dot(vn[a:b, :], dot_t)
            ds = (probs * (dp - inner)).astype(bf16)
            dv_part = dot(probs.astype(bf16), do_n)
            dk_part = dot(ds, q_n)
            if i == last:
                dk[a:b, :] = dk_part
                dv[a:b, :] = dv_part
            else:
                dk[a:b, :] += dk_part
                dv[a:b, :] += dv_part
            dq_part = dot(kt[:, a:b], ds)
            dq = dq_part if dq is None else dq + dq_part
        dq = (dq * SCALE).astype(bf16)
        for h in range(2):
            s = 2 * i + h
            rows = slice(s * TOK, (s + 1) * TOK)
            dqkv[s, 0:48, :] = dq[:, h * TOK : (h + 1) * TOK]
            dqkv[s, 48:96, :] = (jnp.transpose(dk[rows, :]) * SCALE).astype(bf16)
            dqkv[s, 96:144, :] = jnp.transpose(dv[rows, :]).astype(bf16)
        after(i)


def norm_parts(values):
    center = values - jnp.mean(values, axis=-1, keepdims=True)
    spread = jnp.mean(center * center, axis=-1, keepdims=True)
    rs = lax.rsqrt(spread + EPSILON)
    return center * rs, rs


def norm_back(grad, n, rs, gain):
    gg = grad * gain
    return rs * (
        gg - jnp.mean(gg, axis=-1, keepdims=True) - n * jnp.mean(gg * n, axis=-1, keepdims=True)
    )


def over_tokens(values):
    return jnp.sum(values, axis=0, keepdims=True)


def arrived(gauge, sem):
    pltpu.make_async_copy(gauge, gauge, sem).wait()


class Steps:
    def __init__(self, send, recv):
        self.send, self.recv = send, recv
        self.sent = []
        self.live = []
        self.at = 0

    def go(self, group, src, dst, device):
        remote(src, dst, self.send.at[group], self.recv.at[group], device).start()

    def expect(self, group, gauge):
        self.live.append((group, gauge))
        self.sent.append((group, gauge))

    def collect(self):
        for group, gauge in self.live:
            arrived(gauge, self.recv.at[group])
        self.live = []

    def step(self):
        self.collect()
        k = self.at
        self.at = k + 1
        self.run(k)

    def done(self):
        for group, gauge in self.sent:
            arrived(gauge, self.send.at[group])
        self.sent = []


class Scatter(Steps):
    def __init__(self, cuts, parts, recv1, mid, recv2, share, send, recv):
        super().__init__(send, recv)
        self.cuts, self.parts, self.recv1, self.mid, self.recv2, self.share = cuts, parts, recv1, mid, recv2, share

    def put(self, value, offset):
        at, rows = 0, value.shape[0]
        while at < rows:
            k = 0 if offset < 16 * self.cuts[0] else 1
            inside = offset - k * 16 * self.cuts[0]
            block, lo = inside // self.cuts[k], inside % self.cuts[k]
            size = min(self.cuts[k] - lo, rows - at)
            self.parts[k][block // 4, block % 4, lo : lo + size, :] = value[at : at + size]
            at += size
            offset += size

    def run(self, k):
        z, x = axis_place("z"), axis_place("x")
        first, second = self.parts
        if k == 0:
            for j in range(1, 4):
                self.go(0, first.at[:, lax.rem(x + j, 4)], self.recv1[0].at[j - 1], axis_peer("x", j))
                self.go(1, second.at[lax.rem(z + j, 4)], self.recv1[1].at[j - 1], axis_peer("z", j))
            for n in range(2):
                self.expect(n, self.recv1[n])
        elif k == 1:
            for n, mine in enumerate((first[:, x], second[z])):
                acc = mine.astype(f32)
                for j in range(3):
                    acc = acc + self.recv1[n][j].astype(f32)
                self.mid[n][...] = acc.astype(bf16)
            for j in range(1, 4):
                self.go(2, self.mid[0].at[lax.rem(z + j, 4)], self.recv2[0].at[j - 1], axis_peer("z", j))
                self.go(3, self.mid[1].at[lax.rem(x + j, 4)], self.recv2[1].at[j - 1], axis_peer("x", j))
            for n in range(2):
                self.expect(2 + n, self.recv2[n])
        else:
            lo = 0
            for n, here in enumerate((z, x)):
                acc = self.mid[n][here].astype(f32)
                for j in range(3):
                    acc = acc + self.recv2[n][j].astype(f32)
                self.share[lo : lo + self.cuts[n], :] = acc.astype(bf16)
                lo += self.cuts[n]


class Spread(Steps):
    def __init__(self, share, ag, ways, send, recv, own):
        super().__init__(send, recv)
        self.share, self.ag, self.ways, self.own = share, ag, ways, own

    def spot(self, lo, size, whole, **at):
        core = lax.rem(lax.axis_index("rows"), 2)
        index = [at[a] if a in at else slice(None) if a in whole else axis_place(a) for a in "zxy"]
        return self.ag.at[(core, *index, pl.ds(lo, size))]

    def pass_on(self, spot):
        self.go(4, spot, spot, sibling())

    def run(self, k):
        ag = self.ag
        if k == 1:
            self.kept.wait()
        for lo, size, order in self.ways:
            last = order[2]
            here = axis_place(last)
            if k == 0:
                for j in range(1, 4):
                    self.go(0, self.share.at[pl.ds(lo, size)], self.spot(lo, size, ""), axis_peer(order[0], j))
            elif k == 1:
                spot = self.spot(lo, size, order[0])
                for j in range(1, 4):
                    self.go(1, spot, spot, axis_peer(order[1], j))
            elif k == 2:
                spot = self.spot(lo, size, order[:2])
                self.go(2, spot, spot, axis_peer(last, 1))
                self.go(2, spot, spot, axis_peer(last, 3))
                self.pass_on(spot)
            elif k == 3:
                before, after = lax.rem(here + 3, 4), lax.rem(here + 1, 4)
                cut = "x" if last == "z" else "z"
                low = self.spot(lo, size, order[:2], **{last: before, cut: pl.ds(0, 2)})
                high = self.spot(lo, size, order[:2], **{last: after, cut: pl.ds(2, 2)})
                self.go(3, low, low, axis_peer(last, 1))
                self.go(3, high, high, axis_peer(last, 3))
                self.pass_on(self.spot(lo, size, order[:2], **{last: before}))
                self.pass_on(self.spot(lo, size, order[:2], **{last: after}))
            elif k == 4:
                self.pass_on(self.spot(lo, size, order[:2], **{last: lax.rem(here + 2, 4)}))
        three = pl.ds(0, 3)
        if k == 0:
            self.kept = pltpu.make_async_copy(self.share, self.spot(0, self.share.shape[0], ""), self.own)
            self.kept.start()
            self.expect(0, ag.at[0, 0, 0, three])
        elif k == 1:
            self.expect(1, ag.at[0, 0, three])
        elif k == 2:
            self.expect(2, ag.at[0, pl.ds(0, 2)])
        elif k == 3:
            self.expect(3, ag.at[0, 0])
        elif k == 4:
            self.expect(4, ag.at[0])
        else:
            self.done()


class RowSwap(Steps):
    def __init__(self, src, dst, send, recv):
        super().__init__(send, recv)
        self.src, self.dst = src, dst

    def run(self, k):
        r, s = lax.axis_index("rows"), lax.axis_index("seq")
        if k == 0:
            for d in range(1, 8):
                peer = lax.rem(r + d, 8)
                self.go(0, self.src.at[peer], self.dst.at[r], (peer, s))
            self.dst[r] = self.src[r]
            self.expect(0, self.dst.at[pl.ds(0, 7)])
        else:
            self.done()


class RowGather(Steps):
    def __init__(self, dst, send, recv):
        super().__init__(send, recv)
        self.dst = dst

    def run(self, k):
        r = lax.axis_index("rows")
        dst = self.dst
        half = dst.shape[1] // 2
        before, after = lax.rem(r + 6, 8), lax.rem(r + 2, 8)
        if k == 0:
            for device in (axis_peer("y", 1), axis_peer("y", 3)):
                self.go(0, dst.at[r], dst.at[r], device)
            self.go(2, dst.at[r], dst.at[r], sibling())
            self.expect(0, dst.at[pl.ds(0, 2)])
        elif k == 1:
            low, high = dst.at[before, pl.ds(0, half)], dst.at[after, pl.ds(half, half)]
            self.go(1, low, low, axis_peer("y", 1))
            self.go(1, high, high, axis_peer("y", 3))
            for spot in (dst.at[before], dst.at[after]):
                self.go(2, spot, spot, sibling())
            self.expect(1, dst.at[0])
        elif k == 2:
            spot = dst.at[lax.rem(r + 4, 8)]
            self.go(2, spot, spot, sibling())
            self.expect(2, dst.at[pl.ds(0, 4)])
        else:
            self.done()


class Exchange:
    def __init__(self, src, dst, send, recv):
        self.src, self.dst, self.send, self.recv = src, dst, send, recv

    def all(self):
        r = lax.axis_index("rows")
        s = lax.axis_index("seq")
        for d in range(1, 16):
            peer = seq_peer(d)
            remote(self.src.at[peer], self.dst.at[s], self.send, self.recv, (r, peer)).start()
        self.dst[s] = self.src[s]
        return self

    def one(self, block):
        r = lax.axis_index("rows")
        s = lax.axis_index("seq")

        @pl.when(s != block)
        def _():
            remote(self.src.at[block], self.dst.at[s], self.send, self.recv, (r, block)).start()

        @pl.when(s == block)
        def _():
            self.dst[s] = self.src[block]

    def wait(self):
        gauge = self.dst.at[pl.ds(0, 15)]
        arrived(gauge, self.recv)
        arrived(gauge, self.send)


class Gather(Steps):
    def __init__(self, hall, send, recv):
        super().__init__(send, recv)
        self.hall = hall

    def run(self, k):
        z, x = axis_place("z"), axis_place("x")
        hall = self.hall
        if k == 0:
            for j in range(1, 4):
                self.go(0, hall.at[0, z, x], hall.at[0, z, x], axis_peer("x", j))
                self.go(0, hall.at[1, z, x], hall.at[1, z, x], axis_peer("z", j))
            self.expect(0, hall.at[:, pl.ds(0, 3), 0])
        elif k == 1:
            for j in (1, 3):
                self.go(1, hall.at[0, z], hall.at[0, z], axis_peer("z", j))
                self.go(1, hall.at[1, :, x], hall.at[1, :, x], axis_peer("x", j))
            self.expect(1, hall.at[0])
        elif k == 2:
            two, low = pl.ds(2, 2), pl.ds(0, 2)
            for spot, axis, j in (
                (hall.at[0, lax.rem(z + 3, 4), low], "z", 1),
                (hall.at[0, lax.rem(z + 1, 4), two], "z", 3),
                (hall.at[1, low, lax.rem(x + 3, 4)], "x", 1),
                (hall.at[1, two, lax.rem(x + 1, 4)], "x", 3),
            ):
                self.go(2, spot, spot, axis_peer(axis, j))
            self.expect(2, hall.at[:, :, 0])
        else:
            self.done()


class Heads(Steps):
    def __init__(self, part, sib_recv, both, y_recv, share, send, recv):
        super().__init__(send, recv)
        self.part, self.sib_recv, self.both, self.y_recv, self.share = part, sib_recv, both, y_recv, share

    def run(self, k):
        y = axis_place("y")
        if k == 0:
            self.go(0, self.part.at[1], self.sib_recv, sibling())
            self.expect(0, self.sib_recv)
        elif k == 1:
            self.both[...] = (self.part[0].astype(f32) + self.sib_recv[...].astype(f32)).astype(bf16)
            for j in range(1, 4):
                there = lax.rem(y + j, 4)
                self.go(1, self.both.at[pl.ds(there * SHARE, SHARE)], self.y_recv.at[j - 1], axis_peer("y", j))
            self.expect(1, self.y_recv)
        else:
            acc = self.both[pl.ds(y * SHARE, SHARE)].astype(f32)
            for j in range(3):
                acc = acc + self.y_recv[j].astype(f32)
            self.share[0:SHARE, :] = acc.astype(bf16)
            self.done()


class Quarters(Steps):
    def __init__(self, part, y_recv, send, recv):
        super().__init__(send, recv)
        self.part, self.y_recv = part, y_recv

    def run(self, k):
        y = axis_place("y")
        if k == 0:
            for j in range(1, 4):
                self.go(0, self.part.at[lax.rem(y + j, 4)], self.y_recv.at[j - 1], axis_peer("y", j))
            self.expect(0, self.y_recv)
        else:
            acc = self.part[y].astype(f32)
            for j in range(3):
                acc = acc + self.y_recv[j].astype(f32)
            self.done()
            return acc.astype(bf16)

    def total(self):
        self.collect()
        return self.run(1)


class Vectors:
    def __init__(self, buf, slots, send_sem, recv_sem):
        self.buf, self.slots, self.send_sem, self.recv_sem = buf, slots, send_sem, recv_sem
        self.at = 0

    def step(self):
        k = self.at
        self.at = k + 1
        if k == 0:
            value = self.buf[0]
        else:
            gauge = self.slots.at[k - 1, pl.ds(0, 3 if k < 4 else 1)]
            arrived(gauge, self.recv_sem.at[k - 1])
            arrived(gauge, self.send_sem.at[k - 1])
            value = self.slots[k - 1, 0]
            for j in range(1, 4 if k < 4 else 2):
                value = value + self.slots[k - 1, j]
        if k == 4:
            self.buf[1] = value
            return
        here = axis_place("xyz"[k]) if k < 3 else lax.rem(lax.axis_index("rows"), 2)
        devices = [axis_peer("xyz"[k], j) for j in range(1, 4)] if k < 3 else [sibling()]
        self.slots[k, here] = value
        for device in devices:
            spot = self.slots.at[k, here]
            remote(spot, spot, self.send_sem.at[k], self.recv_sem.at[k], device).start()


def block_kernel(
    offs_h, x_h, dy_h, ln1g_h, ln1b_h, bq_h, bv_h, bout_h, ln2g_h, ln2b_h, bup_h, bdown_h,
    wqkv_h, wout_h, wup_h, wdown_h,
    out_h, ig_h, ag0, ag1, agh, vecs_h,
    offs, x_ref, dy_ref, ln1g, ln1b, bq, bv, bout, ln2g, ln2b, bup, bdown,
    out_ref, ig_ref, vecs,
    wqkv, wout, wup, wdown, wsem,
    qkt, vals, rqk, rv, kn, vt, ot, lse, atts, ratt,
    hall, n1, rs1, h2ta, dya, actt, acta, gp, gpa, gb, gbs, attts, gres,
    gattt, rda, kt, vn, qn, don, dk, dv, dqkv, rdq,
    asend, arecv, ssend, srecv,
    *rest,
):
    (vbuf, vrecv, vsend, vrsem, lbuf, lrecv, lsend, lrsem, osem,
     hsend, hrecv, hpart, hsib, hboth, hy, hmine, wop, wor) = rest[:18]
    rest = rest[18:]
    sems = [rest[2 * k : 2 * k + 2] for k in range(12)]
    own, rest = rest[24], rest[25:]
    down_parts, down_recv1, down_mid, down_recv2 = [rest[2 * k : 2 * k + 2] for k in range(4)]
    up_parts, up_recv1, up_mid, up_recv2 = [rest[8 + 2 * k : 10 + 2 * k] for k in range(4)]
    out_parts, out_recv1, out_mid, out_recv2 = [rest[16 + 2 * k : 18 + 2 * k] for k in range(4)]
    down_share, up_share = rest[24:]
    loads = {}

    def load(name, src, dst):
        copy = pltpu.make_async_copy(src, dst, wsem.at[len(loads)])
        copy.start()
        loads[name] = copy

    load("x", x_h, x_ref)
    load("ln1g", ln1g_h, ln1g)
    load("ln1b", ln1b_h, ln1b)
    for t in (1, 0, 2):
        cols = pl.ds(t * D, D)
        load(f"qkv{t}", wqkv_h.at[:, cols], wqkv.at[:, cols])
    load("bq", bq_h, bq)
    load("bv", bv_h, bv)
    load("dy", dy_h, dy_ref)
    load("offs", offs_h, offs)
    load("out", wout_h, wout)
    for name, src, dst in (
        ("bout", bout_h, bout), ("ln2g", ln2g_h, ln2g), ("ln2b", ln2b_h, ln2b),
        ("bup", bup_h, bup), ("bdown", bdown_h, bdown),
    ):
        load(name, src, dst)
    load("up", wup_h, wup)
    load("down", wdown_h, wdown)
    stores = []

    def ready(*names):
        for name in names:
            loads[name].wait()

    def store(src, dst):
        copy = pltpu.make_async_copy(src, dst, osem.at[len(stores)])
        copy.start()
        stores.append(copy)

    bar, count = greet()
    vecg = vbuf.at[0]
    vecl = lbuf.at[0]
    early = Vectors(vbuf, vrecv, vsend, vrsem)
    late = Vectors(lbuf, lrecv, lsend, lrsem)
    gather = Gather(hall, hsend, hrecv)
    heads = Heads(hpart, hsib, hboth, hy, hmine, *sems[0])
    dy_rows = RowGather(dya, *sems[1])
    h2_rows = RowGather(h2ta, *sems[2])
    act_rows = RowSwap(actt, acta, *sems[3])
    gp_rows = RowSwap(gp, gpa, *sems[4])
    quarters = Quarters(wop, wor, *sems[5])
    down_sum = Scatter(CUT_DOWN, down_parts, down_recv1, down_mid, down_recv2, down_share, *sems[6])
    up_sum = Scatter(CUT_UP, up_parts, up_recv1, up_mid, up_recv2, up_share, *sems[7])
    down_all = Spread(down_share, ag0, WAYS_DOWN, *sems[8], own.at[0])
    up_all = Spread(up_share, ag1, WAYS_UP, *sems[9], own.at[1])
    head_all = Spread(hmine, agh, WAYS_LAST, *sems[10], own.at[2])
    out_sum = Scatter(CUT_OUT, out_parts, out_recv1, out_mid, out_recv2, hmine.at[pl.ds(SHARE, sum(CUT_OUT))], *sems[11])
    row = lax.axis_index("rows")

    def line(ref):
        return ref[...].astype(f32).reshape(1, D)

    core = lax.rem(lax.axis_index("rows"), 2)
    other = 1 - core
    sib = sibling()
    to_sib = []

    def send_sib(n, src, dst):
        copy = remote(src, dst, ssend.at[n], srecv.at[n], sib)
        copy.start()
        to_sib.append(copy)

    ready("x", "ln1g", "ln1b")
    x = x_ref[...].astype(f32)
    n, rs = norm_parts(x)
    n1[...] = n
    rs1[...] = rs
    h1f = n * line(ln1g) + line(ln1b)
    h1 = h1f.astype(bf16)
    for half in range(2):
        hall[half, axis_place("z"), axis_place("x")] = h1[:, half * 384 : (half + 1) * 384]
    for t in (1, 0, 2):
        ready(f"qkv{t}")
        y = dot(h1, wqkv[:, t * D : (t + 1) * D])
        if t == 0:
            ready("bq")
            y = y + line(bq)
        if t == 2:
            ready("bv")
            y = y + line(bv)
        low = jnp.transpose(y).astype(bf16).reshape(H, HS, TOK)
        if t < 2:
            qkt[:, t * HS : (t + 1) * HS, :] = low
        else:
            vals[...] = low
        if t == 0:
            pl.semaphore_wait(bar, count)
            moved = [Exchange(qkt, rqk, asend.at[0], arecv.at[0]).all()]
    moved.append(Exchange(vals, rv, asend.at[1], arecv.at[1]).all())
    ready("dy", "offs")
    dya[row] = dy_ref[...]
    dy_rows.step()
    for copy in moved:
        copy.wait()
    gather.step()

    attended = Exchange(atts, ratt, asend.at[2], arecv.at[2])
    attend_forward(
        offs, rqk, rv, kn, vt, ot, lse, atts,
        attended.one,
    )
    ready("out", "bout", "ln2g", "ln2b", "bup", "bdown", "up", "down")
    gather.step()
    attended.wait()
    dy_rows.step()

    att = jnp.transpose(ratt[...].reshape(D, TOK).astype(f32)).astype(bf16)
    send_sib(0, ratt.at[pl.ds(other * 8, 8)], attts)
    resid = x_ref[...].astype(f32) + dot(att, wout[...]) + line(bout)
    n2, rs2 = norm_parts(resid)
    h2f = n2 * line(ln2g) + line(ln2b)
    h2 = h2f.astype(bf16)
    h2ta[row] = jnp.transpose(h2f).astype(bf16)
    h2_rows.step()
    dy = dy_ref[...]
    down = None
    dh2 = None
    for c in range(4):
        cols = slice(c * D, (c + 1) * D)
        pre = dot(h2, wup[:, cols]) + bup[cols].astype(f32).reshape(1, D)
        square = pre * pre
        t = jnp.tanh(GELU_C * (pre + GELU_A * (square * pre)))
        act = 0.5 * pre * (1.0 + t)
        slope = 0.5 * (1.0 + t) + (0.5 * GELU_C) * pre * (1.0 - t * t) * (1.0 + (3.0 * GELU_A) * square)
        part = dot(act.astype(bf16), wdown[cols, :])
        down = part if down is None else down + part
        act_t = jnp.transpose(act).astype(bf16)
        actt[2 * c] = act_t[0:384]
        actt[2 * c + 1] = act_t[384:768]
        gpre = (dot_nt(dy, wdown[cols, :]) * slope).astype(bf16)
        gp[2 * c] = gpre[:, 0:384]
        gp[2 * c + 1] = gpre[:, 384:768]
        vecg[BUP + c : BUP + c + 1, :] = over_tokens(gpre.astype(f32))
        part = dot_nt(gpre, wup[:, cols])
        dh2 = part if dh2 is None else dh2 + part
    act_rows.step()
    gp_rows.step()
    out_ref[...] = (resid + down + line(bdown)).astype(bf16)
    store(out_ref, out_h)
    vecg[BDOWN : BDOWN + 1, :] = over_tokens(dy.astype(f32))
    vecg[LN2G : LN2G + 1, :] = over_tokens(dh2 * n2)
    vecg[LN2B : LN2B + 1, :] = over_tokens(dh2)
    grad = dy.astype(f32) + norm_back(dh2, n2, rs2, line(ln2g))
    gres[...] = grad
    branch = grad.astype(bf16)
    gb[...] = branch
    vecg[BOUT : BOUT + 1, :] = over_tokens(branch.astype(f32))
    gattt[...] = jnp.transpose(dot_nt(branch, wout[...])).astype(bf16).reshape(H, HS, TOK)
    moved = Exchange(gattt, rda, asend.at[3], arecv.at[3]).all()
    h2_rows.step()
    send_sib(1, gb, gbs)

    gather.step()
    moved.wait()

    def part_out():
        for copy in to_sib:
            copy.wait()
        left = jnp.concatenate(
            [ratt[pl.ds(core * 8, 8)].reshape(384, TOK), attts[...].reshape(384, TOK)], axis=1
        )
        right = jnp.concatenate([gb[...], gbs[...]], axis=0)
        res = dot(left, right).astype(bf16)
        for k in range(4):
            for t in range(6):
                wop[k, t * 96 : (t + 1) * 96, :] = res[k * 96 : (k + 1) * 96, t * TOK : (t + 1) * TOK]
        quarters.step()

    def grads_down():
        dy_rows.step()
        act_rows.step()
        left = jnp.concatenate([acta[k] for k in range(8)], axis=1)
        res = dot(left, dya[...].reshape(8 * TOK, D)).astype(bf16)
        for t in range(6):
            down_sum.put(res[:, t * TOK : (t + 1) * TOK], t * 384)
        down_sum.step()

    def grads_up():
        h2_rows.step()
        gp_rows.step()
        left = jnp.concatenate([h2ta[k] for k in range(8)], axis=1)
        res = dot(left, gpa[...].reshape(8 * TOK, 384)).astype(bf16)
        for t in range(3):
            up_sum.put(res[:, t * TOK : (t + 1) * TOK], t * D)
        up_sum.step()

    def grads_out():
        out_sum.put(quarters.total(), 0)
        out_sum.put(jnp.zeros((192, TOK), bf16), 576)
        out_sum.step()

    back = Exchange(dqkv, rdq, asend.at[4], arecv.at[4])

    def between(i):
        for half in (0, 1):
            back.one(2 * i + half)
        if i == 7:
            dy_rows.step()
            early.step()
        elif i == 6:
            part_out()
        elif i == 4:
            grads_down()
        elif i == 1:
            down_sum.step()

    attend_backward(offs, rqk, rv, kn, kt, vn, qn, don, rda, ot, lse, dqkv, dk, dv, between)
    h2_rows.step()
    grads_up()
    back.wait()

    dh1t = None
    ones = jnp.ones((8, TOK), bf16)
    for t in range(3):
        grad_t = rdq[:, t * HS : (t + 1) * HS, :].reshape(D, TOK)
        part = dot(wqkv[:, t * D : (t + 1) * D], grad_t)
        dh1t = part if dh1t is None else dh1t + part
        if t != 1:
            row = BQ if t == 0 else BV
            vecl[row : row + 1, :] = dot_nt(ones, grad_t)[0:1, :]
    dh1 = jnp.transpose(dh1t)
    n = n1[...]
    vecl[LN1G : LN1G + 1, :] = over_tokens(dh1 * n)
    vecl[LN1B : LN1B + 1, :] = over_tokens(dh1)
    vecl[4:8, :] = jnp.zeros((4, D), f32)
    gather.step()
    spread = jnp.concatenate([dqkv[k] for k in range(NB)], axis=1)

    def part_head(slot, half):
        res = dot(spread, hall[half].reshape(SEQ, 384)).astype(bf16)
        for u in range(3):
            hpart[slot, u * 144 : (u + 1) * 144, :] = res[:, u * TOK : (u + 1) * TOK]
        hpart[slot, 432:HEAD_ROWS, :] = jnp.zeros((HEAD_ROWS - 432, TOK), bf16)

    part_head(1, other)
    heads.step()
    down_sum.step()
    down_all.step()
    part_head(0, core)
    early.step()
    late.step()
    grads_out()
    heads.step()
    up_sum.step()
    down_all.step()
    late.step()
    ig_ref[...] = (gres[...] + norm_back(dh1, n, rs1[...], line(ln1g))).astype(bf16)
    store(ig_ref, ig_h)
    out_sum.step()
    heads.step()
    early.step()
    up_sum.step()
    up_all.step()
    down_all.step()
    late.step()
    out_sum.step()
    head_all.step()
    up_all.step()
    early.step()
    down_all.step()
    late.step()
    head_all.step()
    late.step()
    early.step()
    vecs[0] = vbuf[1]
    vecs[1] = lbuf[1]
    store(vecs, vecs_h)
    up_all.step()
    head_all.step()
    up_all.step()
    head_all.step()
    down_all.step()
    up_all.step()
    head_all.step()
    for item in (down_all, up_all, head_all):
        item.step()
    for item in (down_sum, up_sum, out_sum):
        item.done()
    for copy in stores:
        copy.wait()


VMEM = pl.BlockSpec(memory_space=pltpu.VMEM)
SMEM = pl.BlockSpec(memory_space=pltpu.SMEM)
ANY = pl.BlockSpec(memory_space=pl.ANY)
HBM = pl.BlockSpec(memory_space=pltpu.HBM)


def call_block(offsets, x, dy, vectors, weights):
    v = pltpu.VMEM
    dma = pltpu.SemaphoreType.DMA
    shape = jax.ShapeDtypeStruct
    return pl.pallas_call(
        block_kernel,
        out_shape=(
            v((TOK, D), bf16),
            v((TOK, D), bf16),
            v((2, 4, 4, 4, sum(CUT_DOWN), TOK), bf16),
            v((2, 4, 4, 4, sum(CUT_UP), TOK), bf16),
            v((2, 4, 4, 4, ROWS_LAST, TOK), bf16),
            v((2, VROWS, D), f32),
        ),
        in_specs=[HBM] * 16,
        out_specs=(ANY,) * 6,
        scratch_shapes=[
            pltpu.SMEM((1, 8), jnp.int32), v((TOK, D), bf16), v((TOK, D), bf16),
            *[v((FF if k == 7 else D,), bf16) for k in range(9)],
            v((TOK, D), bf16), v((TOK, D), bf16), v((2, VROWS, D), f32),
            v((D, 3 * D), bf16), v((D, D), bf16), v((D, FF), bf16), v((FF, D), bf16), dma((20,)),
            v((NB, 96, TOK), bf16), v((NB, HS, TOK), bf16), v((NB, 96, TOK), bf16), v((NB, HS, TOK), bf16),
            v((SEQ, HS), bf16), v((HS, SEQ), bf16),
            v((HS, SEQ), f32), v((1, SEQ), f32), v((NB, HS, TOK), bf16), v((NB, HS, TOK), bf16),
            v((2, 4, 4, TOK, 384), bf16), v((TOK, D), f32), v((TOK, 1), f32),
            v((8, D, TOK), bf16), v((8, TOK, D), bf16),
            v((8, 384, TOK), bf16), v((8, 384, TOK), bf16), v((8, TOK, 384), bf16), v((8, TOK, 384), bf16),
            v((TOK, D), bf16), v((TOK, D), bf16), v((8, HS, TOK), bf16), v((TOK, D), f32),
            v((NB, HS, TOK), bf16), v((NB, HS, TOK), bf16),
            v((HS, SEQ), bf16), v((SEQ, HS), bf16), v((SEQ, HS), bf16), v((SEQ, HS), bf16),
            v((SEQ, HS), f32), v((SEQ, HS), f32),
            v((NB, 144, TOK), bf16), v((NB, 144, TOK), bf16),
            dma((5,)), dma((5,)), dma((2,)), dma((2,)),
            v((2, VROWS, D), f32), v((4, 4, VROWS, D), f32), dma((4,)), dma((4,)),
            v((2, VROWS, D), f32), v((4, 4, VROWS, D), f32), dma((4,)), dma((4,)), dma((3,)),
            dma((3,)), dma((3,)), v((2, HEAD_ROWS, TOK), bf16), v((HEAD_ROWS, TOK), bf16),
            v((HEAD_ROWS, TOK), bf16), v((3, SHARE, TOK), bf16), v((ROWS_LAST, TOK), bf16),
            v((4, 576, TOK), bf16), v((3, 576, TOK), bf16),
            *[dma((n,)) for n in (2, 3, 3, 1, 1, 1, 4, 4, 5, 5, 5, 4) for _ in range(2)], dma((3,)),
            *[
                v(lead + (cut, TOK), bf16)
                for cuts in (CUT_DOWN, CUT_UP, CUT_OUT)
                for lead in ((4, 4), (3, 4), (4,), (3,))
                for cut in cuts
            ],
            v((sum(CUT_DOWN), TOK), bf16), v((sum(CUT_UP), TOK), bf16),
        ],
        compiler_params=pltpu.CompilerParams(
            collective_id=1, has_side_effects=True, vmem_limit_bytes=43 * 2**20
        ),
    )(*[pltpu.with_memory_space_constraint(a, pltpu.HBM) for a in (offsets, x, dy, *vectors, *weights)])


def widen_kernel(ag0, ag1, agh, vecs, done_h, ig_h, wqkv, wout, wup, wdown, out_h, grad_h, *rest):
    small_h, small = rest[:9], rest[9:18]
    down_out, up_out, out_out, wideb, vsem, ssem, osem = rest[18:]
    passed = [
        pltpu.make_async_copy(done_h, out_h, vsem.at[0]),
        pltpu.make_async_copy(ig_h, grad_h, vsem.at[1]),
    ]

    def pieces(cuts, base, offset, rows):
        at = 0
        while at < rows:
            n = 0 if offset < 16 * cuts[0] else 1
            inside = offset - n * 16 * cuts[0]
            block, lo = inside // cuts[n], inside % cuts[n]
            size = min(cuts[n] - lo, rows - at)
            yield at, size, block // 4, block % 4, base + n * cuts[0] + lo
            at += size
            offset += size

    def widen(ag, cuts, base, k, offset, rows, dst, col):
        for at, size, z, x, lo in pieces(cuts, base, offset, rows):
            part = ag[k % 2, z, x, k // 2, lo : lo + size, :]
            dst[at : at + size, col * TOK : (col + 1) * TOK] = part.astype(f32)

    def head_rows(core, z, x, lo, rows):
        parts = []
        while rows:
            y, inside = lo // SHARE, lo % SHARE
            size = min(SHARE - inside, rows)
            parts.append(agh[core, z, x, y, inside : inside + size, :])
            lo += size
            rows -= size
        return parts

    down_store = [
        pltpu.make_async_copy(down_out.at[k % 3], wdown.at[pl.ds(k * 384, 384)], osem.at[0, k % 3]) for k in range(8)
    ]
    up_store = [
        pltpu.make_async_copy(up_out.at[k % 3], wup.at[:, pl.ds(k * 384, 384)], osem.at[1, k % 3]) for k in range(8)
    ]
    out_store = [
        pltpu.make_async_copy(
            out_out.at[k % 3], wout.at[pl.ds((k % 2) * 384 + (k // 2) * 96, 96)], osem.at[2, k % 3]
        )
        for k in range(8)
    ]
    head_store = [
        pltpu.make_async_copy(wideb.at[k % 3], wqkv.at[pl.ds(k * TOK, TOK)], osem.at[3, k % 3]) for k in range(6)
    ]
    for copy in passed:
        copy.start()
    for k in range(8):
        if k >= 3:
            down_store[k - 3].wait()
        for t in range(6):
            widen(ag0, CUT_DOWN, 0, k, t * 384, 384, down_out.at[k % 3], t)
        down_store[k].start()
        if k >= 3:
            up_store[k - 3].wait()
            out_store[k - 3].wait()
        for t in range(3):
            widen(ag1, CUT_UP, 0, k, t * D, D, up_out.at[k % 3], t)
        up_store[k].start()
        for t in range(6):
            widen(agh, CUT_OUT, SHARE, k, t * 96, 96, out_out.at[k % 3], t)
        out_store[k].start()
        if k < 6:
            if k >= 3:
                head_store[k - 3].wait()
            for t in range(3):
                parts = []
                for head in range(H):
                    parts += head_rows(k // 3, head // 4, head % 4, (k % 3) * 144 + t * HS, HS)
                block = jnp.concatenate(parts, axis=0)
                wideb[k % 3, :, t * D : (t + 1) * D] = jnp.transpose(block.astype(f32))
            head_store[k].start()
        if k == 0:
            places = ((1, LN1G), (1, LN1B), (1, BQ), (1, BV), (0, BOUT), (0, LN2G), (0, LN2B), (0, BUP), (0, BDOWN))
            for n, (ref, (group, line)) in enumerate(zip(small, places)):
                if line == BUP:
                    for c in range(4):
                        ref[c * D : (c + 1) * D] = vecs[0, BUP + c : BUP + c + 1, :].reshape(D)
                else:
                    ref[...] = vecs[group, line : line + 1, :].reshape(D)
                copy = pltpu.make_async_copy(ref, small_h[n], ssem.at[n])
                copy.start()
                passed.append(copy)
    for k in range(5, 8):
        down_store[k].wait()
        up_store[k].wait()
        out_store[k].wait()
        head_store[k - 2].wait()
    for copy in passed:
        copy.wait()


def call_widen(*arrays):
    v = pltpu.VMEM
    dma = pltpu.SemaphoreType.DMA
    shape = jax.ShapeDtypeStruct
    return pl.pallas_call(
        widen_kernel,
        out_shape=(
            shape((D, 3 * D), f32), shape((D, D), f32), shape((D, FF), f32), shape((FF, D), f32),
            shape((TOK, D), bf16), shape((TOK, D), bf16),
        ) + tuple(shape((FF if k == 7 else D,), f32) for k in range(9)),
        in_specs=[VMEM] * 4 + [ANY] * 2,
        out_specs=(ANY,) * 15,
        scratch_shapes=[
            *[v((FF if k == 7 else D,), f32) for k in range(9)],
            v((3, 384, D), f32), v((3, D, 384), f32), v((3, 96, D), f32), v((3, TOK, 3 * D), f32),
            dma((2,)), dma((9,)), dma((4, 3)),
        ],
        compiler_params=pltpu.CompilerParams(vmem_limit_bytes=30 * 2**20),
    )(*[pltpu.with_memory_space_constraint(a, pltpu.VMEM) for a in arrays])


def local(
    block_input, offsets, ln1_gain, ln1_bias, w_qkv, bias_query, bias_value, w_out, bias_out,
    ln2_gain, ln2_bias, w_up, bias_up, w_down, bias_down, cotangent,
):
    out, ig, ag0, ag1, agh, vecs = call_block(
        offsets, block_input.reshape(TOK, D), cotangent.reshape(TOK, D),
        (ln1_gain, ln1_bias, bias_query, bias_value, bias_out, ln2_gain, ln2_bias, bias_up, bias_down),
        (w_qkv, w_out, w_up, w_down),
    )
    wide = call_widen(ag0, ag1, agh, vecs, out, ig)
    g_qkv, g_out, g_up, g_down, out, ig = wide[:6]
    s = wide[6:]
    return (
        out.reshape(1, TOK, D), ig.reshape(1, TOK, D),
        s[0], s[1], g_qkv, s[2], s[3], g_out, s[4], s[5], s[6], g_up, s[7], g_down, s[8],
    )


def solution(mesh):
    tokens = P("rows", "seq", None)
    return jax.shard_map(
        local,
        mesh=mesh,
        in_specs=(tokens, P("rows", None)) + (P(),) * 13 + (tokens,),
        out_specs=(tokens, tokens) + (P(),) * 13,
        check_vma=False,
    )
```

```python
import functools

import jax
import jax.numpy as jnp
from jax import lax
from jax.experimental import pallas as pl
from jax.experimental.pallas import tpu as pltpu
from jax.sharding import PartitionSpec as P

MESH = pl.DeviceIdType.MESH
f32 = jnp.float32
bf16 = jnp.bfloat16

D = 768
H = 16
FF = 3072
HS = 48
SEQ = 2048
TOK = 128
NB = 16
QB = 256
CUT_DOWN = (80, 64)
CUT_UP = (80, 64)
CUT_OUT = (32, 16)
SHARE = 112
HEAD_ROWS = 4 * SHARE
WAYS_DOWN = ((0, 48, "xzy"), (48, 48, "zyx"), (96, 48, "yxz"))
WAYS_UP = WAYS_DOWN
WAYS_HEAD = ((0, 48, "xzy"), (48, 32, "zyx"), (80, 32, "yxz"))
WAYS_OUT = ((0, 16, "xzy"), (16, 16, "zyx"), (32, 16, "yxz"))
SCALE = HS**-0.5
SCALE_LOG2E = SCALE * 1.4426950408889634
NEGATIVE = -1e30
EPSILON = 1e-05
GELU_C = 0.7978845608028654
GELU_A = 0.044715

LN1G, LN1B, BQ, BV = 0, 1, 2, 3
BOUT, LN2G, LN2B, BDOWN, BUP = 0, 1, 2, 3, 4
VROWS = 8
WIDEN_SLOTS = 6


def dot(a, b):
    return jnp.dot(a, b, preferred_element_type=f32)


def dot_nt(a, b):
    return lax.dot_general(a, b, (((1,), (1,)), ((), ())), preferred_element_type=f32)


def turned(block):
    return jnp.transpose(block.astype(f32)).astype(bf16)


def coords():
    r = lax.axis_index("rows")
    s = lax.axis_index("seq")
    return lax.div(r, 2), lax.rem(r, 2), lax.div(s, 4), lax.rem(s, 4)


def device_at(y, c, z, x):
    return (y * 2 + c, z * 4 + x)


def remote(src, dst, send, recv, device):
    return pltpu.make_async_remote_copy(
        src_ref=src, dst_ref=dst, send_sem=send, recv_sem=recv, device_id=device, device_id_type=MESH
    )


def seq_peer(d):
    s = lax.axis_index("seq")
    return lax.rem(s + d, 16)


def axis_peer(axis, j):
    y, c, z, x = coords()
    if axis == "y":
        y = lax.rem(y + j, 4)
    elif axis == "z":
        z = lax.rem(z + j, 4)
    else:
        x = lax.rem(x + j, 4)
    return device_at(y, c, z, x)


def axis_place(axis):
    y, c, z, x = coords()
    return {"y": y, "z": z, "x": x}[axis]


def sibling():
    y, c, z, x = coords()
    return device_at(y, 1 - c, z, x)


def greet():
    bar = pltpu.get_barrier_semaphore()
    r = lax.axis_index("rows")
    s = lax.axis_index("seq")
    devices = [(r, seq_peer(d)) for d in range(1, 16)] + [(lax.rem(r + d, 8), s) for d in range(1, 8)]
    for device in devices:
        pl.semaphore_signal(bar, inc=1, device_id=device, device_id_type=MESH)
    return bar, len(devices)


def masked(scores, start, key0, query0, diagonal):
    key = lax.broadcasted_iota(jnp.int32, scores.shape, 0) + key0
    ok = key >= start
    if diagonal:
        query = lax.broadcasted_iota(jnp.int32, scores.shape, 1) + query0
        ok = ok & (key <= query)
    return jnp.where(ok, scores, NEGATIVE)


def segment_starts(offs_ref, query0, count):
    place = lax.broadcasted_iota(jnp.int32, (1, count), 1) + query0
    start = jnp.zeros((1, count), jnp.int32)
    for j in range(8):
        o = offs_ref[0, j]
        start = jnp.where(place >= o, o, start)
    return start


def pair(ref, i, lo, hi):
    return jnp.concatenate([ref[2 * i, lo:hi, :], ref[2 * i + 1, lo:hi, :]], axis=1)


def attend_forward(offs_ref, qk, vals, kn, vt, ot, lse, atts, after):
    for s in range(NB):
        kn[s * TOK : (s + 1) * TOK, :] = turned(qk[s, 48:96, :])
        vt[:, s * TOK : (s + 1) * TOK] = vals[s]
    for i in range(SEQ // QB):
        q0 = i * QB
        qt = pair(qk, i, 0, 48)
        start = segment_starts(offs_ref, q0, QB)
        sd = masked(dot(kn[q0 : q0 + QB, :], qt) * SCALE_LOG2E, start, q0, q0, True)
        top = jnp.max(sd, axis=0, keepdims=True)
        if i:
            so = masked(dot(kn[0:q0, :], qt) * SCALE_LOG2E, start, 0, q0, False)
            top = jnp.maximum(top, jnp.max(so, axis=0, keepdims=True))
        pd = jnp.exp2(sd - top)
        total = jnp.sum(pd, axis=0, keepdims=True)
        out = dot(vt[:, q0 : q0 + QB], pd.astype(bf16))
        if i:
            po = jnp.exp2(so - top)
            total = total + jnp.sum(po, axis=0, keepdims=True)
            out = out + dot(vt[:, 0:q0], po.astype(bf16))
        out = out / total
        ot[:, q0 : q0 + QB] = out
        lse[:, q0 : q0 + QB] = top + jnp.log2(total)
        low = out.astype(bf16)
        atts[2 * i] = low[:, 0:TOK]
        atts[2 * i + 1] = low[:, TOK:QB]
        after(2 * i)
        after(2 * i + 1)


def attend_backward(offs_ref, qk, vals, kn, kt, vn, qn, don, dor, ot, lse, dqkv, dk, dv, after):
    for s in range(NB):
        rows = slice(s * TOK, (s + 1) * TOK)
        vn[rows, :] = turned(vals[s])
        qn[rows, :] = turned(qk[s, 0:48, :])
        don[rows, :] = turned(dor[s])
        kt[:, rows] = qk[s, 48:96, :]
    last = SEQ // QB - 1
    for i in reversed(range(SEQ // QB)):
        q0 = i * QB
        qt = pair(qk, i, 0, 48)
        dot_t = pair(dor, i, 0, 48)
        start = segment_starts(offs_ref, q0, QB)
        level = lse[:, q0 : q0 + QB]
        inner = jnp.sum(dot_t.astype(f32) * ot[:, q0 : q0 + QB], axis=0, keepdims=True)
        q_n = qn[q0 : q0 + QB, :]
        do_n = don[q0 : q0 + QB, :]
        dq = None
        for a, b, diagonal in ([(0, q0, False)] if i else []) + [(q0, q0 + QB, True)]:
            scores = masked(dot(kn[a:b, :], qt) * SCALE_LOG2E, start, a, q0, diagonal)
            probs = jnp.exp2(scores - level)
            dp = dot(vn[a:b, :], dot_t)
            ds = (probs * (dp - inner)).astype(bf16)
            dv_part = dot(probs.astype(bf16), do_n)
            dk_part = dot(ds, q_n)
            if i == last:
                dk[a:b, :] = dk_part
                dv[a:b, :] = dv_part
            else:
                dk[a:b, :] += dk_part
                dv[a:b, :] += dv_part
            dq_part = dot(kt[:, a:b], ds)
            dq = dq_part if dq is None else dq + dq_part
        dq = (dq * SCALE).astype(bf16)
        for h in range(2):
            s = 2 * i + h
            rows = slice(s * TOK, (s + 1) * TOK)
            dqkv[s, 0:48, :] = dq[:, h * TOK : (h + 1) * TOK]
            dqkv[s, 48:96, :] = (jnp.transpose(dk[rows, :]) * SCALE).astype(bf16)
            dqkv[s, 96:144, :] = jnp.transpose(dv[rows, :]).astype(bf16)
        after(i)


def norm_parts(values):
    center = values - jnp.mean(values, axis=-1, keepdims=True)
    spread = jnp.mean(center * center, axis=-1, keepdims=True)
    rs = lax.rsqrt(spread + EPSILON)
    return center * rs, rs


def norm_back(grad, n, rs, gain):
    gg = grad * gain
    return rs * (
        gg - jnp.mean(gg, axis=-1, keepdims=True) - n * jnp.mean(gg * n, axis=-1, keepdims=True)
    )


def over_tokens(values):
    return jnp.sum(values, axis=0, keepdims=True)


def arrived(gauge, sem):
    pltpu.make_async_copy(gauge, gauge, sem).wait()


class Steps:
    def __init__(self, send, recv):
        self.send, self.recv = send, recv
        self.sent = []
        self.live = []
        self.at = 0

    def go(self, group, src, dst, device):
        remote(src, dst, self.send.at[group], self.recv.at[group], device).start()

    def expect(self, group, gauge):
        self.live.append((group, gauge))
        self.sent.append((group, gauge))

    def collect(self):
        for group, gauge in self.live:
            arrived(gauge, self.recv.at[group])
        self.live = []

    def step(self):
        self.collect()
        k = self.at
        self.at = k + 1
        self.run(k)

    def done(self):
        for group, gauge in self.sent:
            arrived(gauge, self.send.at[group])
        self.sent = []


class Scatter(Steps):
    def __init__(self, cuts, parts, recv1, mid, recv2, share, send, recv):
        super().__init__(send, recv)
        self.cuts, self.parts, self.recv1, self.mid, self.recv2, self.share = cuts, parts, recv1, mid, recv2, share

    def put(self, value, offset):
        at, rows = 0, value.shape[0]
        while at < rows:
            k = 0 if offset < 16 * self.cuts[0] else 1
            inside = offset - k * 16 * self.cuts[0]
            block, lo = inside // self.cuts[k], inside % self.cuts[k]
            size = min(self.cuts[k] - lo, rows - at)
            self.parts[k][block // 4, block % 4, lo : lo + size, :] = value[at : at + size]
            at += size
            offset += size

    def run(self, k):
        z, x = axis_place("z"), axis_place("x")
        first, second = self.parts
        if k == 0:
            for j in range(1, 4):
                self.go(0, first.at[:, lax.rem(x + j, 4)], self.recv1[0].at[j - 1], axis_peer("x", j))
                self.go(1, second.at[lax.rem(z + j, 4)], self.recv1[1].at[j - 1], axis_peer("z", j))
            for n in range(2):
                self.expect(n, self.recv1[n])
        elif k == 1:
            for n, mine in enumerate((first[:, x], second[z])):
                acc = mine.astype(f32)
                for j in range(3):
                    acc = acc + self.recv1[n][j].astype(f32)
                self.mid[n][...] = acc.astype(bf16)
            for j in range(1, 4):
                self.go(2, self.mid[0].at[lax.rem(z + j, 4)], self.recv2[0].at[j - 1], axis_peer("z", j))
                self.go(3, self.mid[1].at[lax.rem(x + j, 4)], self.recv2[1].at[j - 1], axis_peer("x", j))
            for n in range(2):
                self.expect(2 + n, self.recv2[n])
        else:
            lo = 0
            for n, here in enumerate((z, x)):
                acc = self.mid[n][here].astype(f32)
                for j in range(3):
                    acc = acc + self.recv2[n][j].astype(f32)
                self.share[lo : lo + self.cuts[n], :] = acc.astype(bf16)
                lo += self.cuts[n]


class Spread(Steps):
    def __init__(self, share, ag, ways, send, recv, own):
        super().__init__(send, recv)
        self.share, self.ag, self.ways, self.own = share, ag, ways, own

    def spot(self, lo, size, whole, **at):
        core = lax.rem(lax.axis_index("rows"), 2)
        index = [at[a] if a in at else slice(None) if a in whole else axis_place(a) for a in "zxy"]
        return self.ag.at[(core, *index, pl.ds(lo, size))]

    def pass_on(self, spot):
        self.go(4, spot, spot, sibling())

    def run(self, k):
        ag = self.ag
        if k == 1:
            self.kept.wait()
        for lo, size, order in self.ways:
            last = order[2]
            here = axis_place(last)
            if k == 0:
                for j in range(1, 4):
                    self.go(0, self.share.at[pl.ds(lo, size)], self.spot(lo, size, ""), axis_peer(order[0], j))
            elif k == 1:
                spot = self.spot(lo, size, order[0])
                for j in range(1, 4):
                    self.go(1, spot, spot, axis_peer(order[1], j))
            elif k == 2:
                spot = self.spot(lo, size, order[:2])
                self.go(2, spot, spot, axis_peer(last, 1))
                self.go(2, spot, spot, axis_peer(last, 3))
                self.pass_on(spot)
            elif k == 3:
                before, after = lax.rem(here + 3, 4), lax.rem(here + 1, 4)
                cut = "x" if last == "z" else "z"
                low = self.spot(lo, size, order[:2], **{last: before, cut: pl.ds(0, 2)})
                high = self.spot(lo, size, order[:2], **{last: after, cut: pl.ds(2, 2)})
                self.go(3, low, low, axis_peer(last, 1))
                self.go(3, high, high, axis_peer(last, 3))
                self.pass_on(self.spot(lo, size, order[:2], **{last: before}))
                self.pass_on(self.spot(lo, size, order[:2], **{last: after}))
            elif k == 4:
                self.pass_on(self.spot(lo, size, order[:2], **{last: lax.rem(here + 2, 4)}))
        three = pl.ds(0, 3)
        if k == 0:
            self.kept = pltpu.make_async_copy(self.share, self.spot(0, self.share.shape[0], ""), self.own)
            self.kept.start()
            self.expect(0, ag.at[0, 0, 0, three])
        elif k == 1:
            self.expect(1, ag.at[0, 0, three])
        elif k == 2:
            self.expect(2, ag.at[0, pl.ds(0, 2)])
        elif k == 3:
            self.expect(3, ag.at[0, 0])
        elif k == 4:
            self.expect(4, ag.at[0])
        else:
            self.done()


class RowSwap(Steps):
    def __init__(self, src, dst, send, recv):
        super().__init__(send, recv)
        self.src, self.dst = src, dst

    def run(self, k):
        r, s = lax.axis_index("rows"), lax.axis_index("seq")
        if k == 0:
            for d in range(1, 8):
                peer = lax.rem(r + d, 8)
                self.go(0, self.src.at[peer], self.dst.at[r], (peer, s))
            self.dst[r] = self.src[r]
            self.expect(0, self.dst.at[pl.ds(0, 7)])
        else:
            self.done()


class RowGather(Steps):
    def __init__(self, dst, send, recv):
        super().__init__(send, recv)
        self.dst = dst

    def run(self, k):
        r = lax.axis_index("rows")
        dst = self.dst
        half = dst.shape[1] // 2
        before, after = lax.rem(r + 6, 8), lax.rem(r + 2, 8)
        if k == 0:
            for device in (axis_peer("y", 1), axis_peer("y", 3)):
                self.go(0, dst.at[r], dst.at[r], device)
            self.go(2, dst.at[r], dst.at[r], sibling())
            self.expect(0, dst.at[pl.ds(0, 2)])
        elif k == 1:
            low, high = dst.at[before, pl.ds(0, half)], dst.at[after, pl.ds(half, half)]
            self.go(1, low, low, axis_peer("y", 1))
            self.go(1, high, high, axis_peer("y", 3))
            for spot in (dst.at[before], dst.at[after]):
                self.go(2, spot, spot, sibling())
            self.expect(1, dst.at[0])
        elif k == 2:
            spot = dst.at[lax.rem(r + 4, 8)]
            self.go(2, spot, spot, sibling())
            self.expect(2, dst.at[pl.ds(0, 4)])
        else:
            self.done()


class Exchange:
    def __init__(self, src, dst, send, recv):
        self.src, self.dst, self.send, self.recv = src, dst, send, recv

    def all(self):
        r = lax.axis_index("rows")
        s = lax.axis_index("seq")
        for d in range(1, 16):
            peer = seq_peer(d)
            remote(self.src.at[peer], self.dst.at[s], self.send, self.recv, (r, peer)).start()
        self.dst[s] = self.src[s]
        return self

    def one(self, block):
        r = lax.axis_index("rows")
        s = lax.axis_index("seq")

        @pl.when(s != block)
        def _():
            remote(self.src.at[block], self.dst.at[s], self.send, self.recv, (r, block)).start()

        @pl.when(s == block)
        def _():
            self.dst[s] = self.src[block]

    def wait(self):
        gauge = self.dst.at[pl.ds(0, 15)]
        arrived(gauge, self.recv)
        arrived(gauge, self.send)


class Gather(Steps):
    def __init__(self, hall, send, recv):
        super().__init__(send, recv)
        self.hall = hall

    def run(self, k):
        z, x = axis_place("z"), axis_place("x")
        hall = self.hall
        if k == 0:
            for j in range(1, 4):
                self.go(0, hall.at[0, z, x], hall.at[0, z, x], axis_peer("x", j))
                self.go(0, hall.at[1, z, x], hall.at[1, z, x], axis_peer("z", j))
            self.expect(0, hall.at[:, pl.ds(0, 3), 0])
        elif k == 1:
            for j in (1, 3):
                self.go(1, hall.at[0, z], hall.at[0, z], axis_peer("z", j))
                self.go(1, hall.at[1, :, x], hall.at[1, :, x], axis_peer("x", j))
            self.expect(1, hall.at[0])
        elif k == 2:
            two, low = pl.ds(2, 2), pl.ds(0, 2)
            for spot, axis, j in (
                (hall.at[0, lax.rem(z + 3, 4), low], "z", 1),
                (hall.at[0, lax.rem(z + 1, 4), two], "z", 3),
                (hall.at[1, low, lax.rem(x + 3, 4)], "x", 1),
                (hall.at[1, two, lax.rem(x + 1, 4)], "x", 3),
            ):
                self.go(2, spot, spot, axis_peer(axis, j))
            self.expect(2, hall.at[:, :, 0])
        else:
            self.done()


class Heads(Steps):
    def __init__(self, part, sib_recv, both, y_recv, share, send, recv):
        super().__init__(send, recv)
        self.part, self.sib_recv, self.both, self.y_recv, self.share = part, sib_recv, both, y_recv, share

    def run(self, k):
        y = axis_place("y")
        if k == 0:
            self.go(0, self.part.at[1], self.sib_recv, sibling())
            self.expect(0, self.sib_recv)
        elif k == 1:
            self.both[...] = (self.part[0].astype(f32) + self.sib_recv[...].astype(f32)).astype(bf16)
            for j in range(1, 4):
                there = lax.rem(y + j, 4)
                self.go(1, self.both.at[pl.ds(there * SHARE, SHARE)], self.y_recv.at[j - 1], axis_peer("y", j))
            self.expect(1, self.y_recv)
        else:
            acc = self.both[pl.ds(y * SHARE, SHARE)].astype(f32)
            for j in range(3):
                acc = acc + self.y_recv[j].astype(f32)
            self.share[0:SHARE, :] = acc.astype(bf16)
            self.done()


class Quarters(Steps):
    def __init__(self, part, y_recv, send, recv):
        super().__init__(send, recv)
        self.part, self.y_recv = part, y_recv

    def run(self, k):
        y = axis_place("y")
        if k == 0:
            for j in range(1, 4):
                self.go(0, self.part.at[lax.rem(y + j, 4)], self.y_recv.at[j - 1], axis_peer("y", j))
            self.expect(0, self.y_recv)
        else:
            acc = self.part[y].astype(f32)
            for j in range(3):
                acc = acc + self.y_recv[j].astype(f32)
            self.done()
            return acc.astype(bf16)

    def total(self):
        self.collect()
        return self.run(1)


class Vectors:
    def __init__(self, buf, slots, send_sem, recv_sem):
        self.buf, self.slots, self.send_sem, self.recv_sem = buf, slots, send_sem, recv_sem
        self.at = 0

    def step(self):
        k = self.at
        self.at = k + 1
        if k == 0:
            value = self.buf[0]
        else:
            gauge = self.slots.at[k - 1, pl.ds(0, 3 if k < 4 else 1)]
            arrived(gauge, self.recv_sem.at[k - 1])
            arrived(gauge, self.send_sem.at[k - 1])
            value = self.slots[k - 1, 0]
            for j in range(1, 4 if k < 4 else 2):
                value = value + self.slots[k - 1, j]
        if k == 4:
            self.buf[1] = value
            return
        here = axis_place("xyz"[k]) if k < 3 else lax.rem(lax.axis_index("rows"), 2)
        devices = [axis_peer("xyz"[k], j) for j in range(1, 4)] if k < 3 else [sibling()]
        self.slots[k, here] = value
        for device in devices:
            spot = self.slots.at[k, here]
            remote(spot, spot, self.send_sem.at[k], self.recv_sem.at[k], device).start()


def block_kernel(
    offs_h, x_h, dy_h, ln1g_h, ln1b_h, bq_h, bv_h, bout_h, ln2g_h, ln2b_h, bup_h, bdown_h,
    wqkv_h, wout_h, wup_h, wdown_h,
    out_h, ig_h, ag0, ag1, agh, agw, vecs_h,
    offs, x_ref, dy_ref, ln1g, ln1b, bq, bv, bout, ln2g, ln2b, bup, bdown,
    out_ref, ig_ref, vecs,
    wqkv, wout, wup, wdown, wsem,
    qkvt, rqk, kn, vt, ot, lse, atts, ratt,
    hall, n1, rs1, h2ta, dya, actt, acta, gp, gpa, gb, gbs, attts, gres,
    gattt, rda, kt, vn, qn, don, dk, dv, dqkv, rdq,
    asend, arecv, ssend, srecv,
    *rest,
):
    (vbuf, vrecv, vsend, vrsem, lbuf, lrecv, lsend, lrsem, osem,
     hsend, hrecv, hpart, hsib, hboth, hy, hmine, wop, wor) = rest[:18]
    rest = rest[18:]
    sems = [rest[2 * k : 2 * k + 2] for k in range(13)]
    own, rest = rest[26], rest[27:]
    down_parts, down_recv1, down_mid, down_recv2 = [rest[2 * k : 2 * k + 2] for k in range(4)]
    up_parts, up_recv1, up_mid, up_recv2 = [rest[8 + 2 * k : 10 + 2 * k] for k in range(4)]
    out_parts, out_recv1, out_mid, out_recv2 = [rest[16 + 2 * k : 18 + 2 * k] for k in range(4)]
    down_share, up_share, out_share = rest[24:]
    loads = {}

    def load(name, src, dst):
        copy = pltpu.make_async_copy(src, dst, wsem.at[len(loads)])
        copy.start()
        loads[name] = copy

    load("x", x_h, x_ref)
    load("ln1g", ln1g_h, ln1g)
    load("ln1b", ln1b_h, ln1b)
    for t in (1, 0, 2):
        cols = pl.ds(t * D, D)
        load(f"qkv{t}", wqkv_h.at[:, cols], wqkv.at[:, cols])
    load("bq", bq_h, bq)
    load("bv", bv_h, bv)
    load("dy", dy_h, dy_ref)
    load("offs", offs_h, offs)
    stores = []

    def ready(*names):
        for name in names:
            loads[name].wait()

    def store(src, dst):
        copy = pltpu.make_async_copy(src, dst, osem.at[len(stores)])
        copy.start()
        stores.append(copy)

    bar, count = greet()
    vecg = vbuf.at[0]
    vecl = lbuf.at[0]
    early = Vectors(vbuf, vrecv, vsend, vrsem)
    late = Vectors(lbuf, lrecv, lsend, lrsem)
    gather = Gather(hall, hsend, hrecv)
    heads = Heads(hpart, hsib, hboth, hy, hmine, *sems[0])
    dy_rows = RowGather(dya, *sems[1])
    h2_rows = RowGather(h2ta, *sems[2])
    act_rows = RowSwap(actt, acta, *sems[3])
    gp_rows = RowSwap(gp, gpa, *sems[4])
    quarters = Quarters(wop, wor, *sems[5])
    down_sum = Scatter(CUT_DOWN, down_parts, down_recv1, down_mid, down_recv2, down_share, *sems[6])
    up_sum = Scatter(CUT_UP, up_parts, up_recv1, up_mid, up_recv2, up_share, *sems[7])
    down_all = Spread(down_share, ag0, WAYS_DOWN, *sems[8], own.at[0])
    up_all = Spread(up_share, ag1, WAYS_UP, *sems[9], own.at[1])
    head_all = Spread(hmine, agh, WAYS_HEAD, *sems[10], own.at[2])
    out_all = Spread(out_share, agw, WAYS_OUT, *sems[12], own.at[3])
    out_sum = Scatter(CUT_OUT, out_parts, out_recv1, out_mid, out_recv2, out_share, *sems[11])
    row = lax.axis_index("rows")

    def line(ref):
        return ref[...].astype(f32).reshape(1, D)

    core = lax.rem(lax.axis_index("rows"), 2)
    other = 1 - core
    sib = sibling()
    to_sib = []

    def send_sib(n, src, dst):
        copy = remote(src, dst, ssend.at[n], srecv.at[n], sib)
        copy.start()
        to_sib.append(copy)

    ready("x", "ln1g", "ln1b")
    x = x_ref[...].astype(f32)
    n, rs = norm_parts(x)
    n1[...] = n
    rs1[...] = rs
    h1f = n * line(ln1g) + line(ln1b)
    h1 = h1f.astype(bf16)
    for half in range(2):
        hall[half, axis_place("z"), axis_place("x")] = h1[:, half * 384 : (half + 1) * 384]
    for t in (1, 0, 2):
        ready(f"qkv{t}")
        y = dot(h1, wqkv[:, t * D : (t + 1) * D])
        if t == 0:
            ready("bq")
            y = y + line(bq)
        if t == 2:
            ready("bv")
            y = y + line(bv)
        low = jnp.transpose(y).astype(bf16).reshape(H, HS, TOK)
        qkvt[:, t * HS : (t + 1) * HS, :] = low
    pl.semaphore_wait(bar, count)
    moved = Exchange(qkvt, rqk, asend.at[0], arecv.at[0]).all()
    load("out", wout_h, wout)
    for name, src, dst in (
        ("bout", bout_h, bout), ("ln2g", ln2g_h, ln2g), ("ln2b", ln2b_h, ln2b),
        ("bup", bup_h, bup), ("bdown", bdown_h, bdown),
    ):
        load(name, src, dst)
    load("up", wup_h, wup)
    load("down", wdown_h, wdown)
    ready("dy", "offs")
    dya[row] = dy_ref[...]
    dy_rows.step()
    moved.wait()
    rv = rqk.at[:, pl.ds(2 * HS, HS)]
    gather.step()

    attended = Exchange(atts, ratt, asend.at[2], arecv.at[2])
    attend_forward(
        offs, rqk, rv, kn, vt, ot, lse, atts,
        attended.one,
    )
    ready("out", "bout", "ln2g", "ln2b", "bup", "bdown", "up", "down")
    gather.step()
    attended.wait()
    dy_rows.step()

    att = jnp.transpose(ratt[...].reshape(D, TOK).astype(f32)).astype(bf16)
    send_sib(0, ratt.at[pl.ds(other * 8, 8)], attts)
    resid = x_ref[...].astype(f32) + dot(att, wout[...]) + line(bout)
    n2, rs2 = norm_parts(resid)
    h2f = n2 * line(ln2g) + line(ln2b)
    h2 = h2f.astype(bf16)
    h2ta[row] = jnp.transpose(h2f).astype(bf16)
    h2_rows.step()
    dy = dy_ref[...]
    down = None
    dh2 = None
    for c in range(4):
        cols = slice(c * D, (c + 1) * D)
        pre = dot(h2, wup[:, cols]) + bup[cols].astype(f32).reshape(1, D)
        square = pre * pre
        t = jnp.tanh(GELU_C * (pre + GELU_A * (square * pre)))
        act = 0.5 * pre * (1.0 + t)
        slope = 0.5 * (1.0 + t) + (0.5 * GELU_C) * pre * (1.0 - t * t) * (1.0 + (3.0 * GELU_A) * square)
        part = dot(act.astype(bf16), wdown[cols, :])
        down = part if down is None else down + part
        act_t = jnp.transpose(act).astype(bf16)
        actt[2 * c] = act_t[0:384]
        actt[2 * c + 1] = act_t[384:768]
        gpre = (dot_nt(dy, wdown[cols, :]) * slope).astype(bf16)
        gp[2 * c] = gpre[:, 0:384]
        gp[2 * c + 1] = gpre[:, 384:768]
        vecg[BUP + c : BUP + c + 1, :] = over_tokens(gpre.astype(f32))
        part = dot_nt(gpre, wup[:, cols])
        dh2 = part if dh2 is None else dh2 + part
    act_rows.step()
    gp_rows.step()
    out_ref[...] = (resid + down + line(bdown)).astype(bf16)
    store(out_ref, out_h)
    vecg[BDOWN : BDOWN + 1, :] = over_tokens(dy.astype(f32))
    vecg[LN2G : LN2G + 1, :] = over_tokens(dh2 * n2)
    vecg[LN2B : LN2B + 1, :] = over_tokens(dh2)
    grad = dy.astype(f32) + norm_back(dh2, n2, rs2, line(ln2g))
    gres[...] = grad
    branch = grad.astype(bf16)
    gb[...] = branch
    vecg[BOUT : BOUT + 1, :] = over_tokens(branch.astype(f32))
    gattt[...] = jnp.transpose(dot_nt(branch, wout[...])).astype(bf16).reshape(H, HS, TOK)
    moved = Exchange(gattt, rda, asend.at[3], arecv.at[3]).all()
    h2_rows.step()
    send_sib(1, gb, gbs)

    gather.step()
    moved.wait()

    def part_out():
        for copy in to_sib:
            copy.wait()
        left = jnp.concatenate(
            [ratt[pl.ds(core * 8, 8)].reshape(384, TOK), attts[...].reshape(384, TOK)], axis=1
        )
        right = jnp.concatenate([gb[...], gbs[...]], axis=0)
        res = dot(left, right).astype(bf16)
        for k in range(4):
            for t in range(6):
                wop[k, t * 96 : (t + 1) * 96, :] = res[k * 96 : (k + 1) * 96, t * TOK : (t + 1) * TOK]
        quarters.step()

    def grads_down():
        dy_rows.step()
        act_rows.step()
        left = jnp.concatenate([acta[k] for k in range(8)], axis=1)
        res = dot(left, dya[...].reshape(8 * TOK, D)).astype(bf16)
        for t in range(6):
            down_sum.put(res[:, t * TOK : (t + 1) * TOK], t * 384)
        down_sum.step()

    def grads_up():
        h2_rows.step()
        gp_rows.step()
        left = jnp.concatenate([h2ta[k] for k in range(8)], axis=1)
        res = dot(left, gpa[...].reshape(8 * TOK, 384)).astype(bf16)
        for t in range(3):
            up_sum.put(res[:, t * TOK : (t + 1) * TOK], t * D)
        up_sum.step()

    def grads_out():
        out_sum.put(quarters.total(), 0)
        out_sum.put(jnp.zeros((192, TOK), bf16), 576)
        out_sum.step()

    back = Exchange(dqkv, rdq, asend.at[4], arecv.at[4])

    def between(i):
        for half in (0, 1):
            back.one(2 * i + half)
        if i == 7:
            dy_rows.step()
            early.step()
        elif i == 6:
            part_out()
        elif i == 5:
            grads_down()
        elif i == 1:
            down_sum.step()

    attend_backward(offs, rqk, rv, kn, kt, vn, qn, don, rda, ot, lse, dqkv, dk, dv, between)
    gather.step()
    spread = jnp.concatenate([dqkv[k] for k in range(NB)], axis=1)

    def part_head(slot, half):
        res = dot(spread, hall[half].reshape(SEQ, 384)).astype(bf16)
        for u in range(3):
            hpart[slot, u * 144 : (u + 1) * 144, :] = res[:, u * TOK : (u + 1) * TOK]
        hpart[slot, 432:HEAD_ROWS, :] = jnp.zeros((HEAD_ROWS - 432, TOK), bf16)

    part_head(1, other)
    heads.step()
    part_head(0, core)
    h2_rows.step()
    heads.step()
    grads_up()
    back.wait()
    down_sum.step()
    down_all.step()
    dh1t = None
    ones = jnp.ones((8, TOK), bf16)
    for t in range(3):
        grad_t = rdq[:, t * HS : (t + 1) * HS, :].reshape(D, TOK)
        part = dot(wqkv[:, t * D : (t + 1) * D], grad_t)
        dh1t = part if dh1t is None else dh1t + part
        if t != 1:
            row = BQ if t == 0 else BV
            vecl[row : row + 1, :] = dot_nt(ones, grad_t)[0:1, :]
    dh1 = jnp.transpose(dh1t)
    n = n1[...]
    vecl[LN1G : LN1G + 1, :] = over_tokens(dh1 * n)
    vecl[LN1B : LN1B + 1, :] = over_tokens(dh1)
    vecl[4:8, :] = jnp.zeros((4, D), f32)
    early.step()
    late.step()
    grads_out()
    up_sum.step()
    down_all.step()
    late.step()
    out_sum.step()
    heads.step()
    head_all.step()
    up_sum.step()
    up_all.step()
    early.step()
    down_all.step()
    up_all.step()
    head_all.step()
    ig_ref[...] = (gres[...] + norm_back(dh1, n, rs1[...], line(ln1g))).astype(bf16)
    store(ig_ref, ig_h)
    down_all.step()
    out_sum.step()
    out_all.step()
    up_all.step()
    out_all.step()
    late.step()
    head_all.step()
    down_all.step()
    out_all.step()
    up_all.step()
    head_all.step()
    late.step()
    early.step()
    late.step()
    early.step()
    vecs[0] = vbuf[1]
    vecs[1] = lbuf[1]
    store(vecs, vecs_h)
    out_all.step()
    up_all.step()
    head_all.step()
    out_all.step()
    for item in (down_all, up_all, head_all, out_all):
        item.step()
    for item in (down_sum, up_sum, out_sum):
        item.done()
    for copy in stores:
        copy.wait()


VMEM = pl.BlockSpec(memory_space=pltpu.VMEM)
SMEM = pl.BlockSpec(memory_space=pltpu.SMEM)
ANY = pl.BlockSpec(memory_space=pl.ANY)
HBM = pl.BlockSpec(memory_space=pltpu.HBM)


def call_block(offsets, x, dy, vectors, weights):
    v = pltpu.VMEM
    dma = pltpu.SemaphoreType.DMA
    shape = jax.ShapeDtypeStruct
    return pl.pallas_call(
        block_kernel,
        out_shape=(
            v((TOK, D), bf16),
            v((TOK, D), bf16),
            v((2, 4, 4, 4, sum(CUT_DOWN), TOK), bf16),
            v((2, 4, 4, 4, sum(CUT_UP), TOK), bf16),
            v((2, 4, 4, 4, SHARE, TOK), bf16),
            v((2, 4, 4, 4, sum(CUT_OUT), TOK), bf16),
            v((2, VROWS, D), f32),
        ),
        in_specs=[HBM] * 16,
        out_specs=(ANY,) * 7,
        scratch_shapes=[
            pltpu.SMEM((1, 8), jnp.int32), v((TOK, D), bf16), v((TOK, D), bf16),
            *[v((FF if k == 7 else D,), bf16) for k in range(9)],
            v((TOK, D), bf16), v((TOK, D), bf16), v((2, VROWS, D), f32),
            v((D, 3 * D), bf16), v((D, D), bf16), v((D, FF), bf16), v((FF, D), bf16), dma((20,)),
            v((NB, 144, TOK), bf16), v((NB, 144, TOK), bf16),
            v((SEQ, HS), bf16), v((HS, SEQ), bf16),
            v((HS, SEQ), f32), v((1, SEQ), f32), v((NB, HS, TOK), bf16), v((NB, HS, TOK), bf16),
            v((2, 4, 4, TOK, 384), bf16), v((TOK, D), f32), v((TOK, 1), f32),
            v((8, D, TOK), bf16), v((8, TOK, D), bf16),
            v((8, 384, TOK), bf16), v((8, 384, TOK), bf16), v((8, TOK, 384), bf16), v((8, TOK, 384), bf16),
            v((TOK, D), bf16), v((TOK, D), bf16), v((8, HS, TOK), bf16), v((TOK, D), f32),
            v((NB, HS, TOK), bf16), v((NB, HS, TOK), bf16),
            v((HS, SEQ), bf16), v((SEQ, HS), bf16), v((SEQ, HS), bf16), v((SEQ, HS), bf16),
            v((SEQ, HS), f32), v((SEQ, HS), f32),
            v((NB, 144, TOK), bf16), v((NB, 144, TOK), bf16),
            dma((5,)), dma((5,)), dma((2,)), dma((2,)),
            v((2, VROWS, D), f32), v((4, 4, VROWS, D), f32), dma((4,)), dma((4,)),
            v((2, VROWS, D), f32), v((4, 4, VROWS, D), f32), dma((4,)), dma((4,)), dma((3,)),
            dma((3,)), dma((3,)), v((2, HEAD_ROWS, TOK), bf16), v((HEAD_ROWS, TOK), bf16),
            v((HEAD_ROWS, TOK), bf16), v((3, SHARE, TOK), bf16), v((SHARE, TOK), bf16),
            v((4, 576, TOK), bf16), v((3, 576, TOK), bf16),
            *[dma((n,)) for n in (2, 3, 3, 1, 1, 1, 4, 4, 5, 5, 5, 4, 5) for _ in range(2)], dma((4,)),
            *[
                v(lead + (cut, TOK), bf16)
                for cuts in (CUT_DOWN, CUT_UP, CUT_OUT)
                for lead in ((4, 4), (3, 4), (4,), (3,))
                for cut in cuts
            ],
            v((sum(CUT_DOWN), TOK), bf16), v((sum(CUT_UP), TOK), bf16), v((sum(CUT_OUT), TOK), bf16),
        ],
        compiler_params=pltpu.CompilerParams(
            collective_id=1, has_side_effects=True, vmem_limit_bytes=43 * 2**20
        ),
    )(*[pltpu.with_memory_space_constraint(a, pltpu.HBM) for a in (offsets, x, dy, *vectors, *weights)])


def widen_kernel(ag0, ag1, agh, agw, vecs, done_h, ig_h, wqkv, wout, wup, wdown, out_h, grad_h, *rest):
    small_h, small = rest[:9], rest[9:18]
    down_out, up_out, out_out, wideb, vsem, ssem, osem = rest[18:]
    passed = [
        pltpu.make_async_copy(done_h, out_h, vsem.at[0]),
        pltpu.make_async_copy(ig_h, grad_h, vsem.at[1]),
    ]

    def pieces(cuts, base, offset, rows):
        at = 0
        while at < rows:
            n = 0 if offset < 16 * cuts[0] else 1
            inside = offset - n * 16 * cuts[0]
            block, lo = inside // cuts[n], inside % cuts[n]
            size = min(cuts[n] - lo, rows - at)
            yield at, size, block // 4, block % 4, base + n * cuts[0] + lo
            at += size
            offset += size

    def widen(ag, cuts, base, k, offset, rows, dst, col):
        for at, size, z, x, lo in pieces(cuts, base, offset, rows):
            part = ag[k % 2, z, x, k // 2, lo : lo + size, :]
            dst[at : at + size, col * TOK : (col + 1) * TOK] = part.astype(f32)

    def head_rows(core, z, x, lo, rows):
        parts = []
        while rows:
            y, inside = lo // SHARE, lo % SHARE
            size = min(SHARE - inside, rows)
            parts.append(agh[core, z, x, y, inside : inside + size, :])
            lo += size
            rows -= size
        return parts

    down_store = [
        pltpu.make_async_copy(down_out.at[k % 3], wdown.at[pl.ds(k * 384, 384)], osem.at[0, k % 3]) for k in range(8)
    ]
    up_store = [
        pltpu.make_async_copy(up_out.at[k % 3], wup.at[:, pl.ds(k * 384, 384)], osem.at[1, k % 3]) for k in range(8)
    ]
    out_store = [
        pltpu.make_async_copy(
            out_out.at[k % 3], wout.at[pl.ds((k % 2) * 384 + (k // 2) * 96, 96)], osem.at[2, k % 3]
        )
        for k in range(8)
    ]
    head_store = [
        pltpu.make_async_copy(wideb.at[k % 3], wqkv.at[pl.ds(k * TOK, TOK)], osem.at[3, k % 3]) for k in range(6)
    ]
    for copy in passed:
        copy.start()
    for k in range(8):
        if k >= 3:
            down_store[k - 3].wait()
        for t in range(6):
            widen(ag0, CUT_DOWN, 0, k, t * 384, 384, down_out.at[k % 3], t)
        down_store[k].start()
        if k >= 3:
            up_store[k - 3].wait()
            out_store[k - 3].wait()
        for t in range(3):
            widen(ag1, CUT_UP, 0, k, t * D, D, up_out.at[k % 3], t)
        up_store[k].start()
        for t in range(6):
            widen(agw, CUT_OUT, 0, k, t * 96, 96, out_out.at[k % 3], t)
        out_store[k].start()
        if k < 6:
            if k >= 3:
                head_store[k - 3].wait()
            for t in range(3):
                parts = []
                for head in range(H):
                    parts += head_rows(k // 3, head // 4, head % 4, (k % 3) * 144 + t * HS, HS)
                block = jnp.concatenate(parts, axis=0)
                wideb[k % 3, :, t * D : (t + 1) * D] = jnp.transpose(block.astype(f32))
            head_store[k].start()
        if k == 0:
            places = ((1, LN1G), (1, LN1B), (1, BQ), (1, BV), (0, BOUT), (0, LN2G), (0, LN2B), (0, BUP), (0, BDOWN))
            for n, (ref, (group, line)) in enumerate(zip(small, places)):
                if line == BUP:
                    for c in range(4):
                        ref[c * D : (c + 1) * D] = vecs[0, BUP + c : BUP + c + 1, :].reshape(D)
                else:
                    ref[...] = vecs[group, line : line + 1, :].reshape(D)
                copy = pltpu.make_async_copy(ref, small_h[n], ssem.at[n])
                copy.start()
                passed.append(copy)
    for k in range(5, 8):
        down_store[k].wait()
        up_store[k].wait()
        out_store[k].wait()
        head_store[k - 2].wait()
    for copy in passed:
        copy.wait()


def call_widen(*arrays):
    v = pltpu.VMEM
    dma = pltpu.SemaphoreType.DMA
    shape = jax.ShapeDtypeStruct
    return pl.pallas_call(
        widen_kernel,
        out_shape=(
            shape((D, 3 * D), f32), shape((D, D), f32), shape((D, FF), f32), shape((FF, D), f32),
            shape((TOK, D), bf16), shape((TOK, D), bf16),
        ) + tuple(shape((FF if k == 7 else D,), f32) for k in range(9)),
        in_specs=[VMEM] * 5 + [ANY] * 2,
        out_specs=(ANY,) * 15,
        scratch_shapes=[
            *[v((FF if k == 7 else D,), f32) for k in range(9)],
            v((3, 384, D), f32), v((3, D, 384), f32), v((3, 96, D), f32), v((3, TOK, 3 * D), f32),
            dma((2,)), dma((9,)), dma((4, 3)),
        ],
        compiler_params=pltpu.CompilerParams(vmem_limit_bytes=30 * 2**20),
    )(*[pltpu.with_memory_space_constraint(a, pltpu.VMEM) for a in arrays])


def local(
    block_input, offsets, ln1_gain, ln1_bias, w_qkv, bias_query, bias_value, w_out, bias_out,
    ln2_gain, ln2_bias, w_up, bias_up, w_down, bias_down, cotangent,
):
    out, ig, ag0, ag1, agh, agw, vecs = call_block(
        offsets, block_input.reshape(TOK, D), cotangent.reshape(TOK, D),
        (ln1_gain, ln1_bias, bias_query, bias_value, bias_out, ln2_gain, ln2_bias, bias_up, bias_down),
        (w_qkv, w_out, w_up, w_down),
    )
    wide = call_widen(ag0, ag1, agh, agw, vecs, out, ig)
    g_qkv, g_out, g_up, g_down, out, ig = wide[:6]
    s = wide[6:]
    return (
        out.reshape(1, TOK, D), ig.reshape(1, TOK, D),
        s[0], s[1], g_qkv, s[2], s[3], g_out, s[4], s[5], s[6], g_up, s[7], g_down, s[8],
    )


def solution(mesh):
    tokens = P("rows", "seq", None)
    return jax.shard_map(
        local,
        mesh=mesh,
        in_specs=(tokens, P("rows", None)) + (P(),) * 13 + (tokens,),
        out_specs=(tokens, tokens) + (P(),) * 13,
        check_vma=False,
    )
```

```python
import functools

import jax
import jax.numpy as jnp
from jax import lax
from jax.experimental import pallas as pl
from jax.experimental.pallas import tpu as pltpu
from jax.sharding import PartitionSpec as P

MESH = pl.DeviceIdType.MESH
f32 = jnp.float32
bf16 = jnp.bfloat16

D = 768
H = 16
FF = 3072
HS = 48
SEQ = 2048
TOK = 128
NB = 16
QB = 256
CUT_DOWN = (80, 64)
CUT_UP = (80, 64)
CUT_OUT = (32, 16)
SHARE = 112
HEAD_ROWS = 4 * SHARE
WAYS_DOWN = ((0, 48, "xzy"), (48, 48, "zyx"), (96, 48, "yxz"))
WAYS_UP = WAYS_DOWN
WAYS_HEAD = ((0, 48, "xzy"), (48, 32, "zyx"), (80, 32, "yxz"))
WAYS_OUT = ((0, 16, "xzy"), (16, 16, "zyx"), (32, 16, "yxz"))
SCALE = HS**-0.5
SCALE_LOG2E = SCALE * 1.4426950408889634
NEGATIVE = -1e30
EPSILON = 1e-05
GELU_C = 0.7978845608028654
GELU_A = 0.044715

LN1G, LN1B, BQ, BV = 0, 1, 2, 3
BOUT, LN2G, LN2B, BDOWN, BUP = 0, 1, 2, 3, 4
VROWS = 8
WIDEN_SLOTS = 6


def dot(a, b):
    return jnp.dot(a, b, preferred_element_type=f32)


def dot_nt(a, b):
    return lax.dot_general(a, b, (((1,), (1,)), ((), ())), preferred_element_type=f32)


def turned(block):
    return jnp.transpose(block.astype(f32)).astype(bf16)


def coords():
    r = lax.axis_index("rows")
    s = lax.axis_index("seq")
    return lax.div(r, 2), lax.rem(r, 2), lax.div(s, 4), lax.rem(s, 4)


def device_at(y, c, z, x):
    return (y * 2 + c, z * 4 + x)


def remote(src, dst, send, recv, device):
    return pltpu.make_async_remote_copy(
        src_ref=src, dst_ref=dst, send_sem=send, recv_sem=recv, device_id=device, device_id_type=MESH
    )


def seq_peer(d):
    s = lax.axis_index("seq")
    return lax.rem(s + d, 16)


def axis_peer(axis, j):
    y, c, z, x = coords()
    if axis == "y":
        y = lax.rem(y + j, 4)
    elif axis == "z":
        z = lax.rem(z + j, 4)
    else:
        x = lax.rem(x + j, 4)
    return device_at(y, c, z, x)


def axis_place(axis):
    y, c, z, x = coords()
    return {"y": y, "z": z, "x": x}[axis]


def sibling():
    y, c, z, x = coords()
    return device_at(y, 1 - c, z, x)


def greet():
    bar = pltpu.get_barrier_semaphore()
    r = lax.axis_index("rows")
    s = lax.axis_index("seq")
    devices = [(r, seq_peer(d)) for d in range(1, 16)] + [(lax.rem(r + d, 8), s) for d in range(1, 8)]
    for device in devices:
        pl.semaphore_signal(bar, inc=1, device_id=device, device_id_type=MESH)
    return bar, len(devices)


def masked(scores, start, key0, query0, diagonal):
    key = lax.broadcasted_iota(jnp.int32, scores.shape, 0) + key0
    ok = key >= start
    if diagonal:
        query = lax.broadcasted_iota(jnp.int32, scores.shape, 1) + query0
        ok = ok & (key <= query)
    return jnp.where(ok, scores, NEGATIVE)


def segment_starts(offs_ref, query0, count):
    place = lax.broadcasted_iota(jnp.int32, (1, count), 1) + query0
    start = jnp.zeros((1, count), jnp.int32)
    for j in range(8):
        o = offs_ref[0, j]
        start = jnp.where(place >= o, o, start)
    return start


def pair(ref, i, lo, hi):
    return jnp.concatenate([ref[2 * i, lo:hi, :], ref[2 * i + 1, lo:hi, :]], axis=1)


def attend_forward(offs_ref, qk, vals, kn, vt, ot, lse, atts, values_here, after):
    for s in range(NB):
        kn[s * TOK : (s + 1) * TOK, :] = turned(qk[s, 48:96, :])
    values_here()
    for s in range(NB):
        vt[:, s * TOK : (s + 1) * TOK] = vals[s]
    for i in range(SEQ // QB):
        q0 = i * QB
        qt = pair(qk, i, 0, 48)
        start = segment_starts(offs_ref, q0, QB)
        sd = masked(dot(kn[q0 : q0 + QB, :], qt) * SCALE_LOG2E, start, q0, q0, True)
        top = jnp.max(sd, axis=0, keepdims=True)
        if i:
            so = masked(dot(kn[0:q0, :], qt) * SCALE_LOG2E, start, 0, q0, False)
            top = jnp.maximum(top, jnp.max(so, axis=0, keepdims=True))
        pd = jnp.exp2(sd - top)
        total = jnp.sum(pd, axis=0, keepdims=True)
        out = dot(vt[:, q0 : q0 + QB], pd.astype(bf16))
        if i:
            po = jnp.exp2(so - top)
            total = total + jnp.sum(po, axis=0, keepdims=True)
            out = out + dot(vt[:, 0:q0], po.astype(bf16))
        out = out / total
        ot[:, q0 : q0 + QB] = out
        lse[:, q0 : q0 + QB] = top + jnp.log2(total)
        low = out.astype(bf16)
        atts[2 * i] = low[:, 0:TOK]
        atts[2 * i + 1] = low[:, TOK:QB]
        after(2 * i)
        after(2 * i + 1)


def attend_backward(offs_ref, qk, vals, kn, kt, vn, qn, don, dor, ot, lse, dqkv, dk, dv, after):
    for s in range(NB):
        rows = slice(s * TOK, (s + 1) * TOK)
        vn[rows, :] = turned(vals[s])
        qn[rows, :] = turned(qk[s, 0:48, :])
        don[rows, :] = turned(dor[s])
        kt[:, rows] = qk[s, 48:96, :]
    last = SEQ // QB - 1
    for i in reversed(range(SEQ // QB)):
        q0 = i * QB
        qt = pair(qk, i, 0, 48)
        dot_t = pair(dor, i, 0, 48)
        start = segment_starts(offs_ref, q0, QB)
        level = lse[:, q0 : q0 + QB]
        inner = jnp.sum(dot_t.astype(f32) * ot[:, q0 : q0 + QB], axis=0, keepdims=True)
        q_n = qn[q0 : q0 + QB, :]
        do_n = don[q0 : q0 + QB, :]
        dq = None
        for a, b, diagonal in ([(0, q0, False)] if i else []) + [(q0, q0 + QB, True)]:
            scores = masked(dot(kn[a:b, :], qt) * SCALE_LOG2E, start, a, q0, diagonal)
            probs = jnp.exp2(scores - level)
            dp = dot(vn[a:b, :], dot_t)
            ds = (probs * (dp - inner)).astype(bf16)
            dv_part = dot(probs.astype(bf16), do_n)
            dk_part = dot(ds, q_n)
            if i == last:
                dk[a:b, :] = dk_part
                dv[a:b, :] = dv_part
            else:
                dk[a:b, :] += dk_part
                dv[a:b, :] += dv_part
            dq_part = dot(kt[:, a:b], ds)
            dq = dq_part if dq is None else dq + dq_part
        dq = (dq * SCALE).astype(bf16)
        for h in range(2):
            s = 2 * i + h
            rows = slice(s * TOK, (s + 1) * TOK)
            dqkv[s, 0:48, :] = dq[:, h * TOK : (h + 1) * TOK]
            dqkv[s, 48:96, :] = (jnp.transpose(dk[rows, :]) * SCALE).astype(bf16)
            dqkv[s, 96:144, :] = jnp.transpose(dv[rows, :]).astype(bf16)
        after(i)


def norm_parts(values):
    center = values - jnp.mean(values, axis=-1, keepdims=True)
    spread = jnp.mean(center * center, axis=-1, keepdims=True)
    rs = lax.rsqrt(spread + EPSILON)
    return center * rs, rs


def norm_back(grad, n, rs, gain):
    gg = grad * gain
    return rs * (
        gg - jnp.mean(gg, axis=-1, keepdims=True) - n * jnp.mean(gg * n, axis=-1, keepdims=True)
    )


def over_tokens(values):
    return jnp.sum(values, axis=0, keepdims=True)


def arrived(gauge, sem):
    pltpu.make_async_copy(gauge, gauge, sem).wait()


class Steps:
    def __init__(self, send, recv):
        self.send, self.recv = send, recv
        self.sent = []
        self.live = []
        self.at = 0

    def go(self, group, src, dst, device):
        remote(src, dst, self.send.at[group], self.recv.at[group], device).start()

    def expect(self, group, gauge):
        self.live.append((group, gauge))
        self.sent.append((group, gauge))

    def collect(self):
        for group, gauge in self.live:
            arrived(gauge, self.recv.at[group])
        self.live = []

    def step(self):
        self.collect()
        k = self.at
        self.at = k + 1
        self.run(k)

    def done(self):
        for group, gauge in self.sent:
            arrived(gauge, self.send.at[group])
        self.sent = []


class Scatter(Steps):
    def __init__(self, cuts, parts, recv1, mid, recv2, share, send, recv):
        super().__init__(send, recv)
        self.cuts, self.parts, self.recv1, self.mid, self.recv2, self.share = cuts, parts, recv1, mid, recv2, share

    def put(self, value, offset):
        at, rows = 0, value.shape[0]
        while at < rows:
            k = 0 if offset < 16 * self.cuts[0] else 1
            inside = offset - k * 16 * self.cuts[0]
            block, lo = inside // self.cuts[k], inside % self.cuts[k]
            size = min(self.cuts[k] - lo, rows - at)
            self.parts[k][block // 4, block % 4, lo : lo + size, :] = value[at : at + size]
            at += size
            offset += size

    def run(self, k):
        z, x = axis_place("z"), axis_place("x")
        first, second = self.parts
        if k == 0:
            for j in range(1, 4):
                self.go(0, first.at[:, lax.rem(x + j, 4)], self.recv1[0].at[j - 1], axis_peer("x", j))
                self.go(1, second.at[lax.rem(z + j, 4)], self.recv1[1].at[j - 1], axis_peer("z", j))
            for n in range(2):
                self.expect(n, self.recv1[n])
        elif k == 1:
            for n, mine in enumerate((first[:, x], second[z])):
                acc = mine.astype(f32)
                for j in range(3):
                    acc = acc + self.recv1[n][j].astype(f32)
                self.mid[n][...] = acc.astype(bf16)
            for j in range(1, 4):
                self.go(2, self.mid[0].at[lax.rem(z + j, 4)], self.recv2[0].at[j - 1], axis_peer("z", j))
                self.go(3, self.mid[1].at[lax.rem(x + j, 4)], self.recv2[1].at[j - 1], axis_peer("x", j))
            for n in range(2):
                self.expect(2 + n, self.recv2[n])
        else:
            lo = 0
            for n, here in enumerate((z, x)):
                acc = self.mid[n][here].astype(f32)
                for j in range(3):
                    acc = acc + self.recv2[n][j].astype(f32)
                self.share[lo : lo + self.cuts[n], :] = acc.astype(bf16)
                lo += self.cuts[n]


class Spread(Steps):
    def __init__(self, share, ag, ways, send, recv, own):
        super().__init__(send, recv)
        self.share, self.ag, self.ways, self.own = share, ag, ways, own

    def spot(self, lo, size, whole, **at):
        core = lax.rem(lax.axis_index("rows"), 2)
        index = [at[a] if a in at else slice(None) if a in whole else axis_place(a) for a in "zxy"]
        return self.ag.at[(core, *index, pl.ds(lo, size))]

    def pass_on(self, spot):
        self.go(4, spot, spot, sibling())

    def run(self, k):
        ag = self.ag
        if k == 1:
            self.kept.wait()
        for lo, size, order in self.ways:
            last = order[2]
            here = axis_place(last)
            if k == 0:
                for j in range(1, 4):
                    self.go(0, self.share.at[pl.ds(lo, size)], self.spot(lo, size, ""), axis_peer(order[0], j))
            elif k == 1:
                spot = self.spot(lo, size, order[0])
                for j in range(1, 4):
                    self.go(1, spot, spot, axis_peer(order[1], j))
            elif k == 2:
                spot = self.spot(lo, size, order[:2])
                self.go(2, spot, spot, axis_peer(last, 1))
                self.go(2, spot, spot, axis_peer(last, 3))
                self.pass_on(spot)
            elif k == 3:
                before, after = lax.rem(here + 3, 4), lax.rem(here + 1, 4)
                cut = "x" if last == "z" else "z"
                low = self.spot(lo, size, order[:2], **{last: before, cut: pl.ds(0, 2)})
                high = self.spot(lo, size, order[:2], **{last: after, cut: pl.ds(2, 2)})
                self.go(3, low, low, axis_peer(last, 1))
                self.go(3, high, high, axis_peer(last, 3))
                self.pass_on(self.spot(lo, size, order[:2], **{last: before}))
                self.pass_on(self.spot(lo, size, order[:2], **{last: after}))
            elif k == 4:
                self.pass_on(self.spot(lo, size, order[:2], **{last: lax.rem(here + 2, 4)}))
        three = pl.ds(0, 3)
        if k == 0:
            self.kept = pltpu.make_async_copy(self.share, self.spot(0, self.share.shape[0], ""), self.own)
            self.kept.start()
            self.expect(0, ag.at[0, 0, 0, three])
        elif k == 1:
            self.expect(1, ag.at[0, 0, three])
        elif k == 2:
            self.expect(2, ag.at[0, pl.ds(0, 2)])
        elif k == 3:
            self.expect(3, ag.at[0, 0])
        elif k == 4:
            self.expect(4, ag.at[0])
        else:
            self.done()


class RowSwap(Steps):
    def __init__(self, src, dst, send, recv):
        super().__init__(send, recv)
        self.src, self.dst = src, dst

    def run(self, k):
        r, s = lax.axis_index("rows"), lax.axis_index("seq")
        if k == 0:
            for d in range(1, 8):
                peer = lax.rem(r + d, 8)
                self.go(0, self.src.at[peer], self.dst.at[r], (peer, s))
            self.dst[r] = self.src[r]
            self.expect(0, self.dst.at[pl.ds(0, 7)])
        else:
            self.done()


class RowGather(Steps):
    def __init__(self, dst, send, recv):
        super().__init__(send, recv)
        self.dst = dst

    def run(self, k):
        r = lax.axis_index("rows")
        dst = self.dst
        half = dst.shape[1] // 2
        before, after = lax.rem(r + 6, 8), lax.rem(r + 2, 8)
        if k == 0:
            for device in (axis_peer("y", 1), axis_peer("y", 3)):
                self.go(0, dst.at[r], dst.at[r], device)
            self.go(2, dst.at[r], dst.at[r], sibling())
            self.expect(0, dst.at[pl.ds(0, 2)])
        elif k == 1:
            low, high = dst.at[before, pl.ds(0, half)], dst.at[after, pl.ds(half, half)]
            self.go(1, low, low, axis_peer("y", 1))
            self.go(1, high, high, axis_peer("y", 3))
            for spot in (dst.at[before], dst.at[after]):
                self.go(2, spot, spot, sibling())
            self.expect(1, dst.at[0])
        elif k == 2:
            spot = dst.at[lax.rem(r + 4, 8)]
            self.go(2, spot, spot, sibling())
            self.expect(2, dst.at[pl.ds(0, 4)])
        else:
            self.done()


class Exchange:
    def __init__(self, src, dst, send, recv):
        self.src, self.dst, self.send, self.recv = src, dst, send, recv

    def all(self):
        r = lax.axis_index("rows")
        s = lax.axis_index("seq")
        for d in range(1, 16):
            peer = seq_peer(d)
            remote(self.src.at[peer], self.dst.at[s], self.send, self.recv, (r, peer)).start()
        self.dst[s] = self.src[s]
        return self

    def one(self, block):
        r = lax.axis_index("rows")
        s = lax.axis_index("seq")

        @pl.when(s != block)
        def _():
            remote(self.src.at[block], self.dst.at[s], self.send, self.recv, (r, block)).start()

        @pl.when(s == block)
        def _():
            self.dst[s] = self.src[block]

    def wait(self):
        gauge = self.dst.at[pl.ds(0, 15)]
        arrived(gauge, self.recv)
        arrived(gauge, self.send)


class Gather(Steps):
    def __init__(self, hall, send, recv):
        super().__init__(send, recv)
        self.hall = hall

    def run(self, k):
        z, x = axis_place("z"), axis_place("x")
        hall = self.hall
        if k == 0:
            for j in range(1, 4):
                self.go(0, hall.at[0, z, x], hall.at[0, z, x], axis_peer("x", j))
                self.go(0, hall.at[1, z, x], hall.at[1, z, x], axis_peer("z", j))
            self.expect(0, hall.at[:, pl.ds(0, 3), 0])
        elif k == 1:
            for j in (1, 3):
                self.go(1, hall.at[0, z], hall.at[0, z], axis_peer("z", j))
                self.go(1, hall.at[1, :, x], hall.at[1, :, x], axis_peer("x", j))
            self.expect(1, hall.at[0])
        elif k == 2:
            two, low = pl.ds(2, 2), pl.ds(0, 2)
            for spot, axis, j in (
                (hall.at[0, lax.rem(z + 3, 4), low], "z", 1),
                (hall.at[0, lax.rem(z + 1, 4), two], "z", 3),
                (hall.at[1, low, lax.rem(x + 3, 4)], "x", 1),
                (hall.at[1, two, lax.rem(x + 1, 4)], "x", 3),
            ):
                self.go(2, spot, spot, axis_peer(axis, j))
            self.expect(2, hall.at[:, :, 0])
        else:
            self.done()


class Heads(Steps):
    def __init__(self, part, sib_recv, both, y_recv, share, send, recv):
        super().__init__(send, recv)
        self.part, self.sib_recv, self.both, self.y_recv, self.share = part, sib_recv, both, y_recv, share

    def run(self, k):
        y = axis_place("y")
        if k == 0:
            self.go(0, self.part.at[1], self.sib_recv, sibling())
            self.expect(0, self.sib_recv)
        elif k == 1:
            self.both[...] = (self.part[0].astype(f32) + self.sib_recv[...].astype(f32)).astype(bf16)
            for j in range(1, 4):
                there = lax.rem(y + j, 4)
                self.go(1, self.both.at[pl.ds(there * SHARE, SHARE)], self.y_recv.at[j - 1], axis_peer("y", j))
            self.expect(1, self.y_recv)
        else:
            acc = self.both[pl.ds(y * SHARE, SHARE)].astype(f32)
            for j in range(3):
                acc = acc + self.y_recv[j].astype(f32)
            self.share[0:SHARE, :] = acc.astype(bf16)
            self.done()


class Quarters(Steps):
    def __init__(self, part, y_recv, send, recv):
        super().__init__(send, recv)
        self.part, self.y_recv = part, y_recv

    def run(self, k):
        y = axis_place("y")
        if k == 0:
            for j in range(1, 4):
                self.go(0, self.part.at[lax.rem(y + j, 4)], self.y_recv.at[j - 1], axis_peer("y", j))
            self.expect(0, self.y_recv)
        else:
            acc = self.part[y].astype(f32)
            for j in range(3):
                acc = acc + self.y_recv[j].astype(f32)
            self.done()
            return acc.astype(bf16)

    def total(self):
        self.collect()
        return self.run(1)


class Vectors:
    def __init__(self, buf, slots, send_sem, recv_sem):
        self.buf, self.slots, self.send_sem, self.recv_sem = buf, slots, send_sem, recv_sem
        self.at = 0

    def step(self):
        k = self.at
        self.at = k + 1
        if k == 0:
            value = self.buf[0]
        else:
            gauge = self.slots.at[k - 1, pl.ds(0, 3 if k < 4 else 1)]
            arrived(gauge, self.recv_sem.at[k - 1])
            arrived(gauge, self.send_sem.at[k - 1])
            value = self.slots[k - 1, 0]
            for j in range(1, 4 if k < 4 else 2):
                value = value + self.slots[k - 1, j]
        if k == 4:
            self.buf[1] = value
            return
        here = axis_place("xyz"[k]) if k < 3 else lax.rem(lax.axis_index("rows"), 2)
        devices = [axis_peer("xyz"[k], j) for j in range(1, 4)] if k < 3 else [sibling()]
        self.slots[k, here] = value
        for device in devices:
            spot = self.slots.at[k, here]
            remote(spot, spot, self.send_sem.at[k], self.recv_sem.at[k], device).start()


def block_kernel(
    offs_h, x_h, dy_h, ln1g_h, ln1b_h, bq_h, bv_h, bout_h, ln2g_h, ln2b_h, bup_h, bdown_h,
    wqkv_h, wout_h, wup_h, wdown_h,
    out_h, ig_h, ag0, ag1, agh, agw, vecs_h,
    offs, x_ref, dy_ref, ln1g, ln1b, bq, bv, bout, ln2g, ln2b, bup, bdown,
    out_ref, ig_ref, vecs,
    wqkv, wout, wup, wdown, wsem,
    qkt, vals, rqk, rv, kn, vt, ot, lse, atts, ratt,
    hall, n1, rs1, h2ta, dya, actt, acta, gp, gpa, gb, gbs, attts, gres,
    gattt, rda, kt, vn, qn, don, dk, dv, dqkv, rdq,
    asend, arecv, ssend, srecv,
    *rest,
):
    (vbuf, vrecv, vsend, vrsem, lbuf, lrecv, lsend, lrsem, osem,
     hsend, hrecv, hpart, hsib, hboth, hy, hmine, wop, wor) = rest[:18]
    rest = rest[18:]
    sems = [rest[2 * k : 2 * k + 2] for k in range(13)]
    own, rest = rest[26], rest[27:]
    down_parts, down_recv1, down_mid, down_recv2 = [rest[2 * k : 2 * k + 2] for k in range(4)]
    up_parts, up_recv1, up_mid, up_recv2 = [rest[8 + 2 * k : 10 + 2 * k] for k in range(4)]
    out_parts, out_recv1, out_mid, out_recv2 = [rest[16 + 2 * k : 18 + 2 * k] for k in range(4)]
    down_share, up_share, out_share = rest[24:]
    loads = {}

    def load(name, src, dst):
        copy = pltpu.make_async_copy(src, dst, wsem.at[len(loads)])
        copy.start()
        loads[name] = copy

    load("x", x_h, x_ref)
    load("ln1g", ln1g_h, ln1g)
    load("ln1b", ln1b_h, ln1b)
    for t in (1, 0, 2):
        cols = pl.ds(t * D, D)
        load(f"qkv{t}", wqkv_h.at[:, cols], wqkv.at[:, cols])
    load("bq", bq_h, bq)
    load("bv", bv_h, bv)
    load("dy", dy_h, dy_ref)
    load("offs", offs_h, offs)
    stores = []

    def ready(*names):
        for name in names:
            loads[name].wait()

    def store(src, dst):
        copy = pltpu.make_async_copy(src, dst, osem.at[len(stores)])
        copy.start()
        stores.append(copy)

    bar, count = greet()
    vecg = vbuf.at[0]
    vecl = lbuf.at[0]
    early = Vectors(vbuf, vrecv, vsend, vrsem)
    late = Vectors(lbuf, lrecv, lsend, lrsem)
    gather = Gather(hall, hsend, hrecv)
    heads = Heads(hpart, hsib, hboth, hy, hmine, *sems[0])
    dy_rows = RowGather(dya, *sems[1])
    h2_rows = RowGather(h2ta, *sems[2])
    act_rows = RowSwap(actt, acta, *sems[3])
    gp_rows = RowSwap(gp, gpa, *sems[4])
    quarters = Quarters(wop, wor, *sems[5])
    down_sum = Scatter(CUT_DOWN, down_parts, down_recv1, down_mid, down_recv2, down_share, *sems[6])
    up_sum = Scatter(CUT_UP, up_parts, up_recv1, up_mid, up_recv2, up_share, *sems[7])
    down_all = Spread(down_share, ag0, WAYS_DOWN, *sems[8], own.at[0])
    up_all = Spread(up_share, ag1, WAYS_UP, *sems[9], own.at[1])
    head_all = Spread(hmine, agh, WAYS_HEAD, *sems[10], own.at[2])
    out_all = Spread(out_share, agw, WAYS_OUT, *sems[12], own.at[3])
    out_sum = Scatter(CUT_OUT, out_parts, out_recv1, out_mid, out_recv2, out_share, *sems[11])
    row = lax.axis_index("rows")

    def line(ref):
        return ref[...].astype(f32).reshape(1, D)

    core = lax.rem(lax.axis_index("rows"), 2)
    other = 1 - core
    sib = sibling()
    to_sib = []

    def send_sib(n, src, dst):
        copy = remote(src, dst, ssend.at[n], srecv.at[n], sib)
        copy.start()
        to_sib.append(copy)

    ready("x", "ln1g", "ln1b")
    x = x_ref[...].astype(f32)
    n, rs = norm_parts(x)
    n1[...] = n
    rs1[...] = rs
    h1f = n * line(ln1g) + line(ln1b)
    h1 = h1f.astype(bf16)
    for half in range(2):
        hall[half, axis_place("z"), axis_place("x")] = h1[:, half * 384 : (half + 1) * 384]
    for t in (1, 0, 2):
        ready(f"qkv{t}")
        y = dot(h1, wqkv[:, t * D : (t + 1) * D])
        if t == 0:
            ready("bq")
            y = y + line(bq)
        if t == 2:
            ready("bv")
            y = y + line(bv)
        low = jnp.transpose(y).astype(bf16).reshape(H, HS, TOK)
        if t < 2:
            qkt[:, t * HS : (t + 1) * HS, :] = low
        else:
            vals[...] = low
        if t == 0:
            pl.semaphore_wait(bar, count)
            moved = [Exchange(qkt, rqk, asend.at[0], arecv.at[0]).all()]
    moved.append(Exchange(vals, rv, asend.at[1], arecv.at[1]).all())
    load("out", wout_h, wout)
    for name, src, dst in (
        ("bout", bout_h, bout), ("ln2g", ln2g_h, ln2g), ("ln2b", ln2b_h, ln2b),
        ("bup", bup_h, bup), ("bdown", bdown_h, bdown),
    ):
        load(name, src, dst)
    load("up", wup_h, wup)
    load("down", wdown_h, wdown)
    ready("dy", "offs")
    dya[row] = dy_ref[...]
    dy_rows.step()
    moved[0].wait()
    gather.step()

    attended = Exchange(atts, ratt, asend.at[2], arecv.at[2])
    attend_forward(
        offs, rqk, rv, kn, vt, ot, lse, atts,
        moved[1].wait, attended.one,
    )
    ready("out", "bout", "ln2g", "ln2b", "bup", "bdown", "up", "down")
    gather.step()
    attended.wait()
    dy_rows.step()

    att = jnp.transpose(ratt[...].reshape(D, TOK).astype(f32)).astype(bf16)
    send_sib(0, ratt.at[pl.ds(other * 8, 8)], attts)
    resid = x_ref[...].astype(f32) + dot(att, wout[...]) + line(bout)
    n2, rs2 = norm_parts(resid)
    h2f = n2 * line(ln2g) + line(ln2b)
    h2 = h2f.astype(bf16)
    h2ta[row] = jnp.transpose(h2f).astype(bf16)
    h2_rows.step()
    dy = dy_ref[...]
    down = None
    dh2 = None
    for c in range(4):
        cols = slice(c * D, (c + 1) * D)
        pre = dot(h2, wup[:, cols]) + bup[cols].astype(f32).reshape(1, D)
        square = pre * pre
        t = jnp.tanh(GELU_C * (pre + GELU_A * (square * pre)))
        act = 0.5 * pre * (1.0 + t)
        slope = 0.5 * (1.0 + t) + (0.5 * GELU_C) * pre * (1.0 - t * t) * (1.0 + (3.0 * GELU_A) * square)
        part = dot(act.astype(bf16), wdown[cols, :])
        down = part if down is None else down + part
        act_t = jnp.transpose(act).astype(bf16)
        actt[2 * c] = act_t[0:384]
        actt[2 * c + 1] = act_t[384:768]
        gpre = (dot_nt(dy, wdown[cols, :]) * slope).astype(bf16)
        gp[2 * c] = gpre[:, 0:384]
        gp[2 * c + 1] = gpre[:, 384:768]
        vecg[BUP + c : BUP + c + 1, :] = over_tokens(gpre.astype(f32))
        part = dot_nt(gpre, wup[:, cols])
        dh2 = part if dh2 is None else dh2 + part
    act_rows.step()
    gp_rows.step()
    out_ref[...] = (resid + down + line(bdown)).astype(bf16)
    store(out_ref, out_h)
    vecg[BDOWN : BDOWN + 1, :] = over_tokens(dy.astype(f32))
    vecg[LN2G : LN2G + 1, :] = over_tokens(dh2 * n2)
    vecg[LN2B : LN2B + 1, :] = over_tokens(dh2)
    grad = dy.astype(f32) + norm_back(dh2, n2, rs2, line(ln2g))
    gres[...] = grad
    branch = grad.astype(bf16)
    gb[...] = branch
    vecg[BOUT : BOUT + 1, :] = over_tokens(branch.astype(f32))
    gattt[...] = jnp.transpose(dot_nt(branch, wout[...])).astype(bf16).reshape(H, HS, TOK)
    moved = Exchange(gattt, rda, asend.at[3], arecv.at[3]).all()
    h2_rows.step()
    send_sib(1, gb, gbs)

    gather.step()
    moved.wait()

    def part_out():
        for copy in to_sib:
            copy.wait()
        left = jnp.concatenate(
            [ratt[pl.ds(core * 8, 8)].reshape(384, TOK), attts[...].reshape(384, TOK)], axis=1
        )
        right = jnp.concatenate([gb[...], gbs[...]], axis=0)
        res = dot(left, right).astype(bf16)
        for k in range(4):
            for t in range(6):
                wop[k, t * 96 : (t + 1) * 96, :] = res[k * 96 : (k + 1) * 96, t * TOK : (t + 1) * TOK]
        quarters.step()

    def grads_down():
        dy_rows.step()
        act_rows.step()
        left = jnp.concatenate([acta[k] for k in range(8)], axis=1)
        res = dot(left, dya[...].reshape(8 * TOK, D)).astype(bf16)
        for t in range(6):
            down_sum.put(res[:, t * TOK : (t + 1) * TOK], t * 384)
        down_sum.step()

    def grads_up():
        h2_rows.step()
        gp_rows.step()
        left = jnp.concatenate([h2ta[k] for k in range(8)], axis=1)
        res = dot(left, gpa[...].reshape(8 * TOK, 384)).astype(bf16)
        for t in range(3):
            up_sum.put(res[:, t * TOK : (t + 1) * TOK], t * D)
        up_sum.step()

    def grads_out():
        out_sum.put(quarters.total(), 0)
        out_sum.put(jnp.zeros((192, TOK), bf16), 576)
        out_sum.step()

    back = Exchange(dqkv, rdq, asend.at[4], arecv.at[4])

    def between(i):
        for half in (0, 1):
            back.one(2 * i + half)
        if i == 7:
            dy_rows.step()
            early.step()
        elif i == 6:
            part_out()
        elif i == 5:
            grads_down()
        elif i == 1:
            down_sum.step()

    attend_backward(offs, rqk, rv, kn, kt, vn, qn, don, rda, ot, lse, dqkv, dk, dv, between)
    gather.step()
    spread = jnp.concatenate([dqkv[k] for k in range(NB)], axis=1)

    def part_head(slot, half):
        res = dot(spread, hall[half].reshape(SEQ, 384)).astype(bf16)
        for u in range(3):
            hpart[slot, u * 144 : (u + 1) * 144, :] = res[:, u * TOK : (u + 1) * TOK]
        hpart[slot, 432:HEAD_ROWS, :] = jnp.zeros((HEAD_ROWS - 432, TOK), bf16)

    part_head(1, other)
    heads.step()
    part_head(0, core)
    h2_rows.step()
    heads.step()
    grads_up()
    back.wait()
    down_sum.step()
    down_all.step()
    dh1t = None
    ones = jnp.ones((8, TOK), bf16)
    for t in range(3):
        grad_t = rdq[:, t * HS : (t + 1) * HS, :].reshape(D, TOK)
        part = dot(wqkv[:, t * D : (t + 1) * D], grad_t)
        dh1t = part if dh1t is None else dh1t + part
        if t != 1:
            row = BQ if t == 0 else BV
            vecl[row : row + 1, :] = dot_nt(ones, grad_t)[0:1, :]
    dh1 = jnp.transpose(dh1t)
    n = n1[...]
    vecl[LN1G : LN1G + 1, :] = over_tokens(dh1 * n)
    vecl[LN1B : LN1B + 1, :] = over_tokens(dh1)
    vecl[4:8, :] = jnp.zeros((4, D), f32)
    early.step()
    late.step()
    grads_out()
    up_sum.step()
    down_all.step()
    late.step()
    out_sum.step()
    heads.step()
    head_all.step()
    up_sum.step()
    up_all.step()
    early.step()
    down_all.step()
    up_all.step()
    head_all.step()
    ig_ref[...] = (gres[...] + norm_back(dh1, n, rs1[...], line(ln1g))).astype(bf16)
    store(ig_ref, ig_h)
    down_all.step()
    out_sum.step()
    out_all.step()
    up_all.step()
    out_all.step()
    late.step()
    head_all.step()
    down_all.step()
    out_all.step()
    up_all.step()
    head_all.step()
    late.step()
    early.step()
    late.step()
    early.step()
    vecs[0] = vbuf[1]
    vecs[1] = lbuf[1]
    store(vecs, vecs_h)
    out_all.step()
    up_all.step()
    head_all.step()
    out_all.step()
    for item in (down_all, up_all, head_all, out_all):
        item.step()
    for item in (down_sum, up_sum, out_sum):
        item.done()
    for copy in stores:
        copy.wait()


VMEM = pl.BlockSpec(memory_space=pltpu.VMEM)
SMEM = pl.BlockSpec(memory_space=pltpu.SMEM)
ANY = pl.BlockSpec(memory_space=pl.ANY)
HBM = pl.BlockSpec(memory_space=pltpu.HBM)


def call_block(offsets, x, dy, vectors, weights):
    v = pltpu.VMEM
    dma = pltpu.SemaphoreType.DMA
    shape = jax.ShapeDtypeStruct
    return pl.pallas_call(
        block_kernel,
        out_shape=(
            v((TOK, D), bf16),
            v((TOK, D), bf16),
            v((2, 4, 4, 4, sum(CUT_DOWN), TOK), bf16),
            v((2, 4, 4, 4, sum(CUT_UP), TOK), bf16),
            v((2, 4, 4, 4, SHARE, TOK), bf16),
            v((2, 4, 4, 4, sum(CUT_OUT), TOK), bf16),
            v((2, VROWS, D), f32),
        ),
        in_specs=[HBM] * 16,
        out_specs=(ANY,) * 7,
        scratch_shapes=[
            pltpu.SMEM((1, 8), jnp.int32), v((TOK, D), bf16), v((TOK, D), bf16),
            *[v((FF if k == 7 else D,), bf16) for k in range(9)],
            v((TOK, D), bf16), v((TOK, D), bf16), v((2, VROWS, D), f32),
            v((D, 3 * D), bf16), v((D, D), bf16), v((D, FF), bf16), v((FF, D), bf16), dma((20,)),
            v((NB, 96, TOK), bf16), v((NB, HS, TOK), bf16), v((NB, 96, TOK), bf16), v((NB, HS, TOK), bf16),
            v((SEQ, HS), bf16), v((HS, SEQ), bf16),
            v((HS, SEQ), f32), v((1, SEQ), f32), v((NB, HS, TOK), bf16), v((NB, HS, TOK), bf16),
            v((2, 4, 4, TOK, 384), bf16), v((TOK, D), f32), v((TOK, 1), f32),
            v((8, D, TOK), bf16), v((8, TOK, D), bf16),
            v((8, 384, TOK), bf16), v((8, 384, TOK), bf16), v((8, TOK, 384), bf16), v((8, TOK, 384), bf16),
            v((TOK, D), bf16), v((TOK, D), bf16), v((8, HS, TOK), bf16), v((TOK, D), f32),
            v((NB, HS, TOK), bf16), v((NB, HS, TOK), bf16),
            v((HS, SEQ), bf16), v((SEQ, HS), bf16), v((SEQ, HS), bf16), v((SEQ, HS), bf16),
            v((SEQ, HS), f32), v((SEQ, HS), f32),
            v((NB, 144, TOK), bf16), v((NB, 144, TOK), bf16),
            dma((5,)), dma((5,)), dma((2,)), dma((2,)),
            v((2, VROWS, D), f32), v((4, 4, VROWS, D), f32), dma((4,)), dma((4,)),
            v((2, VROWS, D), f32), v((4, 4, VROWS, D), f32), dma((4,)), dma((4,)), dma((3,)),
            dma((3,)), dma((3,)), v((2, HEAD_ROWS, TOK), bf16), v((HEAD_ROWS, TOK), bf16),
            v((HEAD_ROWS, TOK), bf16), v((3, SHARE, TOK), bf16), v((SHARE, TOK), bf16),
            v((4, 576, TOK), bf16), v((3, 576, TOK), bf16),
            *[dma((n,)) for n in (2, 3, 3, 1, 1, 1, 4, 4, 5, 5, 5, 4, 5) for _ in range(2)], dma((4,)),
            *[
                v(lead + (cut, TOK), bf16)
                for cuts in (CUT_DOWN, CUT_UP, CUT_OUT)
                for lead in ((4, 4), (3, 4), (4,), (3,))
                for cut in cuts
            ],
            v((sum(CUT_DOWN), TOK), bf16), v((sum(CUT_UP), TOK), bf16), v((sum(CUT_OUT), TOK), bf16),
        ],
        compiler_params=pltpu.CompilerParams(
            collective_id=1, has_side_effects=True, vmem_limit_bytes=43 * 2**20
        ),
    )(*[pltpu.with_memory_space_constraint(a, pltpu.HBM) for a in (offsets, x, dy, *vectors, *weights)])


def widen_kernel(ag0, ag1, agh, agw, vecs, done_h, ig_h, wqkv, wout, wup, wdown, out_h, grad_h, *rest):
    small_h, small = rest[:9], rest[9:18]
    down_out, up_out, out_out, wideb, vsem, ssem, osem = rest[18:]
    passed = [
        pltpu.make_async_copy(done_h, out_h, vsem.at[0]),
        pltpu.make_async_copy(ig_h, grad_h, vsem.at[1]),
    ]

    def pieces(cuts, base, offset, rows):
        at = 0
        while at < rows:
            n = 0 if offset < 16 * cuts[0] else 1
            inside = offset - n * 16 * cuts[0]
            block, lo = inside // cuts[n], inside % cuts[n]
            size = min(cuts[n] - lo, rows - at)
            yield at, size, block // 4, block % 4, base + n * cuts[0] + lo
            at += size
            offset += size

    def widen(ag, cuts, base, k, offset, rows, dst, col):
        for at, size, z, x, lo in pieces(cuts, base, offset, rows):
            part = ag[k % 2, z, x, k // 2, lo : lo + size, :]
            dst[at : at + size, col * TOK : (col + 1) * TOK] = part.astype(f32)

    def head_rows(core, z, x, lo, rows):
        parts = []
        while rows:
            y, inside = lo // SHARE, lo % SHARE
            size = min(SHARE - inside, rows)
            parts.append(agh[core, z, x, y, inside : inside + size, :])
            lo += size
            rows -= size
        return parts

    down_store = [
        pltpu.make_async_copy(down_out.at[k % 3], wdown.at[pl.ds(k * 384, 384)], osem.at[0, k % 3]) for k in range(8)
    ]
    up_store = [
        pltpu.make_async_copy(up_out.at[k % 3], wup.at[:, pl.ds(k * 384, 384)], osem.at[1, k % 3]) for k in range(8)
    ]
    out_store = [
        pltpu.make_async_copy(
            out_out.at[k % 3], wout.at[pl.ds((k % 2) * 384 + (k // 2) * 96, 96)], osem.at[2, k % 3]
        )
        for k in range(8)
    ]
    head_store = [
        pltpu.make_async_copy(wideb.at[k % 3], wqkv.at[pl.ds(k * TOK, TOK)], osem.at[3, k % 3]) for k in range(6)
    ]
    for copy in passed:
        copy.start()
    for k in range(8):
        if k >= 3:
            down_store[k - 3].wait()
        for t in range(6):
            widen(ag0, CUT_DOWN, 0, k, t * 384, 384, down_out.at[k % 3], t)
        down_store[k].start()
        if k >= 3:
            up_store[k - 3].wait()
            out_store[k - 3].wait()
        for t in range(3):
            widen(ag1, CUT_UP, 0, k, t * D, D, up_out.at[k % 3], t)
        up_store[k].start()
        for t in range(6):
            widen(agw, CUT_OUT, 0, k, t * 96, 96, out_out.at[k % 3], t)
        out_store[k].start()
        if k < 6:
            if k >= 3:
                head_store[k - 3].wait()
            for t in range(3):
                parts = []
                for head in range(H):
                    parts += head_rows(k // 3, head // 4, head % 4, (k % 3) * 144 + t * HS, HS)
                block = jnp.concatenate(parts, axis=0)
                wideb[k % 3, :, t * D : (t + 1) * D] = jnp.transpose(block.astype(f32))
            head_store[k].start()
        if k == 0:
            places = ((1, LN1G), (1, LN1B), (1, BQ), (1, BV), (0, BOUT), (0, LN2G), (0, LN2B), (0, BUP), (0, BDOWN))
            for n, (ref, (group, line)) in enumerate(zip(small, places)):
                if line == BUP:
                    for c in range(4):
                        ref[c * D : (c + 1) * D] = vecs[0, BUP + c : BUP + c + 1, :].reshape(D)
                else:
                    ref[...] = vecs[group, line : line + 1, :].reshape(D)
                copy = pltpu.make_async_copy(ref, small_h[n], ssem.at[n])
                copy.start()
                passed.append(copy)
    for k in range(5, 8):
        down_store[k].wait()
        up_store[k].wait()
        out_store[k].wait()
        head_store[k - 2].wait()
    for copy in passed:
        copy.wait()


def call_widen(*arrays):
    v = pltpu.VMEM
    dma = pltpu.SemaphoreType.DMA
    shape = jax.ShapeDtypeStruct
    return pl.pallas_call(
        widen_kernel,
        out_shape=(
            shape((D, 3 * D), f32), shape((D, D), f32), shape((D, FF), f32), shape((FF, D), f32),
            shape((TOK, D), bf16), shape((TOK, D), bf16),
        ) + tuple(shape((FF if k == 7 else D,), f32) for k in range(9)),
        in_specs=[VMEM] * 5 + [ANY] * 2,
        out_specs=(ANY,) * 15,
        scratch_shapes=[
            *[v((FF if k == 7 else D,), f32) for k in range(9)],
            v((3, 384, D), f32), v((3, D, 384), f32), v((3, 96, D), f32), v((3, TOK, 3 * D), f32),
            dma((2,)), dma((9,)), dma((4, 3)),
        ],
        compiler_params=pltpu.CompilerParams(vmem_limit_bytes=30 * 2**20),
    )(*[pltpu.with_memory_space_constraint(a, pltpu.VMEM) for a in arrays])


def local(
    block_input, offsets, ln1_gain, ln1_bias, w_qkv, bias_query, bias_value, w_out, bias_out,
    ln2_gain, ln2_bias, w_up, bias_up, w_down, bias_down, cotangent,
):
    out, ig, ag0, ag1, agh, agw, vecs = call_block(
        offsets, block_input.reshape(TOK, D), cotangent.reshape(TOK, D),
        (ln1_gain, ln1_bias, bias_query, bias_value, bias_out, ln2_gain, ln2_bias, bias_up, bias_down),
        (w_qkv, w_out, w_up, w_down),
    )
    wide = call_widen(ag0, ag1, agh, agw, vecs, out, ig)
    g_qkv, g_out, g_up, g_down, out, ig = wide[:6]
    s = wide[6:]
    return (
        out.reshape(1, TOK, D), ig.reshape(1, TOK, D),
        s[0], s[1], g_qkv, s[2], s[3], g_out, s[4], s[5], s[6], g_up, s[7], g_down, s[8],
    )


def solution(mesh):
    tokens = P("rows", "seq", None)
    return jax.shard_map(
        local,
        mesh=mesh,
        in_specs=(tokens, P("rows", None)) + (P(),) * 13 + (tokens,),
        out_specs=(tokens, tokens) + (P(),) * 13,
        check_vma=False,
    )
```

```python
import functools

import jax
import jax.numpy as jnp
from jax import lax
from jax.experimental import pallas as pl
from jax.experimental.pallas import tpu as pltpu
from jax.sharding import PartitionSpec as P

MESH = pl.DeviceIdType.MESH
f32 = jnp.float32
bf16 = jnp.bfloat16

D = 768
H = 16
FF = 3072
HS = 48
SEQ = 2048
TOK = 128
NB = 16
QB = 256
CUT_DOWN = (80, 64)
CUT_UP = (80, 64)
CUT_OUT = (32, 16)
SHARE = 112
HEAD_ROWS = 4 * SHARE
WAYS_DOWN = ((0, 48, "xzy"), (48, 48, "zyx"), (96, 48, "yxz"))
WAYS_UP = WAYS_DOWN
WAYS_HEAD = ((0, 48, "xzy"), (48, 32, "zyx"), (80, 32, "yxz"))
WAYS_OUT = ((0, 16, "xzy"), (16, 16, "zyx"), (32, 16, "yxz"))
SCALE = HS**-0.5
SCALE_LOG2E = SCALE * 1.4426950408889634
NEGATIVE = -1e30
EPSILON = 1e-05
GELU_C = 0.7978845608028654
GELU_A = 0.044715

LN1G, LN1B, BQ, BV = 0, 1, 2, 3
BOUT, LN2G, LN2B, BDOWN, BUP = 0, 1, 2, 3, 4
VROWS = 8
WIDEN_SLOTS = 6


def dot(a, b):
    return jnp.dot(a, b, preferred_element_type=f32)


def dot_nt(a, b):
    return lax.dot_general(a, b, (((1,), (1,)), ((), ())), preferred_element_type=f32)


def turned(block):
    return jnp.transpose(block.astype(f32)).astype(bf16)


def coords():
    r = lax.axis_index("rows")
    s = lax.axis_index("seq")
    return lax.div(r, 2), lax.rem(r, 2), lax.div(s, 4), lax.rem(s, 4)


def device_at(y, c, z, x):
    return (y * 2 + c, z * 4 + x)


def remote(src, dst, send, recv, device):
    return pltpu.make_async_remote_copy(
        src_ref=src, dst_ref=dst, send_sem=send, recv_sem=recv, device_id=device, device_id_type=MESH
    )


def seq_peer(d):
    s = lax.axis_index("seq")
    return lax.rem(s + d, 16)


def axis_peer(axis, j):
    y, c, z, x = coords()
    if axis == "y":
        y = lax.rem(y + j, 4)
    elif axis == "z":
        z = lax.rem(z + j, 4)
    else:
        x = lax.rem(x + j, 4)
    return device_at(y, c, z, x)


def axis_place(axis):
    y, c, z, x = coords()
    return {"y": y, "z": z, "x": x}[axis]


def sibling():
    y, c, z, x = coords()
    return device_at(y, 1 - c, z, x)


def greet():
    bar = pltpu.get_barrier_semaphore()
    r = lax.axis_index("rows")
    s = lax.axis_index("seq")
    devices = [(r, seq_peer(d)) for d in range(1, 16)] + [(lax.rem(r + d, 8), s) for d in range(1, 8)]
    for device in devices:
        pl.semaphore_signal(bar, inc=1, device_id=device, device_id_type=MESH)
    return bar, len(devices)


def masked(scores, start, key0, query0, diagonal):
    key = lax.broadcasted_iota(jnp.int32, scores.shape, 0) + key0
    ok = key >= start
    if diagonal:
        query = lax.broadcasted_iota(jnp.int32, scores.shape, 1) + query0
        ok = ok & (key <= query)
    return jnp.where(ok, scores, NEGATIVE)


def segment_starts(offs_ref, query0, count):
    place = lax.broadcasted_iota(jnp.int32, (1, count), 1) + query0
    start = jnp.zeros((1, count), jnp.int32)
    for j in range(8):
        o = offs_ref[0, j]
        start = jnp.where(place >= o, o, start)
    return start


def pair(ref, i, lo, hi):
    return jnp.concatenate([ref[2 * i, lo:hi, :], ref[2 * i + 1, lo:hi, :]], axis=1)


def attend_forward(offs_ref, qk, vals, kn, vt, ot, lse, atts, values_here, after):
    for s in range(NB):
        kn[s * TOK : (s + 1) * TOK, :] = turned(qk[s, 48:96, :])
    values_here()
    for s in range(NB):
        vt[:, s * TOK : (s + 1) * TOK] = vals[s]
    for i in range(SEQ // QB):
        q0 = i * QB
        qt = pair(qk, i, 0, 48)
        start = segment_starts(offs_ref, q0, QB)
        sd = masked(dot(kn[q0 : q0 + QB, :], qt) * SCALE_LOG2E, start, q0, q0, True)
        top = jnp.max(sd, axis=0, keepdims=True)
        if i:
            so = masked(dot(kn[0:q0, :], qt) * SCALE_LOG2E, start, 0, q0, False)
            top = jnp.maximum(top, jnp.max(so, axis=0, keepdims=True))
        pd = jnp.exp2(sd - top)
        total = jnp.sum(pd, axis=0, keepdims=True)
        out = dot(vt[:, q0 : q0 + QB], pd.astype(bf16))
        if i:
            po = jnp.exp2(so - top)
            total = total + jnp.sum(po, axis=0, keepdims=True)
            out = out + dot(vt[:, 0:q0], po.astype(bf16))
        out = out / total
        ot[:, q0 : q0 + QB] = out
        lse[:, q0 : q0 + QB] = top + jnp.log2(total)
        low = out.astype(bf16)
        atts[2 * i] = low[:, 0:TOK]
        atts[2 * i + 1] = low[:, TOK:QB]
        after(2 * i)
        after(2 * i + 1)


def attend_backward(offs_ref, qk, vals, kn, kt, vn, qn, don, dor, ot, lse, dqkv, dk, dv, after):
    for s in range(NB):
        rows = slice(s * TOK, (s + 1) * TOK)
        vn[rows, :] = turned(vals[s])
        qn[rows, :] = turned(qk[s, 0:48, :])
        don[rows, :] = turned(dor[s])
        kt[:, rows] = qk[s, 48:96, :]
    last = SEQ // QB - 1
    for i in reversed(range(SEQ // QB)):
        q0 = i * QB
        qt = pair(qk, i, 0, 48)
        dot_t = pair(dor, i, 0, 48)
        start = segment_starts(offs_ref, q0, QB)
        level = lse[:, q0 : q0 + QB]
        inner = jnp.sum(dot_t.astype(f32) * ot[:, q0 : q0 + QB], axis=0, keepdims=True)
        q_n = qn[q0 : q0 + QB, :]
        do_n = don[q0 : q0 + QB, :]
        dq = None
        for a, b, diagonal in ([(0, q0, False)] if i else []) + [(q0, q0 + QB, True)]:
            scores = masked(dot(kn[a:b, :], qt) * SCALE_LOG2E, start, a, q0, diagonal)
            probs = jnp.exp2(scores - level)
            dp = dot(vn[a:b, :], dot_t)
            ds = (probs * (dp - inner)).astype(bf16)
            dv_part = dot(probs.astype(bf16), do_n)
            dk_part = dot(ds, q_n)
            if i == last:
                dk[a:b, :] = dk_part
                dv[a:b, :] = dv_part
            else:
                dk[a:b, :] += dk_part
                dv[a:b, :] += dv_part
            dq_part = dot(kt[:, a:b], ds)
            dq = dq_part if dq is None else dq + dq_part
        dq = (dq * SCALE).astype(bf16)
        for h in range(2):
            s = 2 * i + h
            rows = slice(s * TOK, (s + 1) * TOK)
            dqkv[s, 0:48, :] = dq[:, h * TOK : (h + 1) * TOK]
            dqkv[s, 48:96, :] = (jnp.transpose(dk[rows, :]) * SCALE).astype(bf16)
            dqkv[s, 96:144, :] = jnp.transpose(dv[rows, :]).astype(bf16)
        after(i)


def norm_parts(values):
    center = values - jnp.mean(values, axis=-1, keepdims=True)
    spread = jnp.mean(center * center, axis=-1, keepdims=True)
    rs = lax.rsqrt(spread + EPSILON)
    return center * rs, rs


def norm_back(grad, n, rs, gain):
    gg = grad * gain
    return rs * (
        gg - jnp.mean(gg, axis=-1, keepdims=True) - n * jnp.mean(gg * n, axis=-1, keepdims=True)
    )


def over_tokens(values):
    return jnp.sum(values, axis=0, keepdims=True)


def arrived(gauge, sem):
    pltpu.make_async_copy(gauge, gauge, sem).wait()


class Steps:
    def __init__(self, send, recv):
        self.send, self.recv = send, recv
        self.sent = []
        self.live = []
        self.at = 0

    def go(self, group, src, dst, device):
        remote(src, dst, self.send.at[group], self.recv.at[group], device).start()

    def expect(self, group, gauge):
        self.live.append((group, gauge))
        self.sent.append((group, gauge))

    def collect(self):
        for group, gauge in self.live:
            arrived(gauge, self.recv.at[group])
        self.live = []

    def step(self):
        self.collect()
        k = self.at
        self.at = k + 1
        self.run(k)

    def done(self):
        for group, gauge in self.sent:
            arrived(gauge, self.send.at[group])
        self.sent = []


class Scatter(Steps):
    def __init__(self, cuts, parts, recv1, mid, recv2, share, send, recv):
        super().__init__(send, recv)
        self.cuts, self.parts, self.recv1, self.mid, self.recv2, self.share = cuts, parts, recv1, mid, recv2, share

    def put(self, value, offset):
        at, rows = 0, value.shape[0]
        while at < rows:
            k = 0 if offset < 16 * self.cuts[0] else 1
            inside = offset - k * 16 * self.cuts[0]
            block, lo = inside // self.cuts[k], inside % self.cuts[k]
            size = min(self.cuts[k] - lo, rows - at)
            self.parts[k][block // 4, block % 4, lo : lo + size, :] = value[at : at + size]
            at += size
            offset += size

    def run(self, k):
        z, x = axis_place("z"), axis_place("x")
        first, second = self.parts
        if k == 0:
            for j in range(1, 4):
                self.go(0, first.at[:, lax.rem(x + j, 4)], self.recv1[0].at[j - 1], axis_peer("x", j))
                self.go(1, second.at[lax.rem(z + j, 4)], self.recv1[1].at[j - 1], axis_peer("z", j))
            for n in range(2):
                self.expect(n, self.recv1[n])
        elif k == 1:
            for n, mine in enumerate((first[:, x], second[z])):
                acc = mine.astype(f32)
                for j in range(3):
                    acc = acc + self.recv1[n][j].astype(f32)
                self.mid[n][...] = acc.astype(bf16)
            for j in range(1, 4):
                self.go(2, self.mid[0].at[lax.rem(z + j, 4)], self.recv2[0].at[j - 1], axis_peer("z", j))
                self.go(3, self.mid[1].at[lax.rem(x + j, 4)], self.recv2[1].at[j - 1], axis_peer("x", j))
            for n in range(2):
                self.expect(2 + n, self.recv2[n])
        else:
            lo = 0
            for n, here in enumerate((z, x)):
                acc = self.mid[n][here].astype(f32)
                for j in range(3):
                    acc = acc + self.recv2[n][j].astype(f32)
                self.share[lo : lo + self.cuts[n], :] = acc.astype(bf16)
                lo += self.cuts[n]


class Spread(Steps):
    def __init__(self, share, ag, ways, send, recv, own, at_once=False):
        super().__init__(send, recv)
        self.share, self.ag, self.ways, self.own, self.at_once = share, ag, ways, own, at_once

    def spot(self, lo, size, whole, **at):
        core = lax.rem(lax.axis_index("rows"), 2)
        index = [at[a] if a in at else slice(None) if a in whole else axis_place(a) for a in "zxy"]
        return self.ag.at[(core, *index, pl.ds(lo, size))]

    def pass_on(self, spot):
        if not self.at_once:
            self.go(4, spot, spot, sibling())

    def run(self, k):
        ag = self.ag
        if k == 1:
            self.kept.wait()
        for lo, size, order in self.ways:
            last = order[2]
            here = axis_place(last)
            if k == 0:
                for j in range(1, 4):
                    self.go(0, self.share.at[pl.ds(lo, size)], self.spot(lo, size, ""), axis_peer(order[0], j))
            elif k == 1:
                spot = self.spot(lo, size, order[0])
                for j in range(1, 4):
                    self.go(1, spot, spot, axis_peer(order[1], j))
            elif k == 2:
                spot = self.spot(lo, size, order[:2])
                self.go(2, spot, spot, axis_peer(last, 1))
                self.go(2, spot, spot, axis_peer(last, 3))
                self.pass_on(spot)
            elif k == 3:
                before, after = lax.rem(here + 3, 4), lax.rem(here + 1, 4)
                cut = "x" if last == "z" else "z"
                low = self.spot(lo, size, order[:2], **{last: before, cut: pl.ds(0, 2)})
                high = self.spot(lo, size, order[:2], **{last: after, cut: pl.ds(2, 2)})
                self.go(3, low, low, axis_peer(last, 1))
                self.go(3, high, high, axis_peer(last, 3))
                self.pass_on(self.spot(lo, size, order[:2], **{last: before}))
                self.pass_on(self.spot(lo, size, order[:2], **{last: after}))
            elif k == 4:
                self.pass_on(self.spot(lo, size, order[:2], **{last: lax.rem(here + 2, 4)}))
        three = pl.ds(0, 3)
        if k == 0:
            self.kept = pltpu.make_async_copy(self.share, self.spot(0, self.share.shape[0], ""), self.own)
            self.kept.start()
            self.expect(0, ag.at[0, 0, 0, three])
        elif k == 1:
            self.expect(1, ag.at[0, 0, three])
        elif k == 2:
            self.expect(2, ag.at[0, pl.ds(0, 2)])
        elif k == 3:
            self.expect(3, ag.at[0, 0])
        elif k == 4:
            if self.at_once:
                spot = ag.at[lax.rem(lax.axis_index("rows"), 2)]
                self.go(4, spot, spot, sibling())
            self.expect(4, ag.at[0])
        else:
            self.done()


class RowSwap(Steps):
    def __init__(self, src, dst, send, recv):
        super().__init__(send, recv)
        self.src, self.dst = src, dst

    def run(self, k):
        r, s = lax.axis_index("rows"), lax.axis_index("seq")
        if k == 0:
            for d in range(1, 8):
                peer = lax.rem(r + d, 8)
                self.go(0, self.src.at[peer], self.dst.at[r], (peer, s))
            self.dst[r] = self.src[r]
            self.expect(0, self.dst.at[pl.ds(0, 7)])
        else:
            self.done()


class RowGather(Steps):
    def __init__(self, dst, send, recv):
        super().__init__(send, recv)
        self.dst = dst

    def run(self, k):
        r = lax.axis_index("rows")
        dst = self.dst
        half = dst.shape[1] // 2
        before, after = lax.rem(r + 6, 8), lax.rem(r + 2, 8)
        if k == 0:
            for device in (axis_peer("y", 1), axis_peer("y", 3)):
                self.go(0, dst.at[r], dst.at[r], device)
            self.go(2, dst.at[r], dst.at[r], sibling())
            self.expect(0, dst.at[pl.ds(0, 2)])
        elif k == 1:
            low, high = dst.at[before, pl.ds(0, half)], dst.at[after, pl.ds(half, half)]
            self.go(1, low, low, axis_peer("y", 1))
            self.go(1, high, high, axis_peer("y", 3))
            for spot in (dst.at[before], dst.at[after]):
                self.go(2, spot, spot, sibling())
            self.expect(1, dst.at[0])
        elif k == 2:
            spot = dst.at[lax.rem(r + 4, 8)]
            self.go(2, spot, spot, sibling())
            self.expect(2, dst.at[pl.ds(0, 4)])
        else:
            self.done()


class Exchange:
    def __init__(self, src, dst, send, recv):
        self.src, self.dst, self.send, self.recv = src, dst, send, recv

    def all(self):
        r = lax.axis_index("rows")
        s = lax.axis_index("seq")
        for d in range(1, 16):
            peer = seq_peer(d)
            remote(self.src.at[peer], self.dst.at[s], self.send, self.recv, (r, peer)).start()
        self.dst[s] = self.src[s]
        return self

    def one(self, block):
        r = lax.axis_index("rows")
        s = lax.axis_index("seq")

        @pl.when(s != block)
        def _():
            remote(self.src.at[block], self.dst.at[s], self.send, self.recv, (r, block)).start()

        @pl.when(s == block)
        def _():
            self.dst[s] = self.src[block]

    def wait(self):
        gauge = self.dst.at[pl.ds(0, 15)]
        arrived(gauge, self.recv)
        arrived(gauge, self.send)


class Gather(Steps):
    def __init__(self, hall, send, recv):
        super().__init__(send, recv)
        self.hall = hall

    def run(self, k):
        z, x = axis_place("z"), axis_place("x")
        hall = self.hall
        if k == 0:
            for j in range(1, 4):
                self.go(0, hall.at[0, z, x], hall.at[0, z, x], axis_peer("x", j))
                self.go(0, hall.at[1, z, x], hall.at[1, z, x], axis_peer("z", j))
            self.expect(0, hall.at[:, pl.ds(0, 3), 0])
        elif k == 1:
            for j in (1, 3):
                self.go(1, hall.at[0, z], hall.at[0, z], axis_peer("z", j))
                self.go(1, hall.at[1, :, x], hall.at[1, :, x], axis_peer("x", j))
            self.expect(1, hall.at[0])
        elif k == 2:
            two, low = pl.ds(2, 2), pl.ds(0, 2)
            for spot, axis, j in (
                (hall.at[0, lax.rem(z + 3, 4), low], "z", 1),
                (hall.at[0, lax.rem(z + 1, 4), two], "z", 3),
                (hall.at[1, low, lax.rem(x + 3, 4)], "x", 1),
                (hall.at[1, two, lax.rem(x + 1, 4)], "x", 3),
            ):
                self.go(2, spot, spot, axis_peer(axis, j))
            self.expect(2, hall.at[:, :, 0])
        else:
            self.done()


class Heads(Steps):
    def __init__(self, part, sib_recv, both, y_recv, share, send, recv):
        super().__init__(send, recv)
        self.part, self.sib_recv, self.both, self.y_recv, self.share = part, sib_recv, both, y_recv, share

    def run(self, k):
        y = axis_place("y")
        if k == 0:
            self.go(0, self.part.at[1], self.sib_recv, sibling())
            self.expect(0, self.sib_recv)
        elif k == 1:
            self.both[...] = (self.part[0].astype(f32) + self.sib_recv[...].astype(f32)).astype(bf16)
            for j in range(1, 4):
                there = lax.rem(y + j, 4)
                self.go(1, self.both.at[pl.ds(there * SHARE, SHARE)], self.y_recv.at[j - 1], axis_peer("y", j))
            self.expect(1, self.y_recv)
        else:
            acc = self.both[pl.ds(y * SHARE, SHARE)].astype(f32)
            for j in range(3):
                acc = acc + self.y_recv[j].astype(f32)
            self.share[0:SHARE, :] = acc.astype(bf16)
            self.done()


class Quarters(Steps):
    def __init__(self, part, y_recv, send, recv):
        super().__init__(send, recv)
        self.part, self.y_recv = part, y_recv

    def run(self, k):
        y = axis_place("y")
        if k == 0:
            for j in range(1, 4):
                self.go(0, self.part.at[lax.rem(y + j, 4)], self.y_recv.at[j - 1], axis_peer("y", j))
            self.expect(0, self.y_recv)
        else:
            acc = self.part[y].astype(f32)
            for j in range(3):
                acc = acc + self.y_recv[j].astype(f32)
            self.done()
            return acc.astype(bf16)

    def total(self):
        self.collect()
        return self.run(1)


class Vectors:
    def __init__(self, buf, slots, send_sem, recv_sem):
        self.buf, self.slots, self.send_sem, self.recv_sem = buf, slots, send_sem, recv_sem
        self.at = 0

    def step(self):
        k = self.at
        self.at = k + 1
        if k == 0:
            value = self.buf[0]
        else:
            gauge = self.slots.at[k - 1, pl.ds(0, 3 if k < 4 else 1)]
            arrived(gauge, self.recv_sem.at[k - 1])
            arrived(gauge, self.send_sem.at[k - 1])
            value = self.slots[k - 1, 0]
            for j in range(1, 4 if k < 4 else 2):
                value = value + self.slots[k - 1, j]
        if k == 4:
            self.buf[1] = value
            return
        here = axis_place("xyz"[k]) if k < 3 else lax.rem(lax.axis_index("rows"), 2)
        devices = [axis_peer("xyz"[k], j) for j in range(1, 4)] if k < 3 else [sibling()]
        self.slots[k, here] = value
        for device in devices:
            spot = self.slots.at[k, here]
            remote(spot, spot, self.send_sem.at[k], self.recv_sem.at[k], device).start()


def block_kernel(
    offs_h, x_h, dy_h, ln1g_h, ln1b_h, bq_h, bv_h, bout_h, ln2g_h, ln2b_h, bup_h, bdown_h,
    wqkv_h, wout_h, wup_h, wdown_h,
    out_h, ig_h, ag0, ag1, agh, agw, vecs_h,
    offs, x_ref, dy_ref, ln1g, ln1b, bq, bv, bout, ln2g, ln2b, bup, bdown,
    out_ref, ig_ref, vecs,
    wqkv, wout, wup, wdown, wsem,
    qkt, vals, rqk, rv, kn, vt, ot, lse, atts, ratt,
    hall, n1, rs1, h2ta, dya, actt, acta, gp, gpa, gb, gbs, attts, gres,
    gattt, rda, kt, vn, qn, don, dk, dv, dqkv, rdq,
    asend, arecv, ssend, srecv,
    *rest,
):
    (vbuf, vrecv, vsend, vrsem, lbuf, lrecv, lsend, lrsem, osem,
     hsend, hrecv, hpart, hsib, hboth, hy, hmine, wop, wor) = rest[:18]
    rest = rest[18:]
    sems = [rest[2 * k : 2 * k + 2] for k in range(13)]
    own, rest = rest[26], rest[27:]
    down_parts, down_recv1, down_mid, down_recv2 = [rest[2 * k : 2 * k + 2] for k in range(4)]
    up_parts, up_recv1, up_mid, up_recv2 = [rest[8 + 2 * k : 10 + 2 * k] for k in range(4)]
    out_parts, out_recv1, out_mid, out_recv2 = [rest[16 + 2 * k : 18 + 2 * k] for k in range(4)]
    down_share, up_share, out_share = rest[24:]
    bar, count = greet()
    loads = {}

    def load(name, src, dst):
        copy = pltpu.make_async_copy(src, dst, wsem.at[len(loads)])
        copy.start()
        loads[name] = copy

    load("x", x_h, x_ref)
    load("ln1g", ln1g_h, ln1g)
    load("ln1b", ln1b_h, ln1b)
    for t in (1, 0, 2):
        cols = pl.ds(t * D, D)
        load(f"qkv{t}", wqkv_h.at[:, cols], wqkv.at[:, cols])
    load("bq", bq_h, bq)
    load("bv", bv_h, bv)
    load("dy", dy_h, dy_ref)
    load("offs", offs_h, offs)
    stores = []

    def ready(*names):
        for name in names:
            loads[name].wait()

    def store(src, dst):
        copy = pltpu.make_async_copy(src, dst, osem.at[len(stores)])
        copy.start()
        stores.append(copy)

    vecg = vbuf.at[0]
    vecl = lbuf.at[0]
    early = Vectors(vbuf, vrecv, vsend, vrsem)
    late = Vectors(lbuf, lrecv, lsend, lrsem)
    gather = Gather(hall, hsend, hrecv)
    heads = Heads(hpart, hsib, hboth, hy, hmine, *sems[0])
    dy_rows = RowGather(dya, *sems[1])
    h2_rows = RowGather(h2ta, *sems[2])
    act_rows = RowSwap(actt, acta, *sems[3])
    gp_rows = RowSwap(gp, gpa, *sems[4])
    quarters = Quarters(wop, wor, *sems[5])
    down_sum = Scatter(CUT_DOWN, down_parts, down_recv1, down_mid, down_recv2, down_share, *sems[6])
    up_sum = Scatter(CUT_UP, up_parts, up_recv1, up_mid, up_recv2, up_share, *sems[7])
    down_all = Spread(down_share, ag0, WAYS_DOWN, *sems[8], own.at[0], True)
    up_all = Spread(up_share, ag1, WAYS_UP, *sems[9], own.at[1])
    head_all = Spread(hmine, agh, WAYS_HEAD, *sems[10], own.at[2])
    out_all = Spread(out_share, agw, WAYS_OUT, *sems[12], own.at[3])
    out_sum = Scatter(CUT_OUT, out_parts, out_recv1, out_mid, out_recv2, out_share, *sems[11])
    row = lax.axis_index("rows")

    def line(ref):
        return ref[...].astype(f32).reshape(1, D)

    core = lax.rem(lax.axis_index("rows"), 2)
    other = 1 - core
    sib = sibling()
    to_sib = []

    def send_sib(n, src, dst):
        copy = remote(src, dst, ssend.at[n], srecv.at[n], sib)
        copy.start()
        to_sib.append(copy)

    ready("x", "ln1g", "ln1b")
    x = x_ref[...].astype(f32)
    n, rs = norm_parts(x)
    n1[...] = n
    rs1[...] = rs
    h1f = n * line(ln1g) + line(ln1b)
    h1 = h1f.astype(bf16)
    for half in range(2):
        hall[half, axis_place("z"), axis_place("x")] = h1[:, half * 384 : (half + 1) * 384]
    for t in (1, 0, 2):
        ready(f"qkv{t}")
        y = dot(h1, wqkv[:, t * D : (t + 1) * D])
        if t == 0:
            ready("bq")
            y = y + line(bq)
        if t == 2:
            ready("bv")
            y = y + line(bv)
        low = jnp.transpose(y).astype(bf16).reshape(H, HS, TOK)
        if t < 2:
            qkt[:, t * HS : (t + 1) * HS, :] = low
        else:
            vals[...] = low
        if t == 0:
            pl.semaphore_wait(bar, count)
            moved = [Exchange(qkt, rqk, asend.at[0], arecv.at[0]).all()]
    moved.append(Exchange(vals, rv, asend.at[1], arecv.at[1]).all())
    load("out", wout_h, wout)
    for name, src, dst in (
        ("bout", bout_h, bout), ("ln2g", ln2g_h, ln2g), ("ln2b", ln2b_h, ln2b),
        ("bup", bup_h, bup), ("bdown", bdown_h, bdown),
    ):
        load(name, src, dst)
    load("up", wup_h, wup)
    load("down", wdown_h, wdown)
    ready("dy", "offs")
    dya[row] = dy_ref[...]
    dy_rows.step()
    moved[0].wait()
    gather.step()

    attended = Exchange(atts, ratt, asend.at[2], arecv.at[2])
    attend_forward(
        offs, rqk, rv, kn, vt, ot, lse, atts,
        moved[1].wait, attended.one,
    )
    ready("out", "bout", "ln2g", "ln2b", "bup", "bdown", "up", "down")
    gather.step()
    attended.wait()
    dy_rows.step()

    att = jnp.transpose(ratt[...].reshape(D, TOK).astype(f32)).astype(bf16)
    send_sib(0, ratt.at[pl.ds(other * 8, 8)], attts)
    resid = x_ref[...].astype(f32) + dot(att, wout[...]) + line(bout)
    n2, rs2 = norm_parts(resid)
    h2f = n2 * line(ln2g) + line(ln2b)
    h2 = h2f.astype(bf16)
    h2ta[row] = jnp.transpose(h2f).astype(bf16)
    h2_rows.step()
    dy = dy_ref[...]
    down = None
    dh2 = None
    for c in range(4):
        cols = slice(c * D, (c + 1) * D)
        pre = dot(h2, wup[:, cols]) + bup[cols].astype(f32).reshape(1, D)
        square = pre * pre
        t = jnp.tanh(GELU_C * (pre + GELU_A * (square * pre)))
        act = 0.5 * pre * (1.0 + t)
        slope = 0.5 * (1.0 + t) + (0.5 * GELU_C) * pre * (1.0 - t * t) * (1.0 + (3.0 * GELU_A) * square)
        part = dot(act.astype(bf16), wdown[cols, :])
        down = part if down is None else down + part
        act_t = jnp.transpose(act).astype(bf16)
        actt[2 * c] = act_t[0:384]
        actt[2 * c + 1] = act_t[384:768]
        gpre = (dot_nt(dy, wdown[cols, :]) * slope).astype(bf16)
        gp[2 * c] = gpre[:, 0:384]
        gp[2 * c + 1] = gpre[:, 384:768]
        vecg[BUP + c : BUP + c + 1, :] = over_tokens(gpre.astype(f32))
        part = dot_nt(gpre, wup[:, cols])
        dh2 = part if dh2 is None else dh2 + part
    act_rows.step()
    gp_rows.step()
    out_ref[...] = (resid + down + line(bdown)).astype(bf16)
    store(out_ref, out_h)
    vecg[BDOWN : BDOWN + 1, :] = over_tokens(dy.astype(f32))
    vecg[LN2G : LN2G + 1, :] = over_tokens(dh2 * n2)
    vecg[LN2B : LN2B + 1, :] = over_tokens(dh2)
    grad = dy.astype(f32) + norm_back(dh2, n2, rs2, line(ln2g))
    gres[...] = grad
    branch = grad.astype(bf16)
    gb[...] = branch
    vecg[BOUT : BOUT + 1, :] = over_tokens(branch.astype(f32))
    gattt[...] = jnp.transpose(dot_nt(branch, wout[...])).astype(bf16).reshape(H, HS, TOK)
    moved = Exchange(gattt, rda, asend.at[3], arecv.at[3]).all()
    h2_rows.step()
    send_sib(1, gb, gbs)

    gather.step()
    moved.wait()

    def part_out():
        for copy in to_sib:
            copy.wait()
        left = jnp.concatenate(
            [ratt[pl.ds(core * 8, 8)].reshape(384, TOK), attts[...].reshape(384, TOK)], axis=1
        )
        right = jnp.concatenate([gb[...], gbs[...]], axis=0)
        res = dot(left, right).astype(bf16)
        for k in range(4):
            for t in range(6):
                wop[k, t * 96 : (t + 1) * 96, :] = res[k * 96 : (k + 1) * 96, t * TOK : (t + 1) * TOK]
        quarters.step()

    def grads_down():
        dy_rows.step()
        act_rows.step()
        left = jnp.concatenate([acta[k] for k in range(8)], axis=1)
        res = dot(left, dya[...].reshape(8 * TOK, D)).astype(bf16)
        for t in range(6):
            down_sum.put(res[:, t * TOK : (t + 1) * TOK], t * 384)
        down_sum.step()

    def grads_up():
        h2_rows.step()
        gp_rows.step()
        left = jnp.concatenate([h2ta[k] for k in range(8)], axis=1)
        res = dot(left, gpa[...].reshape(8 * TOK, 384)).astype(bf16)
        for t in range(3):
            up_sum.put(res[:, t * TOK : (t + 1) * TOK], t * D)
        up_sum.step()

    def grads_out():
        out_sum.put(quarters.total(), 0)
        out_sum.put(jnp.zeros((192, TOK), bf16), 576)
        out_sum.step()

    back = Exchange(dqkv, rdq, asend.at[4], arecv.at[4])

    def between(i):
        for half in (0, 1):
            back.one(2 * i + half)
        if i == 7:
            dy_rows.step()
            early.step()
        elif i == 6:
            part_out()
        elif i == 5:
            grads_down()
        elif i == 1:
            down_sum.step()

    attend_backward(offs, rqk, rv, kn, kt, vn, qn, don, rda, ot, lse, dqkv, dk, dv, between)
    gather.step()
    spread = jnp.concatenate([dqkv[k] for k in range(NB)], axis=1)

    def part_head(slot, half):
        res = dot(spread, hall[half].reshape(SEQ, 384)).astype(bf16)
        for u in range(3):
            hpart[slot, u * 144 : (u + 1) * 144, :] = res[:, u * TOK : (u + 1) * TOK]
        hpart[slot, 432:HEAD_ROWS, :] = jnp.zeros((HEAD_ROWS - 432, TOK), bf16)

    part_head(1, other)
    heads.step()
    part_head(0, core)
    h2_rows.step()
    heads.step()
    grads_up()
    back.wait()
    down_sum.step()
    down_all.step()
    dh1t = None
    ones = jnp.ones((8, TOK), bf16)
    for t in range(3):
        grad_t = rdq[:, t * HS : (t + 1) * HS, :].reshape(D, TOK)
        part = dot(wqkv[:, t * D : (t + 1) * D], grad_t)
        dh1t = part if dh1t is None else dh1t + part
        if t != 1:
            row = BQ if t == 0 else BV
            vecl[row : row + 1, :] = dot_nt(ones, grad_t)[0:1, :]
    dh1 = jnp.transpose(dh1t)
    n = n1[...]
    vecl[LN1G : LN1G + 1, :] = over_tokens(dh1 * n)
    vecl[LN1B : LN1B + 1, :] = over_tokens(dh1)
    vecl[4:8, :] = jnp.zeros((4, D), f32)
    early.step()
    late.step()
    grads_out()
    up_sum.step()
    down_all.step()
    late.step()
    out_sum.step()
    heads.step()
    head_all.step()
    up_sum.step()
    up_all.step()
    early.step()
    down_all.step()
    up_all.step()
    head_all.step()
    ig_ref[...] = (gres[...] + norm_back(dh1, n, rs1[...], line(ln1g))).astype(bf16)
    store(ig_ref, ig_h)
    down_all.step()
    out_sum.step()
    out_all.step()
    up_all.step()
    out_all.step()
    late.step()
    head_all.step()
    down_all.step()
    out_all.step()
    up_all.step()
    head_all.step()
    late.step()
    early.step()
    late.step()
    early.step()
    vecs[0] = vbuf[1]
    vecs[1] = lbuf[1]
    store(vecs, vecs_h)
    out_all.step()
    up_all.step()
    head_all.step()
    out_all.step()
    for item in (down_all, up_all, head_all, out_all):
        item.step()
    for item in (down_sum, up_sum, out_sum):
        item.done()
    for copy in stores:
        copy.wait()


VMEM = pl.BlockSpec(memory_space=pltpu.VMEM)
SMEM = pl.BlockSpec(memory_space=pltpu.SMEM)
ANY = pl.BlockSpec(memory_space=pl.ANY)
HBM = pl.BlockSpec(memory_space=pltpu.HBM)


def call_block(offsets, x, dy, vectors, weights):
    v = pltpu.VMEM
    dma = pltpu.SemaphoreType.DMA
    shape = jax.ShapeDtypeStruct
    return pl.pallas_call(
        block_kernel,
        out_shape=(
            v((TOK, D), bf16),
            v((TOK, D), bf16),
            v((2, 4, 4, 4, sum(CUT_DOWN), TOK), bf16),
            v((2, 4, 4, 4, sum(CUT_UP), TOK), bf16),
            v((2, 4, 4, 4, SHARE, TOK), bf16),
            v((2, 4, 4, 4, sum(CUT_OUT), TOK), bf16),
            v((2, VROWS, D), f32),
        ),
        in_specs=[HBM] * 16,
        out_specs=(ANY,) * 7,
        scratch_shapes=[
            pltpu.SMEM((1, 8), jnp.int32), v((TOK, D), bf16), v((TOK, D), bf16),
            *[v((FF if k == 7 else D,), bf16) for k in range(9)],
            v((TOK, D), bf16), v((TOK, D), bf16), v((2, VROWS, D), f32),
            v((D, 3 * D), bf16), v((D, D), bf16), v((D, FF), bf16), v((FF, D), bf16), dma((20,)),
            v((NB, 96, TOK), bf16), v((NB, HS, TOK), bf16), v((NB, 96, TOK), bf16), v((NB, HS, TOK), bf16),
            v((SEQ, HS), bf16), v((HS, SEQ), bf16),
            v((HS, SEQ), f32), v((1, SEQ), f32), v((NB, HS, TOK), bf16), v((NB, HS, TOK), bf16),
            v((2, 4, 4, TOK, 384), bf16), v((TOK, D), f32), v((TOK, 1), f32),
            v((8, D, TOK), bf16), v((8, TOK, D), bf16),
            v((8, 384, TOK), bf16), v((8, 384, TOK), bf16), v((8, TOK, 384), bf16), v((8, TOK, 384), bf16),
            v((TOK, D), bf16), v((TOK, D), bf16), v((8, HS, TOK), bf16), v((TOK, D), f32),
            v((NB, HS, TOK), bf16), v((NB, HS, TOK), bf16),
            v((HS, SEQ), bf16), v((SEQ, HS), bf16), v((SEQ, HS), bf16), v((SEQ, HS), bf16),
            v((SEQ, HS), f32), v((SEQ, HS), f32),
            v((NB, 144, TOK), bf16), v((NB, 144, TOK), bf16),
            dma((5,)), dma((5,)), dma((2,)), dma((2,)),
            v((2, VROWS, D), f32), v((4, 4, VROWS, D), f32), dma((4,)), dma((4,)),
            v((2, VROWS, D), f32), v((4, 4, VROWS, D), f32), dma((4,)), dma((4,)), dma((3,)),
            dma((3,)), dma((3,)), v((2, HEAD_ROWS, TOK), bf16), v((HEAD_ROWS, TOK), bf16),
            v((HEAD_ROWS, TOK), bf16), v((3, SHARE, TOK), bf16), v((SHARE, TOK), bf16),
            v((4, 576, TOK), bf16), v((3, 576, TOK), bf16),
            *[dma((n,)) for n in (2, 3, 3, 1, 1, 1, 4, 4, 5, 5, 5, 4, 5) for _ in range(2)], dma((4,)),
            *[
                v(lead + (cut, TOK), bf16)
                for cuts in (CUT_DOWN, CUT_UP, CUT_OUT)
                for lead in ((4, 4), (3, 4), (4,), (3,))
                for cut in cuts
            ],
            v((sum(CUT_DOWN), TOK), bf16), v((sum(CUT_UP), TOK), bf16), v((sum(CUT_OUT), TOK), bf16),
        ],
        compiler_params=pltpu.CompilerParams(
            collective_id=1, has_side_effects=True, vmem_limit_bytes=43 * 2**20
        ),
    )(*[pltpu.with_memory_space_constraint(a, pltpu.HBM) for a in (offsets, x, dy, *vectors, *weights)])


def widen_kernel(ag0, ag1, agh, agw, vecs, done_h, ig_h, wqkv, wout, wup, wdown, out_h, grad_h, *rest):
    small_h, small = rest[:9], rest[9:18]
    down_out, up_out, out_out, wideb, vsem, ssem, osem = rest[18:]
    passed = [
        pltpu.make_async_copy(done_h, out_h, vsem.at[0]),
        pltpu.make_async_copy(ig_h, grad_h, vsem.at[1]),
    ]

    def pieces(cuts, base, offset, rows):
        at = 0
        while at < rows:
            n = 0 if offset < 16 * cuts[0] else 1
            inside = offset - n * 16 * cuts[0]
            block, lo = inside // cuts[n], inside % cuts[n]
            size = min(cuts[n] - lo, rows - at)
            yield at, size, block // 4, block % 4, base + n * cuts[0] + lo
            at += size
            offset += size

    def widen(ag, cuts, base, k, offset, rows, dst, col):
        for at, size, z, x, lo in pieces(cuts, base, offset, rows):
            part = ag[k % 2, z, x, k // 2, lo : lo + size, :]
            dst[at : at + size, col * TOK : (col + 1) * TOK] = part.astype(f32)

    def head_rows(core, z, x, lo, rows):
        parts = []
        while rows:
            y, inside = lo // SHARE, lo % SHARE
            size = min(SHARE - inside, rows)
            parts.append(agh[core, z, x, y, inside : inside + size, :])
            lo += size
            rows -= size
        return parts

    down_store = [
        pltpu.make_async_copy(down_out.at[k % 3], wdown.at[pl.ds(k * 384, 384)], osem.at[0, k % 3]) for k in range(8)
    ]
    up_store = [
        pltpu.make_async_copy(up_out.at[k % 3], wup.at[:, pl.ds(k * 384, 384)], osem.at[1, k % 3]) for k in range(8)
    ]
    out_store = [
        pltpu.make_async_copy(
            out_out.at[k % 3], wout.at[pl.ds((k % 2) * 384 + (k // 2) * 96, 96)], osem.at[2, k % 3]
        )
        for k in range(8)
    ]
    head_store = [
        pltpu.make_async_copy(wideb.at[k % 3], wqkv.at[pl.ds(k * TOK, TOK)], osem.at[3, k % 3]) for k in range(6)
    ]
    for copy in passed:
        copy.start()
    for k in range(8):
        if k >= 3:
            down_store[k - 3].wait()
        for t in range(6):
            widen(ag0, CUT_DOWN, 0, k, t * 384, 384, down_out.at[k % 3], t)
        down_store[k].start()
        if k >= 3:
            up_store[k - 3].wait()
            out_store[k - 3].wait()
        for t in range(3):
            widen(ag1, CUT_UP, 0, k, t * D, D, up_out.at[k % 3], t)
        up_store[k].start()
        for t in range(6):
            widen(agw, CUT_OUT, 0, k, t * 96, 96, out_out.at[k % 3], t)
        out_store[k].start()
        if k < 6:
            if k >= 3:
                head_store[k - 3].wait()
            for t in range(3):
                parts = []
                for head in range(H):
                    parts += head_rows(k // 3, head // 4, head % 4, (k % 3) * 144 + t * HS, HS)
                block = jnp.concatenate(parts, axis=0)
                wideb[k % 3, :, t * D : (t + 1) * D] = jnp.transpose(block.astype(f32))
            head_store[k].start()
        if k == 0:
            places = ((1, LN1G), (1, LN1B), (1, BQ), (1, BV), (0, BOUT), (0, LN2G), (0, LN2B), (0, BUP), (0, BDOWN))
            for n, (ref, (group, line)) in enumerate(zip(small, places)):
                if line == BUP:
                    for c in range(4):
                        ref[c * D : (c + 1) * D] = vecs[0, BUP + c : BUP + c + 1, :].reshape(D)
                else:
                    ref[...] = vecs[group, line : line + 1, :].reshape(D)
                copy = pltpu.make_async_copy(ref, small_h[n], ssem.at[n])
                copy.start()
                passed.append(copy)
    for k in range(5, 8):
        down_store[k].wait()
        up_store[k].wait()
        out_store[k].wait()
        head_store[k - 2].wait()
    for copy in passed:
        copy.wait()


def call_widen(*arrays):
    v = pltpu.VMEM
    dma = pltpu.SemaphoreType.DMA
    shape = jax.ShapeDtypeStruct
    return pl.pallas_call(
        widen_kernel,
        out_shape=(
            shape((D, 3 * D), f32), shape((D, D), f32), shape((D, FF), f32), shape((FF, D), f32),
            shape((TOK, D), bf16), shape((TOK, D), bf16),
        ) + tuple(shape((FF if k == 7 else D,), f32) for k in range(9)),
        in_specs=[VMEM] * 5 + [ANY] * 2,
        out_specs=(ANY,) * 15,
        scratch_shapes=[
            *[v((FF if k == 7 else D,), f32) for k in range(9)],
            v((3, 384, D), f32), v((3, D, 384), f32), v((3, 96, D), f32), v((3, TOK, 3 * D), f32),
            dma((2,)), dma((9,)), dma((4, 3)),
        ],
        compiler_params=pltpu.CompilerParams(vmem_limit_bytes=30 * 2**20),
    )(*[pltpu.with_memory_space_constraint(a, pltpu.VMEM) for a in arrays])


def local(
    block_input, offsets, ln1_gain, ln1_bias, w_qkv, bias_query, bias_value, w_out, bias_out,
    ln2_gain, ln2_bias, w_up, bias_up, w_down, bias_down, cotangent,
):
    out, ig, ag0, ag1, agh, agw, vecs = call_block(
        offsets, block_input.reshape(TOK, D), cotangent.reshape(TOK, D),
        (ln1_gain, ln1_bias, bias_query, bias_value, bias_out, ln2_gain, ln2_bias, bias_up, bias_down),
        (w_qkv, w_out, w_up, w_down),
    )
    wide = call_widen(ag0, ag1, agh, agw, vecs, out, ig)
    g_qkv, g_out, g_up, g_down, out, ig = wide[:6]
    s = wide[6:]
    return (
        out.reshape(1, TOK, D), ig.reshape(1, TOK, D),
        s[0], s[1], g_qkv, s[2], s[3], g_out, s[4], s[5], s[6], g_up, s[7], g_down, s[8],
    )


def solution(mesh):
    tokens = P("rows", "seq", None)
    return jax.shard_map(
        local,
        mesh=mesh,
        in_specs=(tokens, P("rows", None)) + (P(),) * 13 + (tokens,),
        out_specs=(tokens, tokens) + (P(),) * 13,
        check_vma=False,
    )
```
